32 devices in a mesh: section: 2 (over core), tensor: 4 (over z), dp: 4 (over y, x).
Axes of the slice: x: 2, y: 2, z: 4, core: 2. Of those that a mesh axis runs over, the one named last changes fastest.
Arguments:
- inputs: bfloat16 [8192, 1024], P('dp'), may hold values from -6 to 6
- cotangent: bfloat16 [8192, 1024], P('dp'), may hold values from -6 to 6
- lengths: int32 [8], P('dp'), may hold values from 256 to 1024, as said below
- w_query: bfloat16 [2, 1024, 1024], P('section', None, 'tensor'), may hold values from -0.1875 to 0.1875
- w_latent: bfloat16 [2, 1024, 512], P('section'), may hold values from -0.1875 to 0.1875
- w_key: bfloat16 [2, 256, 1024], P('section', None, 'tensor'), may hold values from -0.375 to 0.375
- w_value: bfloat16 [2, 256, 1024], P('section', None, 'tensor'), may hold values from -0.375 to 0.375
- w_out: bfloat16 [2, 1024, 1024], P('section', 'tensor'), may hold values from -3 to 3
- gains: float32 [2, 2, 1024], P('section'), may hold values from 0.1 to 1.9
- w_gate: bfloat16 [2, 1024, 2816], P('section', None, 'tensor'), may hold values from -0.1875 to 0.1875
- w_up: bfloat16 [2, 1024, 2816], P('section', None, 'tensor'), may hold values from -0.25 to 0.25
- w_down: bfloat16 [2, 2816, 1024], P('section', 'tensor'), may hold values from -0.21875 to 0.21875
Outputs:
- layer_outputs: bfloat16 [2, 8192, 1024], P('section', 'dp')
- input_grads: bfloat16 [2, 8192, 1024], P('section', 'dp')
- grad_query: float32 [2, 1024, 1024], P('section', 'dp', 'tensor')
- grad_latent: float32 [2, 1024, 512], P('section', ('tensor', 'dp'))
- grad_key: float32 [2, 256, 1024], P('section', 'dp', 'tensor')
- grad_value: float32 [2, 256, 1024], P('section', 'dp', 'tensor')
- grad_out: float32 [2, 1024, 1024], P('section', 'tensor', 'dp')
- grad_gains: float32 [2, 2, 1024], P('section', None, ('tensor', 'dp'))
- grad_gate: float32 [2, 1024, 2816], P('section', 'dp', 'tensor')
- grad_up: float32 [2, 1024, 2816], P('section', 'dp', 'tensor')
- grad_down: float32 [2, 2816, 1024], P('section', 'tensor', 'dp')
The draws below stay inside these ranges and needn't reach their ends.
Inputs may be any that keep to these rules, and one draw needn't show every extreme that they name: lengths[s] counts the live rows of sequence s, the rest of its bucket is padding; some sequence fills its bucket exactly.
All inputs are finite; a program needn't handle non-finite values.
Results may differ from the reference program's by a relative error of at most 0.025.
Values may be sent and summed in bfloat16 or wider, within the bound.
No kernel may reach another device: no remote copies, remote signals or barrier semaphores. Data moves between devices by JAX's collectives and lax.ppermute only.
A program may use at most 256 MiB of HBM per device.

```python
import jax
import jax.numpy as jnp
from jax import lax

D = 1024
HEADS = 16
HEAD_DIM = 64
KV_HEADS = 2
LATENT = 256
FF = 2816
BUCKET = 1024
MIN_LEN = 256
QBLOCK = 512
LAYERS = 2
SEQS = 8
TOKENS = 8192
N_TENSOR = 4


def draw_lengths(key, part):
    key = jax.random.fold_in(key, 5)
    first, second = jax.random.split(key)
    grain = 1000
    raw = jax.random.randint(first, (SEQS,), 0, grain + 1)
    curve = raw * raw // grain
    lengths = MIN_LEN + curve * (BUCKET - MIN_LEN) // grain
    pick = jax.random.randint(second, (), 0, SEQS)
    return jnp.where(jnp.arange(SEQS) == pick, BUCKET, lengths).astype(jnp.int32)


def steps_of(rng, extent, cuts, smallest, high):
    level, own = 1.0, jax.random.fold_in(rng, 6)
    for axis_at, shards_of in cuts:
        steps = jnp.exp(jax.random.uniform(jax.random.fold_in(own, axis_at), (shards_of,), jnp.float32, smallest / len(cuts), high / len(cuts)))
        level = level * jnp.repeat(steps, extent[axis_at] // shards_of).reshape([-1 if axis == axis_at else 1 for axis in range(len(extent))])
    return level


def gaussian(stream_key, shape, scale, reach, shards=(), kind=jnp.bfloat16):
    loudness = steps_of(stream_key, shape, shards, -0.22, 0.18) if shards else 1.0
    entries = jax.random.normal(stream_key, shape, jnp.float32) * scale * loudness
    return jnp.minimum(jnp.maximum(entries, -reach), reach).astype(kind)


def setup_inputs(seed: int = 0) -> dict:
    seeds = jax.random.split(jax.random.key(seed), 13)
    inputs = gaussian(seeds[0], (TOKENS, D), 1.0, 6.0, ((0, 4),))
    cotangent = gaussian(seeds[1], (TOKENS, D), 1.0, 6.0, ((0, 4),))
    lengths = draw_lengths(jax.random.fold_in(seeds[12], 71), 0)
    w_query = gaussian(seeds[3], (LAYERS, D, HEADS * HEAD_DIM), D ** -0.5, 0.1875, ((0, 2), (2, 4)))
    w_latent = gaussian(seeds[4], (LAYERS, D, KV_HEADS * LATENT), D ** -0.5, 0.1875, ((0, 2),))
    w_key = gaussian(seeds[5], (LAYERS, LATENT, HEADS * HEAD_DIM), LATENT ** -0.5, 0.375, ((0, 2), (2, 4)))
    w_value = gaussian(seeds[6], (LAYERS, LATENT, HEADS * HEAD_DIM), LATENT ** -0.5, 0.375, ((0, 2), (2, 4)))
    w_out = gaussian(seeds[7], (LAYERS, HEADS * HEAD_DIM, D), (max(1, HEADS * HEAD_DIM * 4 // BUCKET)) ** -0.5, 3.0, ((0, 2), (1, 4)))
    gains = jnp.clip(1.0 + 0.18 * jax.random.normal(seeds[8], (LAYERS, 2, D), jnp.float32), 0.1, 1.9)
    w_gate = gaussian(seeds[9], (LAYERS, D, FF), D ** -0.5, 0.1875, ((0, 2), (2, 4)))
    w_up = gaussian(seeds[10], (LAYERS, D, FF), (D // 2) ** -0.5, 0.25, ((0, 2), (2, 4)))
    w_down = gaussian(seeds[11], (LAYERS, FF, D), (FF // 4) ** -0.5, 0.21875, ((0, 2), (1, 4)))
    return {"inputs": inputs, "cotangent": cotangent, "lengths": lengths, "w_query": w_query, "w_latent": w_latent, "w_key": w_key, "w_value": w_value, "w_out": w_out, "gains": gains, "w_gate": w_gate, "w_up": w_up, "w_down": w_down}


eps = 1e-06
masked_score = -1e+30

@jax.custom_vjp
def low(v):
    return lax.optimization_barrier(v.astype(jnp.bfloat16)).astype(jnp.float32)

@jax.custom_vjp
def low_back(v):
    return v

def low_keep(v):
    return (low(v), None)

def low_pass(kept, grad):
    return (grad,)

def back_keep(v):
    return (v, None)

def back_low(kept, grad):
    return (low(grad),)
low.defvjp(low_keep, low_pass)
low_back.defvjp(back_keep, back_low)

def matmul(left, right):
    return jnp.dot(left, right, preferred_element_type=jnp.float32, precision=lax.Precision.HIGHEST)

def rms_rows(rows, gain):
    return rows * lax.rsqrt(lax.optimization_barrier(jnp.mean(rows * rows, axis=-1, keepdims=True)) + eps) * gain

def attention_block(query_block, keys, values, start, length):
    scores = jnp.einsum('qhd,khd->hqk', query_block, keys, precision=lax.Precision.HIGHEST) * HEAD_DIM ** (-0.5)
    scores = low_back(scores)
    rows_here = query_block.shape[0]
    query_pos = start + lax.broadcasted_iota(jnp.int32, (rows_here, keys.shape[0]), 0)
    key_pos = lax.broadcasted_iota(jnp.int32, (rows_here, keys.shape[0]), 1)
    allowed = (key_pos <= query_pos) & (key_pos < length)
    scores = jnp.where(allowed[None], scores, masked_score)
    peak = lax.optimization_barrier(jnp.max(scores, axis=-1, keepdims=True))
    expo = jnp.exp(scores - peak)
    probs = low(expo / lax.optimization_barrier(jnp.sum(expo, axis=-1, keepdims=True)))
    mixed = jnp.einsum('hqk,khd->qhd', probs, values, precision=lax.Precision.HIGHEST)
    return low_back(low(mixed))

def layer(rows, length, w_query, w_latent, w_key, w_value, w_out, gains, w_gate, w_up, w_down):
    count = rows.shape[0]
    normed = low(rms_rows(rows, gains[0]))
    queries = low_back(low(matmul(normed, w_query)))
    latent = low(matmul(normed, w_latent))
    heads_dev = HEADS // N_TENSOR
    group_heads = HEADS // KV_HEADS
    cols = heads_dev * HEAD_DIM
    starts = jnp.arange(count // QBLOCK, dtype=jnp.int32) * QBLOCK
    branch = jnp.zeros((count, D), jnp.float32)
    for share in range(N_TENSOR):
        group = share * heads_dev // group_heads
        own = low_back(latent[:, group * LATENT:(group + 1) * LATENT])
        keys = low_back(low(matmul(own, w_key[:, share * cols:(share + 1) * cols]))).reshape(count, heads_dev, HEAD_DIM)
        values = low_back(low(matmul(own, w_value[:, share * cols:(share + 1) * cols]))).reshape(count, heads_dev, HEAD_DIM)
        blocks = queries[:, share * cols:(share + 1) * cols].reshape(count // QBLOCK, QBLOCK, heads_dev, HEAD_DIM)

        def one_block(item, keys=keys, values=values):
            return attention_block(item[0], keys, values, item[1], length)
        mixed = lax.map(jax.checkpoint(one_block), (blocks, starts)).reshape(count, cols)
        branch = branch + matmul(mixed, w_out[share * cols:(share + 1) * cols])
    branch = low_back(branch)
    residual = rows + branch
    normed2 = low(rms_rows(residual, gains[1]))
    gate = low_back(matmul(normed2, w_gate))
    up = low_back(matmul(normed2, w_up))
    hidden = low(jax.nn.silu(gate) * up)
    feed = low_back(matmul(hidden, w_down))
    live = (jnp.arange(count, dtype=jnp.int32) < length).astype(jnp.float32)[:, None]
    return low(live * (residual + feed))

def reference(inputs, cotangent, lengths, w_query, w_latent, w_key, w_value, w_out, gains, w_gate, w_up, w_down):
    weights = tuple((w.astype(jnp.float32) for w in (w_query, w_latent, w_key, w_value, w_out, gains, w_gate, w_up, w_down)))
    seqs = lengths.shape[0]
    feed_rows = inputs.astype(jnp.float32).reshape(seqs, BUCKET, D)
    targets = cotangent.astype(jnp.float32).reshape(seqs, BUCKET, D)

    def one_sequence(totals, item):
        rows, target, length = item

        def forward(start_rows, probes, params):
            outputs = []
            current = start_rows
            for level in range(LAYERS):
                current = layer(current, length, *[p[level] for p in params])
                if level + 1 < LAYERS:
                    current = low_back(current + probes[level])
                outputs.append(current)
            return jnp.stack(outputs)
        probes = jnp.zeros((LAYERS - 1, BUCKET, D), jnp.float32)
        outputs, pull = jax.vjp(forward, rows, probes, weights)
        upstream = jnp.zeros_like(outputs).at[LAYERS - 1].set(target)
        grad_rows, grad_probes, grad_weights = pull(upstream)
        grads_in = jnp.concatenate([grad_rows[None], grad_probes], axis=0)
        totals = jax.tree.map(lambda a, b: a + b, totals, grad_weights)
        return (totals, (outputs, grads_in))
    start = jax.tree.map(jnp.zeros_like, weights)
    totals, (outputs, grads_in) = lax.scan(one_sequence, start, (feed_rows, targets, lengths))
    outputs = jnp.transpose(outputs, (1, 0, 2, 3)).reshape(LAYERS, seqs * BUCKET, D).astype(jnp.bfloat16)
    grads_in = jnp.transpose(grads_in, (1, 0, 2, 3)).reshape(LAYERS, seqs * BUCKET, D).astype(jnp.bfloat16)
    return (outputs, grads_in, totals[0], totals[1], totals[2], totals[3], totals[4], totals[5], totals[6], totals[7], totals[8])
```

```python
import functools

import jax
import jax.numpy as jnp
from jax import lax
from jax.experimental import pallas as pl
from jax.experimental.pallas import tpu as pltpu
from jax.sharding import PartitionSpec as P

HEAD_DIM = 64
eps = 1e-06
masked_score = -1e30
f32 = jnp.float32
bf16 = jnp.bfloat16


def dot_nn(left, right):
    return lax.dot_general(left, right, (((1,), (0,)), ((), ())), preferred_element_type=f32)


def dot_nt(left, right):
    return lax.dot_general(left, right, (((1,), (1,)), ((), ())), preferred_element_type=f32)


def dot_tn(left, right):
    return lax.dot_general(left, right, (((0,), (0,)), ((), ())), preferred_element_type=f32)


def core_swap(value):
    return lax.ppermute(value, "section", [(0, 1), (1, 0)])


def z_swap(value, step):
    count = lax.axis_size("tensor")
    return lax.ppermute(value, "tensor", [(i, i ^ step) for i in range(count)])


def plane_swap(value, bit):
    count = lax.axis_size("dp")
    return lax.ppermute(value, "dp", [(i, i ^ bit) for i in range(count)])


def tie(first, *others):
    return lax.optimization_barrier((first,) + others)[0]


def bits_of(count):
    return [1 << i for i in range(count.bit_length() - 1)]


def plane_gather(piece):
    count = lax.axis_size("dp")
    half = piece.shape[-2] // 2
    have = {0: (piece,)}
    for key in sorted(range(1, count), key=lambda k: (k.bit_count(), k)):
        bits = [b for b in bits_of(count) if key & b]
        if len(bits) == 1:
            have[key] = (plane_swap(piece, key),)
            continue
        parts = []
        for at, bit in enumerate((bits[-1], bits[0])):
            source = have[key ^ bit]
            part = source[at] if len(source) == 2 else lax.slice_in_dim(source[0], at * half, (at + 1) * half, axis=-2)
            parts.append(plane_swap(part, bit))
        have[key] = tuple(parts)
    return jnp.stack([jnp.concatenate(have[k], axis=-2) if len(have[k]) > 1 else have[k][0] for k in range(count)])


class Scatter:
    def __init__(self, keep, send):
        self.parts = [keep, core_swap(send)]

    def split(self):
        count = lax.axis_size("dp")
        order = bits_of(count)
        rows = self.parts[0].shape[2]
        self.halves = []
        for at, way in enumerate((order, order[::-1])):
            terms = [lax.slice_in_dim(p, at * (rows // 2), (at + 1) * (rows // 2), axis=2) for p in self.parts]
            terms = [
                t.reshape(t.shape[:1] + (2,) * len(order) + t.shape[2:]) for t in terms
            ]
            self.halves.append((terms, list(way), sorted(order, reverse=True)))

    def step(self):
        me = lax.axis_index("dp")
        after = []
        for terms, way, axes in self.halves:
            bit = way[0]
            axis = 1 + axes.index(bit)
            mine = (me // bit) % 2
            keep = sum(lax.dynamic_index_in_dim(t, mine, axis, False) for t in terms)
            send = sum(lax.dynamic_index_in_dim(t, 1 - mine, axis, False) for t in terms)
            after.append(([keep, plane_swap(send, bit)], way[1:], [a for a in axes if a != bit]))
        self.halves = after

    def leaves(self):
        return [t for terms, _, _ in self.halves for t in terms]

    def result(self):
        return jnp.concatenate([sum(terms) for terms, _, _ in self.halves], axis=1)


def by_plane(values, flip_of):
    count = values.shape[0]
    for bit in bits_of(count):
        order = [k ^ bit for k in range(count)]
        flipped = jnp.stack([values[k] for k in order])
        values = jnp.where((flip_of // bit) % 2 == 1, flipped, values)
    return values


def inverse_rms(rows):
    return lax.rsqrt(jnp.mean(rows * rows, axis=-1, keepdims=True) + eps)


def norm_back(rows, gain, grad_norm):
    scale = inverse_rms(rows)
    weighted = grad_norm * gain
    inner = jnp.mean(weighted * rows, axis=-1, keepdims=True)
    grad_rows = scale * weighted - rows * scale * scale * scale * inner
    grad_gain = jnp.sum(grad_norm * rows * scale, axis=0)
    return (grad_rows, grad_gain)


LENGTH, FIRST, CORE, MEMBER, RANK = range(5)


def kernel_call(kernel, info, arrays, grid, in_specs, out_specs, out_shape, scratch, name, flops, transcendentals=0):
    size = sum(a.size * a.dtype.itemsize for a in arrays)
    size += sum(o.size * o.dtype.itemsize for o in out_shape)
    return pl.pallas_call(
        kernel,
        grid_spec=pltpu.PrefetchScalarGridSpec(
            num_scalar_prefetch=1,
            grid=grid,
            in_specs=in_specs,
            out_specs=out_specs,
            scratch_shapes=scratch,
        ),
        out_shape=out_shape,
        compiler_params=pltpu.CompilerParams(
            dimension_semantics=("arbitrary",) * len(grid), vmem_limit_bytes=56 * 1024 * 1024
        ),
        cost_estimate=pl.CostEstimate(flops=flops, bytes_accessed=size, transcendentals=transcendentals),
        name=name,
    )(info, *arrays)


def whole(array):
    shape = array.shape
    return pl.BlockSpec(shape, lambda i, info: (0,) * len(shape))


def lead(array):
    shape = array.shape[1:]
    return pl.BlockSpec((1,) + shape, lambda i, info: (i,) + (0,) * len(shape))


def like(shape, dtype):
    return jax.ShapeDtypeStruct(shape, dtype)


def place_pack(info, step, own, near, other, pack):
    members, _, rows, cols = near.shape

    @pl.when(step == 0)
    def _():
        pack[...] = own[...]

    @pl.when(step > 0)
    def _():
        for key in range(members):
            for source, core in ((near, info[CORE]), (other, 1 - info[CORE])):
                at = (core * members + (info[MEMBER] ^ key)) * rows
                pack[pl.ds(pl.multiple_of(at, 16), rows), :] = source[key, 0]


def fill_bias(info, bias):
    keys, rows = bias.shape
    key_pos = lax.broadcasted_iota(jnp.int32, (keys, rows), 0)
    query_pos = lax.broadcasted_iota(jnp.int32, (keys, rows), 1) + info[FIRST]
    allowed = (key_pos <= query_pos) & (key_pos < info[LENGTH])
    bias[...] = jnp.where(allowed, 0.0, masked_score)


def attend_kernel(
    info, x, normed, lat0, lat1, lat2, lat3, own, near, other, gain, mixed_out, lse_out, lat_out, residual, normed2, bias, pack
):
    step = pl.program_id(0)
    rows, width = normed.shape
    latent = lat_out.shape[2]
    cols = pack.shape[1]

    @pl.when(step == 0)
    def _():
        fill_bias(info, bias)
        residual[...] = x[...].astype(f32)
        for key, piece in enumerate((lat0, lat1, lat2, lat3)):
            at = pl.multiple_of((info[RANK] ^ key) * rows, 16)
            for group in range(2):
                lat_out[group, pl.ds(at, rows), :] = piece[:, group * latent : (group + 1) * latent]

    place_pack(info, step, own, near, other, pack)
    w_query = pack[0:width]
    w_key = pack[width : width + latent]
    w_value = pack[width + latent : width + 2 * latent]
    w_out_t = pack[width + 2 * latent :]
    here = lat_out[step // 2]
    query = dot_nn(normed[...], w_query).astype(bf16) * bf16(HEAD_DIM**-0.5)
    keys = dot_nn(here, w_key).astype(bf16)
    values_t = dot_nn(here, w_value).astype(bf16).T
    lane_head = lax.broadcasted_iota(jnp.int32, (rows, cols), 1) // HEAD_DIM
    mixed_parts = []
    for head in range(cols // HEAD_DIM):
        query_here = jnp.where(lane_head == head, query, bf16(0))
        scores = dot_nt(keys, query_here) + bias[...]
        peak = jnp.max(scores, axis=0, keepdims=True)
        expo = jnp.exp(scores - peak)
        total = jnp.sum(expo, axis=0, keepdims=True)
        part = dot_nn(values_t[head * HEAD_DIM : (head + 1) * HEAD_DIM], expo.astype(bf16))
        mixed_parts.append(part * (1.0 / total))
        lse_out[0, head : head + 1, :] = peak + jnp.log(total)
    mixed = jnp.concatenate(mixed_parts, axis=0).T.astype(bf16)
    mixed_out[0] = mixed
    residual[...] += dot_nt(mixed, w_out_t)

    @pl.when(step == pl.num_programs(0) - 1)
    def _():
        full = residual[...]
        normed2[...] = (full * inverse_rms(full) * gain[...]).astype(bf16)


def attend_back_kernel(
    info, grad_branch, normed, lat, own, near, other, mixed_in, lse_in, grad_norm, grad_lat, keep, send, bias, pack
):
    step = pl.program_id(0)
    rows, width = normed.shape
    keys_count, latent = lat.shape[1:]
    cols = pack.shape[1]
    scale = HEAD_DIM**-0.5
    pieces = keep.shape[1]

    @pl.when(step == 0)
    def _():
        fill_bias(info, bias)
        grad_norm[...] = jnp.zeros_like(grad_norm)

    @pl.when(step % 2 == 0)
    def _():
        grad_lat[...] = jnp.zeros_like(grad_lat)

    place_pack(info, step, own, near, other, pack)
    w_query = pack[0:width]
    w_key = pack[width : width + latent]
    w_value = pack[width + latent : width + 2 * latent]
    w_out_t = pack[width + 2 * latent :]
    here = lat[0]
    query = dot_nn(normed[...], w_query).astype(bf16) * bf16(scale)
    keys = dot_nn(here, w_key).astype(bf16)
    keys_t = keys.T
    values = dot_nn(here, w_value).astype(bf16)
    mixed = mixed_in[0]
    grad_mixed = dot_nn(grad_branch[...], w_out_t).astype(bf16)
    centre = (grad_mixed.astype(f32) * mixed.astype(f32)).T
    lane_head = lax.broadcasted_iota(jnp.int32, (rows, cols), 1) // HEAD_DIM
    grad_keys = jnp.zeros((keys_count, cols), f32)
    grad_values = jnp.zeros((keys_count, cols), f32)
    grad_query_parts = []
    for head in range(cols // HEAD_DIM):
        mine = slice(head * HEAD_DIM, (head + 1) * HEAD_DIM)
        query_here = jnp.where(lane_head == head, query, bf16(0))
        grad_here = jnp.where(lane_head == head, grad_mixed, bf16(0))
        scores = dot_nt(keys, query_here) + bias[...]
        probs = jnp.exp(scores - lse_in[0, head : head + 1, :])
        grad_probs = dot_nt(values, grad_here)
        inner = jnp.sum(centre[mine], axis=0, keepdims=True)
        grad_scores = (probs * (grad_probs - inner)).astype(bf16)
        grad_values += dot_nn(probs.astype(bf16), grad_here)
        grad_keys += dot_nn(grad_scores, query_here)
        grad_query_parts.append(dot_nn(keys_t[mine], grad_scores) * scale)
    grad_keys = grad_keys.astype(bf16)
    grad_values = grad_values.astype(bf16)
    grad_query = jnp.concatenate(grad_query_parts, axis=0).T.astype(bf16)
    grad_norm[...] += dot_nt(grad_query, w_query)
    grad_lat[0] += dot_nt(grad_keys, w_key) + dot_nt(grad_values, w_value)
    halves = (
        (dot_tn(normed[...], grad_query), dot_tn(here, grad_keys)),
        (dot_tn(here, grad_values), dot_tn(grad_branch[...], mixed)),
    )
    for half, results in enumerate(halves):
        for out, wanted in ((keep, half), (send, 1 - half)):

            @pl.when(info[CORE] == wanted)
            def _(out=out, results=results):
                at = 0
                for result in results:
                    size = result.shape[0] // pieces
                    for piece in range(pieces):
                        out[0, piece, at : at + size, :] = result[piece * size : (piece + 1) * size].astype(bf16)
                    at += size


def attend_call(info, x, normed, lats, own, near, other, gain):
    rows, width = normed.shape
    members, others, _, cols = near.shape
    sets = others + 1
    latent = lats[0].shape[1] // 2
    keys = rows * 4
    heads = cols // HEAD_DIM
    piece = pl.BlockSpec((members, 1) + near.shape[2:], lambda i, info: (0, jnp.maximum(i - 1, 0), 0, 0))
    outs = [
        like((sets, rows, cols), bf16),
        like((sets, heads, rows), f32),
        like((2, keys, latent), bf16),
        like((rows, width), f32),
        like((rows, width), bf16),
    ]
    return kernel_call(
        attend_kernel,
        info,
        (x, normed, *lats, own, near, other, gain),
        (sets,),
        [whole(x), whole(normed)] + [whole(v) for v in lats] + [whole(own), piece, piece, whole(gain)],
        [lead(outs[0]), lead(outs[1])] + [whole(o) for o in outs[2:]],
        outs,
        [pltpu.VMEM((keys, rows), f32), pltpu.VMEM(own.shape, bf16)],
        "attend",
        2 * sets * rows * (2 * keys * cols * heads + width * cols * 2) + 4 * sets * keys * latent * cols,
        sets * heads * keys * rows,
    )


def attend_back_call(info, grad_branch, normed, lat, own, near, other, mixed, lse):
    rows, width = normed.shape
    members, others, piece_rows, cols = near.shape
    sets = others + 1
    keys, latent = lat.shape[1:]
    heads = cols // HEAD_DIM
    piece = pl.BlockSpec((members, 1) + near.shape[2:], lambda i, info: (0, jnp.maximum(i - 1, 0), 0, 0))
    group = pl.BlockSpec((1, keys, latent), lambda i, info: (i // 2, 0, 0))
    outs = [
        like((rows, width), f32),
        like((2, keys, latent), f32),
        like((sets, members, piece_rows, cols), bf16),
        like((sets, members, piece_rows, cols), bf16),
    ]
    return kernel_call(
        attend_back_kernel,
        info,
        (grad_branch, normed, lat, own, near, other, mixed, lse),
        (sets,),
        [whole(grad_branch), whole(normed), group, whole(own), piece, piece, lead(mixed), lead(lse)],
        [whole(outs[0]), group, lead(outs[2]), lead(outs[3])],
        outs,
        [pltpu.VMEM((keys, rows), f32), pltpu.VMEM(own.shape, bf16)],
        "attend_back",
        2 * sets * rows * (5 * keys * cols * heads + width * cols * 5) + 16 * sets * keys * latent * cols,
        sets * heads * keys * rows,
    )


def place_feed(info, step, own, near, other, weights):
    members, _, rows, _ = near.shape

    @pl.when(step == 0)
    def _():
        weights[...] = own[...]

    @pl.when(step > 0)
    def _():
        for key in range(members):
            for source, core in ((near, info[CORE]), (other, 1 - info[CORE])):
                at = (core * members + (info[MEMBER] ^ key)) * rows
                weights[:, pl.ds(pl.multiple_of(at, 16), rows), :] = source[key]


def feed_kernel(info, value, own, near, other, total_out, saved, weights, total):
    step = pl.program_id(0)
    place_feed(info, step, own, near, other, weights)
    gate = dot_nn(value[...], weights[0])
    up = dot_nn(value[...], weights[1])
    saved[0, 0] = gate.astype(bf16)
    saved[0, 1] = up.astype(bf16)
    hidden = (gate * jax.nn.sigmoid(gate) * up).astype(bf16)
    part = dot_nt(hidden, weights[2])

    @pl.when(step == 0)
    def _():
        total[...] = part

    @pl.when(step > 0)
    def _():
        total_out[...] = (total[...] + part).astype(total_out.dtype)


def feed_back_kernel(info, value, own, near, other, saved, total_out, rights, weights, total):
    step = pl.program_id(0)
    place_feed(info, step, own, near, other, weights)
    grad_hidden = dot_nn(value[...], weights[2])
    gate = saved[0, 0].astype(f32)
    up = saved[0, 1].astype(f32)
    sigma = jax.nn.sigmoid(gate)
    silu = gate * sigma
    grad_gate = (grad_hidden * up * sigma * (1.0 + gate * (1.0 - sigma))).astype(bf16)
    grad_up = (grad_hidden * silu).astype(bf16)
    rights[0, 0] = grad_gate
    rights[0, 1] = grad_up
    rights[0, 2] = (silu * up).astype(bf16)
    part = dot_nt(grad_gate, weights[0]) + dot_nt(grad_up, weights[1])

    @pl.when(step == 0)
    def _():
        total[...] = part

    @pl.when(step > 0)
    def _():
        total_out[...] = (total[...] + part).astype(total_out.dtype)


def feed_weights_kernel(info, normed2, far_normed2, grad, far_grad, rights, far_rights, keep, send, lefts):
    step = pl.program_id(0)
    rows = normed2.shape[0]
    pieces, size = keep.shape[2:4]

    @pl.when(step == 0)
    def _():
        for at, (near, far) in enumerate(((normed2, far_normed2), (grad, far_grad))):
            lefts[at, :, 0:rows] = near[...].T
            lefts[at, :, rows : 2 * rows] = far[...].T

    for kind in range(3):
        right = jnp.concatenate([rights[0, kind], far_rights[0, kind]], axis=0)
        for out, half in ((keep, info[CORE]), (send, 1 - info[CORE])):
            for piece in range(pieces):
                at = pl.multiple_of((2 * piece + half) * size, 16)
                left = lefts[kind // 2, pl.ds(at, size), :]
                out[0, kind, piece] = dot_nn(left, right).astype(bf16)


def feed_call(info, value, own, near, other, dtype):
    rows, width = value.shape
    cols = own.shape[2]
    outs = [like((rows, width), dtype), like((2, 2, rows, cols), bf16)]
    return kernel_call(
        feed_kernel,
        info,
        (value, own, near, other),
        (2,),
        [whole(value), whole(own), whole(near), whole(other)],
        [whole(outs[0]), lead(outs[1])],
        outs,
        [pltpu.VMEM(own.shape, bf16), pltpu.VMEM((rows, width), f32)],
        "feed",
        2 * 2 * 3 * rows * width * cols,
    )


def feed_back_call(info, value, own, near, other, saved, dtype):
    rows, width = value.shape
    cols = own.shape[2]
    outs = [like((rows, width), dtype), like((2, 3, rows, cols), bf16)]
    return kernel_call(
        feed_back_kernel,
        info,
        (value, own, near, other, saved),
        (2,),
        [whole(value), whole(own), whole(near), whole(other), lead(saved)],
        [whole(outs[0]), lead(outs[1])],
        outs,
        [pltpu.VMEM(own.shape, bf16), pltpu.VMEM((rows, width), f32)],
        "feed_back",
        2 * 2 * 3 * rows * width * cols,
    )


def feed_weights_call(info, values, rights, pieces):
    rows, width = values[0].shape
    cols = rights[0].shape[3]
    outs = [like((2, 3, pieces, width // pieces // 2, cols), bf16)] * 2
    return kernel_call(
        feed_weights_kernel,
        info,
        (*values, *rights),
        (2,),
        [whole(v) for v in values] + [lead(r) for r in rights],
        [lead(o) for o in outs],
        outs,
        [pltpu.VMEM((2, width, 2 * rows), bf16)],
        "feed_weights",
        2 * 2 * 3 * 2 * rows * width * cols,
    )


def shards(inputs, cotangent, lengths, w_query, w_latent, w_key, w_value, w_out, gains, w_gate, w_up, w_down):
    core = lax.axis_index("section")
    z = lax.axis_index("tensor")
    d = lax.axis_index("dp")
    planes = lax.axis_size("tensor")
    dp = lax.axis_size("dp")
    seqs = lengths.shape[0]
    bucket = inputs.shape[0] // seqs
    width = inputs.shape[1]
    layers = 2
    per_seq = planes // seqs * 2
    rows = bucket // per_seq
    rank = (z % (planes // seqs)) * 2 + core
    seq = z // (planes // seqs)
    first = rank * rows
    length = lax.dynamic_index_in_dim(lengths, seq, 0, False)
    info = jnp.stack([length, first, core, d, rank]).astype(jnp.int32)
    live = (lax.broadcasted_iota(jnp.int32, (rows, 1), 0) + first < length).astype(f32)
    row_at = seq * bucket + first
    own_in = lax.dynamic_slice_in_dim(inputs, row_at, rows, 0)
    own_target = lax.dynamic_slice_in_dim(cotangent, row_at, rows, 0)
    latent = w_latent.shape[2] // 2
    far_group = z // (planes // 2)

    pack_own = jnp.concatenate([w_query[0], w_key[0], w_value[0], w_out[0].T], axis=0)
    feed_own = jnp.stack([w_gate[0], w_up[0], w_down[0].T])

    def both(value):
        other = core_swap(value)
        return [jnp.where(core == layer, value, other) for layer in range(layers)]

    packs = both(pack_own)
    latents_w = both(w_latent[0])
    gains_all = both(gains[0])
    feeds = both(feed_own)
    pack_rows, cols = pack_own.shape
    hidden_cols = feed_own.shape[2]

    def gather_pack(own):
        lanes = own.reshape(2, dp, pack_rows // 2 // dp, cols)
        piece = lax.dynamic_slice(lanes, (core, d, 0, 0), (1, 1) + lanes.shape[2:])[0, 0]
        near = plane_gather(jnp.stack([z_swap(piece, step) for step in range(1, planes)]))
        return near, core_swap(near)

    def gather_feed(own):
        lanes = own.reshape(3, 2, dp, width // 2 // dp, hidden_cols)
        piece = lax.dynamic_slice(lanes, (0, core, d, 0, 0), (3, 1, 1) + lanes.shape[3:])[:, 0, 0]
        near = plane_gather(z_swap(piece, planes // 2))
        return near, core_swap(near)

    def by_group(value):
        return by_plane(value, far_group)

    def forward(layer, x, pack, feed_w):
        gain = gains_all[layer]
        x32 = x.astype(f32)
        normed = (x32 * inverse_rms(x32) * gain[0]).astype(bf16)
        own_lat = dot_nn(normed, latents_w[layer]).astype(bf16)
        own_lat = jnp.where(
            far_group == 1, jnp.concatenate([own_lat[:, latent:], own_lat[:, :latent]], axis=1), own_lat
        )
        far_lat = z_swap(own_lat, 1)
        lats = (own_lat, core_swap(own_lat), far_lat, core_swap(far_lat))
        mixed, lse, lat, residual, normed2 = attend_call(info, x, normed, lats, *pack, gain[1][None])
        far_normed2 = z_swap(normed2, 1)
        part, saved = feed_call(info, normed2, *feed_w, f32)
        far_part, far_saved = feed_call(info, far_normed2, *feed_w, bf16)
        feed = part + z_swap(far_part, 1).astype(f32)
        out = (live * (residual + feed)).astype(bf16)
        return out, (x, normed, lat, mixed, lse, residual, normed2, far_normed2, saved, far_saved)

    def gather_rows(layer, own):
        other = lax.ppermute(own, "section", [(1 - layer, layer)])
        chip = jnp.concatenate([own, other] if layer == 0 else [other, own], axis=0)
        found = [chip]
        for step in range(1, planes):
            pairs = [(layer * planes + i, layer * planes + (i ^ step)) for i in range(planes)]
            found.append(lax.ppermute(chip, ("section", "tensor"), pairs))
        return found

    def finish_rows(firsts, seconds):
        chosen = jnp.stack([jnp.where(core == 0, a, b) for a, b in zip(firsts, seconds)])
        return by_plane(chosen, z).reshape(planes * 2 * rows, width)

    def finish_core(firsts, seconds):
        mine = jnp.where(core == 0, firsts, seconds)
        other = core_swap(jnp.where(core == 0, seconds, firsts))
        return jnp.where(core == 0, jnp.stack([mine, other]), jnp.stack([other, mine]))

    def backward(layer, grad_out, stored, pack, feed_w, before):
        x, normed, lat, mixed, lse, residual, normed2, far_normed2, saved, far_saved = stored
        gain = gains_all[layer]
        grad_res = live * grad_out.astype(f32)
        grad_feed = grad_res.astype(bf16)
        far_feed = z_swap(grad_feed, 1)
        part, rights = feed_back_call(info, grad_feed, *feed_w, saved, f32)
        if before:
            far_feed = tie(far_feed, *before.pop(0)())
        far_part, far_rights = feed_back_call(info, far_feed, *feed_w, far_saved, bf16)
        back = z_swap(far_part, 1)
        keep, send = feed_weights_call(
            info, (normed2, far_normed2, grad_feed, far_feed), (rights, far_rights), dp
        )
        feed_shape = (6, dp) + keep.shape[3:]
        feed_sum = Scatter(keep.reshape(feed_shape), send.reshape(feed_shape))
        back = tie(back, keep)
        grad_norm2 = part + back.astype(f32)
        grad_residual, gain_second = norm_back(residual, gain[1], grad_norm2)
        grad_residual = grad_residual + grad_res
        grad_branch = grad_residual.astype(bf16)
        feed_sum.split()
        feed_sum.step()
        grad_branch = tie(grad_branch, *feed_sum.leaves()[::2])
        if before:
            grad_branch = tie(grad_branch, *before.pop(0)())

        grad_norm, grad_lat, keep, send = attend_back_call(
            info, grad_branch, normed, lat, *pack, mixed, lse
        )
        pack_sum = Scatter(keep, send)
        grad_lat = grad_lat.astype(bf16).reshape(2, per_seq // 2, 2, rows, latent)
        lat_sum = lax.dynamic_index_in_dim(grad_lat, core, 2, False) + core_swap(
            lax.dynamic_index_in_dim(grad_lat, 1 - core, 2, False)
        )
        near = rank // 2
        lat_own = lax.dynamic_index_in_dim(lat_sum, near, 1, False) + z_swap(
            lax.dynamic_index_in_dim(lat_sum, 1 - near, 1, False), 1
        )
        lat_own = by_group(lat_own)
        lat_own = jnp.concatenate([lat_own[0], lat_own[1]], axis=1)
        grad_norm = grad_norm + dot_nt(lat_own, latents_w[layer])
        grad_x, gain_first = norm_back(x.astype(f32), gain[0], grad_norm)
        grad_x = (grad_x + grad_residual).astype(bf16)

        lat_w = dot_tn(normed, lat_own).astype(bf16).reshape(planes, dp, width // planes // dp * 2, latent)
        gain_g = jnp.stack([gain_first, gain_second]).astype(bf16)
        gain_g = gain_g.reshape(2, planes, dp, -1).transpose(1, 2, 0, 3).reshape(planes, dp, 1, -1)
        gain_g = jnp.pad(gain_g, ((0, 0), (0, 0), (0, 31), (0, latent - gain_g.shape[3])))
        small = by_plane(jnp.concatenate([lat_w, gain_g], axis=2), z)
        half = small.shape[2] // 2
        small_keep = lax.dynamic_slice_in_dim(small, core * half, half, 2)
        small_send = lax.dynamic_slice_in_dim(small, (1 - core) * half, half, 2)
        small_sum = small_keep + core_swap(small_send)

        def feed_rest():
            while feed_sum.halves[0][1]:
                feed_sum.step()
            return feed_sum.leaves()

        def feed_far():
            sums = feed_sum.result()
            feed_sum.final = sums[:3] + z_swap(sums[3:], planes // 2)
            return [feed_sum.final]

        def pack_first():
            pack_sum.parts = [jnp.concatenate([sum(pack_sum.parts), small_sum], axis=2)]
            pack_sum.split()
            pack_sum.step()
            return pack_sum.leaves()

        def pack_rest():
            while pack_sum.halves[0][1]:
                pack_sum.step()
            return pack_sum.leaves()

        def pack_far():
            sums = pack_sum.result()
            pair = sums[0::2] + z_swap(sums[1::2], 1)
            pack_sum.final = pair[0] + z_swap(pair[1], 2)
            return [pack_sum.final]

        return grad_x, feed_sum, pack_sum, [feed_rest, pack_first, feed_far, pack_rest, pack_far]

    pack0 = (packs[0],) + gather_pack(packs[0])
    feed0 = (feeds[0],) + gather_feed(feeds[0])
    pack1 = (packs[1],) + gather_pack(packs[1])
    feed1 = (feeds[1],) + gather_feed(feeds[1])
    out0, stored0 = forward(0, own_in, pack0, feed0)
    out1, stored1 = forward(1, out0, pack1, feed1)
    outs0, outs1 = gather_rows(0, out0), gather_rows(1, out1)
    grad1, feed_sum1, pack_sum1, rest = backward(1, own_target, stored1, pack1, feed1, [])
    grads1 = gather_rows(1, grad1)
    grad0, feed_sum0, pack_sum0, last = backward(0, grad1, stored0, pack0, feed0, rest)
    grads0 = gather_rows(0, grad0)
    for step in rest + last:
        step()
    layer_outputs = finish_rows(outs0, outs1)
    input_grads = finish_rows(grads0, grads1)

    feed_total = finish_core(feed_sum0.final, feed_sum1.final).astype(f32)
    gate_t, up_t, down_t = jnp.moveaxis(feed_total, 0, 1).reshape(3, width // dp, hidden_cols)
    halves = finish_core(pack_sum0.final, pack_sum1.final).astype(f32)
    main = pack_rows // dp // 2
    query_t, key_t = halves[0, : width // dp], halves[0, width // dp : main]
    value_t, out_t = halves[1, : latent // dp], halves[1, latent // dp : main]
    small = halves[:, main:].reshape(-1, latent)
    lat_rows = width // planes // dp * 2
    lat_t = small[:lat_rows].reshape(lat_rows // 2, 2 * latent)
    gain_t = small[lat_rows, : 2 * width // planes // dp].reshape(2, -1)
    return (
        layer_outputs[None],
        input_grads[None],
        query_t[None],
        lat_t[None],
        key_t[None],
        value_t[None],
        out_t.T[None],
        gain_t[None],
        gate_t[None],
        up_t[None],
        down_t.T[None],
    )


def solution(mesh):
    placed = (
        P("dp", None),
        P("dp", None),
        P("dp"),
        P("section", None, "tensor"),
        P("section", None, None),
        P("section", None, "tensor"),
        P("section", None, "tensor"),
        P("section", "tensor", None),
        P("section", None, None),
        P("section", None, "tensor"),
        P("section", None, "tensor"),
        P("section", "tensor", None),
    )
    return jax.shard_map(
        shards,
        mesh=mesh,
        in_specs=placed,
        out_specs=(
            P("section", "dp", None),
            P("section", "dp", None),
            P("section", "dp", "tensor"),
            P("section", ("tensor", "dp"), None),
            P("section", "dp", "tensor"),
            P("section", "dp", "tensor"),
            P("section", "tensor", "dp"),
            P("section", None, ("tensor", "dp")),
            P("section", "dp", "tensor"),
            P("section", "dp", "tensor"),
            P("section", "tensor", "dp"),
        ),
        check_vma=False,
    )
```

```python
import functools

import jax
import jax.numpy as jnp
from jax import lax
from jax.experimental import pallas as pl
from jax.experimental.pallas import tpu as pltpu
from jax.sharding import PartitionSpec as P

HEAD_DIM = 64
eps = 1e-06
masked_score = -1e30
f32 = jnp.float32
bf16 = jnp.bfloat16


def dot_nn(left, right):
    return lax.dot_general(left, right, (((1,), (0,)), ((), ())), preferred_element_type=f32)


def dot_nt(left, right):
    return lax.dot_general(left, right, (((1,), (1,)), ((), ())), preferred_element_type=f32)


def dot_tn(left, right):
    return lax.dot_general(left, right, (((0,), (0,)), ((), ())), preferred_element_type=f32)


def core_swap(value):
    return lax.ppermute(value, "section", [(0, 1), (1, 0)])


def z_swap(value, step):
    count = lax.axis_size("tensor")
    return lax.ppermute(value, "tensor", [(i, i ^ step) for i in range(count)])


def tie(first, *others):
    return lax.optimization_barrier((first,) + others)[0]


def bits_of(count):
    return [1 << i for i in range(count.bit_length() - 1)]


def plane_gather(piece):
    count = lax.axis_size("dp")
    return lax.all_to_all(jnp.broadcast_to(piece[None], (count,) + piece.shape), "dp", 0, 0)


def plane_sum(parts):
    return jnp.sum(lax.all_to_all(parts, "dp", 0, 0).astype(f32), axis=0).astype(bf16)


def by_plane(values, flip_of):
    count = values.shape[0]
    for bit in bits_of(count):
        order = [k ^ bit for k in range(count)]
        flipped = jnp.stack([values[k] for k in order])
        values = jnp.where((flip_of // bit) % 2 == 1, flipped, values)
    return values


def inverse_rms(rows):
    return lax.rsqrt(jnp.mean(rows * rows, axis=-1, keepdims=True) + eps)


def norm_back(rows, gain, grad_norm):
    scale = inverse_rms(rows)
    weighted = grad_norm * gain
    inner = jnp.mean(weighted * rows, axis=-1, keepdims=True)
    grad_rows = scale * weighted - rows * scale * scale * scale * inner
    grad_gain = jnp.sum(grad_norm * rows * scale, axis=0)
    return (grad_rows, grad_gain)


LENGTH, FIRST, CORE, MEMBER, RANK, PLANE = range(6)


def kernel_call(kernel, info, arrays, grid, in_specs, out_specs, out_shape, scratch, name, flops, transcendentals=0):
    size = sum(a.size * a.dtype.itemsize for a in arrays)
    size += sum(o.size * o.dtype.itemsize for o in out_shape)
    return pl.pallas_call(
        kernel,
        grid_spec=pltpu.PrefetchScalarGridSpec(
            num_scalar_prefetch=1,
            grid=grid,
            in_specs=in_specs,
            out_specs=out_specs,
            scratch_shapes=scratch,
        ),
        out_shape=out_shape,
        compiler_params=pltpu.CompilerParams(
            dimension_semantics=("arbitrary",) * len(grid), vmem_limit_bytes=56 * 1024 * 1024
        ),
        cost_estimate=pl.CostEstimate(flops=flops, bytes_accessed=size, transcendentals=transcendentals),
        name=name,
    )(info, *arrays)


def whole(array):
    shape = array.shape
    return pl.BlockSpec(shape, lambda i, info: (0,) * len(shape))


def lead(array):
    shape = array.shape[1:]
    return pl.BlockSpec((1,) + shape, lambda i, info: (i,) + (0,) * len(shape))


def like(shape, dtype):
    return jax.ShapeDtypeStruct(shape, dtype)


class PackCopies:
    def __init__(self, info, layer, parts, held, sems):
        self.info, self.layer, self.parts, self.held, self.sems = info, layer, parts, held, sems

    def own(self, slot, there):
        for at, (part, target) in enumerate(zip(self.parts, self.held)):
            source = part[1] if there else part[0]
            rows = source.shape[0]
            yield pltpu.make_async_copy(source, target.at[slot, pl.ds(0, rows)], self.sems.at[slot, at])

    def pieces(self, slot, step):
        at = 0
        for (_, _, near, other, begin, rows), held in zip(self.parts, self.held):
            members = near.shape[0]
            source_at = pl.multiple_of(begin + (step - 1) * rows, 16)
            for key in range(members):
                for source, core in ((near, self.info[CORE]), (other, 1 - self.info[CORE])):
                    target = pl.multiple_of((core * members + key) * rows, 16)
                    yield pltpu.make_async_copy(
                        source.at[key, pl.ds(source_at, rows)],
                        held.at[slot, pl.ds(target, rows)],
                        self.sems.at[slot, at],
                    )
                    at += 1

    def each(self, step, act):
        slot = step % 2

        def run(copies):
            for copy in copies:
                act(copy)

        there = self.info[CORE] != self.layer
        pl.when((step == 0) & there)(lambda: run(self.own(slot, True)))
        pl.when((step == 0) & jnp.logical_not(there))(lambda: run(self.own(slot, False)))
        pl.when(step > 0)(lambda: run(self.pieces(slot, step)))

    def start(self, step):
        self.each(step, lambda copy: copy.start())

    def turn(self, step, first, last):
        @pl.when(step == first)
        def _():
            self.start(step)

        @pl.when(step < last)
        def _():
            self.start(step + 1)

        self.each(step, lambda copy: copy.wait())
        return [held.at[step % 2] for held in self.held]


def pack_refs(spec, refs):
    return [tuple(refs[4 * at : 4 * at + 4]) + part for at, part in enumerate(spec)]


def fill_bias(info, bias):
    keys, rows = bias.shape
    key_pos = lax.broadcasted_iota(jnp.int32, (keys, rows), 0)
    query_pos = lax.broadcasted_iota(jnp.int32, (keys, rows), 1) + info[FIRST]
    allowed = (key_pos <= query_pos) & (key_pos < info[LENGTH])
    bias[...] = jnp.where(allowed, 0.0, masked_score)


def head_parts(heads, width, latent):
    at = (0, width, width + latent, width + 2 * latent)
    return [heads[lo:hi] for lo, hi in zip(at[:-1], at[1:])]


def attend_sets(keys, values_t, query, bias, heads):
    lane_head = lax.broadcasted_iota(jnp.int32, query.shape, 1) // HEAD_DIM
    mixed, sums = [], []
    for head in range(heads):
        query_here = jnp.where(lane_head == head, query, bf16(0))
        scores = dot_nt(keys, query_here) + bias
        peak = jnp.max(scores, axis=0, keepdims=True)
        expo = jnp.exp(scores - peak)
        total = jnp.sum(expo, axis=0, keepdims=True)
        part = dot_nn(values_t[head * HEAD_DIM : (head + 1) * HEAD_DIM], expo.astype(bf16))
        mixed.append(part * (1.0 / total))
        sums.append(peak + jnp.log(total))
    return jnp.concatenate(mixed, axis=0), jnp.concatenate(sums, axis=0)


def attend_first_kernel(
    info, x, lat_here, lat_there, heads_here, heads_there, gain_here, gain_there, out, normed, query_all, keys_all, values_t_all
):
    keys_count, width = x.shape
    latent = lat_here.shape[1]
    cols = heads_here.shape[1]
    heads = cols // HEAD_DIM
    rows = keys_count // out.shape[0]
    here = info[2] == 0
    gain = jnp.where(here, gain_here[0:1], gain_there[0:1])
    pack = jnp.where(here, heads_here[...], heads_there[...])
    w_latent = jnp.where(here, lat_here[...], lat_there[...])
    for block in range(keys_count // rows):
        here = slice(block * rows, (block + 1) * rows)
        value = x[here].astype(f32)
        normed[here] = (value * inverse_rms(value) * gain).astype(bf16)
    w_query, w_key, w_value = head_parts(pack, width, latent)
    query_all[...] = dot_nn(normed[...], w_query).astype(bf16) * bf16(HEAD_DIM**-0.5)
    lat = dot_nn(normed[...], w_latent).astype(bf16)
    keys_all[...] = dot_nn(lat, w_key).astype(bf16)
    values_t_all[...] = dot_nn(lat, w_value).astype(bf16).T
    for block in range(keys_count // rows):
        first = block * rows
        end = first + rows
        key_pos = lax.broadcasted_iota(jnp.int32, (end, rows), 0)
        query_pos = lax.broadcasted_iota(jnp.int32, (end, rows), 1) + first
        bias = jnp.where((key_pos <= query_pos) & (key_pos < info[0]), 0.0, masked_score)
        mixed, sums = attend_sets(keys_all[0:end], values_t_all[:, 0:end], query_all[first:end], bias, heads)
        high = sums.astype(bf16)
        low = (sums - high.astype(f32)).astype(bf16)
        at = info[1] ^ block
        out[at, 0:rows, :] = mixed.T.astype(bf16)
        out[at, rows:, :] = jnp.concatenate([high, low, jnp.zeros((16 - 2 * heads, rows), bf16)], axis=0)


def attend_out_kernel(
    spec, layer, info, x, m0, m1, m2, m3, gain, o0, o1, o2, o3, mixed_out, lse_out, residual, normed2, sets, outs, sems
):
    step = pl.program_id(0)
    rows, width = x.shape
    heads = lse_out.shape[1]
    copies = PackCopies(info, layer, pack_refs(spec, (o0, o1, o2, o3)), [outs], sems)
    w_out = copies.turn(step, 0, pl.num_programs(0) - 1)[0]

    @pl.when(step == 0)
    def _():
        residual[...] = x[...].astype(f32)
        for key, piece in enumerate((m0, m1, m2, m3)):
            sets[key ^ info[RANK] ^ info[PLANE]] = piece[...]

    mixed = sets[step, 0:rows, :]
    tail = sets[step, rows:, :].astype(f32)
    mixed_out[0] = mixed
    lse_out[0] = tail[0:heads] + tail[heads : 2 * heads]
    residual[...] += dot_nn(mixed, w_out[0 : mixed.shape[1]])

    @pl.when(step == pl.num_programs(0) - 1)
    def _():
        full = residual[...]
        normed2[...] = (full * inverse_rms(full) * gain[...]).astype(bf16)


def attend_kernel(
    spec, layer, info, x, normed, lat0, lat1, lat2, lat3, gain, h0, h1, h2, h3, o0, o1, o2, o3,
    mixed_out, lse_out, lat_out, residual, normed2, bias, heads_held, outs_held, sems,
):
    step = pl.program_id(0)
    rows, width = normed.shape
    latent = lat_out.shape[2]
    heads = lse_out.shape[1]
    parts = pack_refs(spec, (h0, h1, h2, h3, o0, o1, o2, o3))
    copies = PackCopies(info, layer, parts, [heads_held, outs_held], sems)
    w_heads, w_out = copies.turn(step, 0, pl.num_programs(0) - 1)

    @pl.when(step == 0)
    def _():
        fill_bias(info, bias)
        residual[...] = x[...].astype(f32)
        for key, piece in enumerate((lat0, lat1, lat2, lat3)):
            at = pl.multiple_of((info[RANK] ^ key) * rows, 16)
            for group in range(2):
                lat_out[group, pl.ds(at, rows), :] = piece[:, group * latent : (group + 1) * latent]

    w_query, w_key, w_value = head_parts(w_heads, width, latent)
    lat = lat_out[step // 2]
    query = dot_nn(normed[...], w_query).astype(bf16) * bf16(HEAD_DIM**-0.5)
    keys = dot_nn(lat, w_key).astype(bf16)
    values_t = dot_nn(lat, w_value).astype(bf16).T
    mixed, sums = attend_sets(keys, values_t, query, bias[...], heads)
    lse_out[0] = sums
    mixed = mixed.T.astype(bf16)
    mixed_out[0] = mixed
    residual[...] += dot_nn(mixed, w_out[0 : mixed.shape[1]])

    @pl.when(step == pl.num_programs(0) - 1)
    def _():
        full = residual[...]
        normed2[...] = (full * inverse_rms(full) * gain[...]).astype(bf16)


def attend_back_kernel(
    first_set, spec, layer, info, grad_branch, normed, lat, mixed_in, lse_in, h0, h1, h2, h3, o0, o1, o2, o3,
    grad_norm, grad_lat, keep, send, bias, heads_held, outs_held, sems, lat_sum,
):
    step = pl.program_id(0)
    rows, width = normed.shape
    keys_count, latent = grad_lat.shape
    cols = heads_held.shape[2]
    scale = HEAD_DIM**-0.5
    members = keep.shape[0]
    parts = pack_refs(spec, (h0, h1, h2, h3, o0, o1, o2, o3))
    copies = PackCopies(info, layer, parts, [heads_held, outs_held], sems)
    w_heads, w_out = copies.turn(step + first_set, first_set, first_set + pl.num_programs(0) - 1)

    @pl.when(step == 0)
    def _():
        fill_bias(info, bias)
        grad_norm[...] = jnp.zeros_like(grad_norm)
        lat_sum[...] = jnp.zeros_like(lat_sum)

    w_query, w_key, w_value = head_parts(w_heads, width, latent)
    here = lat[0]
    query = dot_nn(normed[...], w_query).astype(bf16) * bf16(scale)
    keys = dot_nn(here, w_key).astype(bf16)
    keys_t = keys.T
    values = dot_nn(here, w_value).astype(bf16)
    mixed = mixed_in[0]
    grad_mixed = dot_nt(grad_branch[...], w_out[0:cols]).astype(bf16)
    centre = (grad_mixed.astype(f32) * mixed.astype(f32)).T
    lane_head = lax.broadcasted_iota(jnp.int32, (rows, cols), 1) // HEAD_DIM
    grad_keys = jnp.zeros((keys_count, cols), f32)
    grad_values = jnp.zeros((keys_count, cols), f32)
    grad_query_parts = []
    for head in range(cols // HEAD_DIM):
        mine = slice(head * HEAD_DIM, (head + 1) * HEAD_DIM)
        query_here = jnp.where(lane_head == head, query, bf16(0))
        grad_here = jnp.where(lane_head == head, grad_mixed, bf16(0))
        scores = dot_nt(keys, query_here) + bias[...]
        probs = jnp.exp(scores - lse_in[0, head : head + 1, :])
        grad_probs = dot_nt(values, grad_here)
        inner = jnp.sum(centre[mine], axis=0, keepdims=True)
        grad_scores = (probs * (grad_probs - inner)).astype(bf16)
        grad_values += dot_nn(probs.astype(bf16), grad_here)
        grad_keys += dot_nn(grad_scores, query_here)
        grad_query_parts.append(dot_nn(keys_t[mine], grad_scores) * scale)
    grad_keys = grad_keys.astype(bf16)
    grad_values = grad_values.astype(bf16)
    grad_query = jnp.concatenate(grad_query_parts, axis=0).T.astype(bf16)
    grad_norm[...] += dot_nt(grad_query, w_query)
    lat_sum[...] += dot_nt(grad_keys, w_key) + dot_nt(grad_values, w_value)
    halves = (
        (dot_tn(normed[...], grad_query), dot_tn(here, grad_keys)),
        (dot_tn(here, grad_values), dot_tn(grad_branch[...], mixed)),
    )
    for half, results in enumerate(halves):
        for out, wanted in ((keep, half), (send, 1 - half)):

            @pl.when(info[CORE] == wanted)
            def _(out=out, results=results):
                at = 0
                for result in results:
                    size = result.shape[0] // members
                    for member in range(members):
                        out[member, 0, at : at + size, :] = result[member * size : (member + 1) * size].astype(bf16)
                    at += size

    @pl.when(step == pl.num_programs(0) - 1)
    def _():
        grad_lat[...] = lat_sum[...].astype(bf16)


def attend_first_call(info, x, lat_here, lat_there, heads_here, heads_there, gain_here, gain_there, keys, blocks):
    width = x.shape[1]
    latent = lat_here.shape[1] // 2
    cols = heads_here.shape[1]
    outs = [like((blocks, keys // blocks + 16, cols), bf16)]
    arrays = (x, lat_here, lat_there, heads_here, heads_there, gain_here, gain_there)
    group = pl.BlockSpec((width, latent), lambda i, info: (0, info[3]))
    return kernel_call(
        attend_first_kernel,
        info,
        arrays,
        (1,),
        [pl.BlockSpec((keys, width), lambda i, info: (info[2], 0)), group, group] + [whole(v) for v in arrays[3:]],
        [whole(o) for o in outs],
        outs,
        [pltpu.VMEM((keys, width), bf16)] + [pltpu.VMEM((keys, cols), bf16)] * 2 + [pltpu.VMEM((cols, keys), bf16)],
        "attend_first",
        2 * keys * width * (cols + latent) + 4 * keys * latent * cols + 4 * keys * keys * cols * 3,
        keys * keys * 3,
    )[0]


def pack_in(*parts):
    arrays = sum((tuple(part[0:4]) for part in parts), ())
    spec = tuple(tuple(part[4:]) for part in parts)
    members = parts[0][2].shape[0]
    scratch = [pltpu.VMEM((2, 2 * members * part[5], part[0].shape[1]), bf16) for part in parts]
    scratch.append(pltpu.SemaphoreType.DMA((2, 2 * members * len(parts))))
    return arrays, spec, [pl.BlockSpec(memory_space=pl.ANY)] * len(arrays), scratch


def attend_out_call(info, layer, x, messages, outs_w, gain):
    rows, width = x.shape
    arrays, spec, specs, scratch = pack_in(outs_w)
    sets = 4
    cols = messages[0].shape[1]
    heads = cols // HEAD_DIM
    outs = [
        like((sets, rows, cols), bf16),
        like((sets, heads, rows), f32),
        like((rows, width), f32),
        like((rows, width), bf16),
    ]
    return kernel_call(
        functools.partial(attend_out_kernel, spec, layer),
        info,
        (x, *messages, gain) + arrays,
        (sets,),
        [whole(x)] + [whole(m) for m in messages] + [whole(gain)] + specs,
        [lead(outs[0]), lead(outs[1]), whole(outs[2]), whole(outs[3])],
        outs,
        [pltpu.VMEM((sets,) + messages[0].shape, bf16)] + scratch,
        "attend_out",
        2 * sets * rows * width * cols,
    )


def attend_call(info, layer, x, normed, lats, pack, gain):
    rows, width = normed.shape
    arrays, spec, specs, scratch = pack_in(*pack)
    sets = 4
    cols = arrays[0].shape[1]
    latent = lats[0].shape[1] // 2
    keys = rows * len(lats)
    heads = cols // HEAD_DIM
    outs = [
        like((sets, rows, cols), bf16),
        like((sets, heads, rows), f32),
        like((2, keys, latent), bf16),
        like((rows, width), f32),
        like((rows, width), bf16),
    ]
    return kernel_call(
        functools.partial(attend_kernel, spec, layer),
        info,
        (x, normed, *lats, gain) + arrays,
        (sets,),
        [whole(x), whole(normed)] + [whole(v) for v in lats] + [whole(gain)] + specs,
        [lead(outs[0]), lead(outs[1])] + [whole(o) for o in outs[2:]],
        outs,
        [pltpu.VMEM((keys, rows), f32)] + scratch,
        "attend",
        2 * sets * rows * (2 * keys * cols * heads + width * cols * 2) + 4 * sets * keys * latent * cols,
        sets * heads * keys * rows,
    )


def attend_back_call(first_set, info, layer, grad_branch, normed, lat, pack, mixed, lse, members):
    rows, width = normed.shape
    arrays, spec, specs, scratch = pack_in(*pack)
    cols = arrays[0].shape[1]
    piece_rows = (arrays[0].shape[0] + width) // members // 2
    sets = 2
    keys, latent = lat.shape[1:]
    heads = cols // HEAD_DIM
    group = pl.BlockSpec((1, keys, latent), lambda i, info: (first_set // 2, 0, 0))
    outs = [
        like((rows, width), f32),
        like((keys, latent), bf16),
        like((members, sets, piece_rows, cols), bf16),
        like((members, sets, piece_rows, cols), bf16),
    ]
    summed = pl.BlockSpec((members, 1, piece_rows, cols), lambda i, info: (0, i, 0, 0))
    mine = [pl.BlockSpec((1,) + v.shape[1:], lambda i, info: (i + first_set, 0, 0)) for v in (mixed, lse)]
    return kernel_call(
        functools.partial(attend_back_kernel, first_set, spec, layer),
        info,
        (grad_branch, normed, lat, mixed, lse) + arrays,
        (sets,),
        [whole(grad_branch), whole(normed), group] + mine + specs,
        [whole(outs[0]), whole(outs[1]), summed, summed],
        outs,
        [pltpu.VMEM((keys, rows), f32)] + scratch + [pltpu.VMEM((keys, latent), f32)],
        "attend_back",
        2 * sets * rows * (5 * keys * cols * heads + width * cols * 5) + 16 * sets * keys * latent * cols,
        sets * heads * keys * rows,
    )


def feed_shards(spec, layer, info, refs, weights, sems, use):
    here, there, pieces = refs[0:3], refs[3:6], refs[6:12]
    hidden = here[0].shape[0]

    def run(act, far):
        if not far:
            for wanted, sources in ((True, here), (False, there)):

                @pl.when((info[CORE] == layer) == wanted)
                def _(sources=sources):
                    for kind, source in enumerate(sources):
                        act(pltpu.make_async_copy(source, weights.at[0, kind, pl.ds(0, hidden)], sems.at[kind]))

            return
        at = 3
        for kind, (begin, rows) in enumerate(spec):
            members = pieces[2 * kind].shape[0]
            for key in range(members):
                for source, core in ((pieces[2 * kind], info[CORE]), (pieces[2 * kind + 1], 1 - info[CORE])):
                    target = pl.multiple_of((core * members + key) * rows, 16)
                    act(
                        pltpu.make_async_copy(
                            source.at[key, pl.ds(begin, rows)], weights.at[1, kind, pl.ds(target, rows)], sems.at[at]
                        )
                    )
                    at += 1

    run(lambda copy: copy.start(), False)
    run(lambda copy: copy.start(), True)
    run(lambda copy: copy.wait(), False)
    use(0, [weights[0, kind, 0:hidden] for kind in range(3)])
    run(lambda copy: copy.wait(), True)
    use(1, [weights[1, kind, 0:hidden] for kind in range(3)])


def feed_kernel(spec, layer, info, value, *refs):
    total_out, saved, weights, sems, total = refs[12:]

    def use(shard, held):
        gate = dot_nt(value[...], held[0])
        up = dot_nt(value[...], held[1])
        saved[shard, 0] = gate.astype(bf16)
        saved[shard, 1] = up.astype(bf16)
        hidden = (gate * jax.nn.sigmoid(gate) * up).astype(bf16)
        part = dot_nn(hidden, held[2])
        if shard == 0:
            total[...] = part
        else:
            total_out[...] = (total[...] + part).astype(total_out.dtype)

    feed_shards(spec, layer, info, refs[0:12], weights, sems, use)


def feed_back_kernel(spec, layer, info, value, saved, *refs):
    total_out, keep, send, weights, sems, total = refs[12:]

    width = saved.shape[3]

    def use(shard, held):
        grad_hidden = dot_nt(value[...], held[2])
        gate = saved[shard, 0].astype(f32)
        up = saved[shard, 1].astype(f32)
        sigma = jax.nn.sigmoid(gate)
        silu = gate * sigma
        grad_gate = (grad_hidden * up * sigma * (1.0 + gate * (1.0 - sigma))).astype(bf16)
        grad_up = (grad_hidden * silu).astype(bf16)
        hidden = (silu * up).astype(bf16)
        mine = info[CORE] == layer if shard == 0 else info[CORE] != layer
        for out, wanted in ((keep, mine), (send, jnp.logical_not(mine))):

            @pl.when(wanted)
            def _(out=out):
                out[0, :, 0:width] = grad_gate
                out[1, :, 0:width] = grad_up
                out[2, :, 0:width] = hidden

        part = dot_nn(grad_gate, held[0]) + dot_nn(grad_up, held[1])
        if shard == 0:
            total[...] = part
        else:
            total_out[...] = (total[...] + part).astype(total_out.dtype)

    feed_shards(spec, layer, info, refs[0:12], weights, sems, use)


def feed_weights_kernel(hidden, info, *refs):
    lefts, rights, out, turned = refs[0:8], refs[8:12], refs[12], refs[13]
    kind = pl.program_id(0)
    rows = lefts[0].shape[0]
    members, _, size, lanes = out.shape

    @pl.when(kind == 0)
    def _():
        for at in range(2):
            for block in range(4):
                turned[at, :, block * rows : (block + 1) * rows] = lefts[4 * at + block][...].T

    right = jnp.concatenate([r[0] for r in rights], axis=0)
    left = turned[kind // 2]
    for first in range(0, hidden, 256):
        end = min(first + 256, hidden)
        result = dot_nn(left, right[:, first:end]).astype(bf16)
        for member in range(members):
            out[member, 0, :, first:end] = result[member * size : (member + 1) * size]
    out[:, :, :, hidden:] = jnp.zeros((members, 1, size, lanes - hidden), bf16)


def whole_lanes(count):
    return -(-count // 128) * 128


def feed_in(feed_w):
    here, there, pieces = feed_w
    arrays = (*here, *there, *sum((part[0:2] for part in pieces), ()))
    spec = tuple(part[2:4] for part in pieces)
    members, _, width = pieces[0][0].shape
    scratch = [
        pltpu.VMEM((2, 3, 2 * members * pieces[0][3], width), bf16),
        pltpu.SemaphoreType.DMA((3 + 6 * members,)),
    ]
    return arrays, spec, [pl.BlockSpec(memory_space=pl.ANY)] * len(arrays), scratch


def feed_call(info, layer, value, feed_w, dtype):
    rows, width = value.shape
    arrays, spec, specs, scratch = feed_in(feed_w)
    hidden = arrays[0].shape[0]
    outs = [like((rows, width), dtype), like((2, 2, rows, hidden), bf16)]
    return kernel_call(
        functools.partial(feed_kernel, spec, layer),
        info,
        (value,) + arrays,
        (1,),
        [whole(value)] + specs,
        [whole(o) for o in outs],
        outs,
        scratch + [pltpu.VMEM((rows, width), f32)],
        "feed",
        2 * 2 * 3 * rows * width * hidden,
    )


def feed_back_call(info, layer, value, saved, feed_w, dtype):
    rows, width = value.shape
    arrays, spec, specs, scratch = feed_in(feed_w)
    hidden = arrays[0].shape[0]
    outs = [like((rows, width), dtype)] + [like((3, rows, whole_lanes(hidden)), bf16)] * 2
    return kernel_call(
        functools.partial(feed_back_kernel, spec, layer),
        info,
        (value, saved) + arrays,
        (1,),
        [whole(value), whole(saved)] + specs,
        [whole(o) for o in outs],
        outs,
        scratch + [pltpu.VMEM((rows, width), f32)],
        "feed_back",
        2 * 2 * 3 * rows * width * hidden,
    )


def feed_weights_call(info, lefts, rights, members, hidden):
    rows, width = lefts[0].shape
    kinds, _, lanes = rights[0].shape
    shape = (members, kinds, width // members, lanes)
    outs = [like(shape, bf16)]
    return kernel_call(
        functools.partial(feed_weights_kernel, hidden),
        info,
        (*lefts, *rights),
        (kinds,),
        [whole(v) for v in lefts] + [lead(r) for r in rights],
        [pl.BlockSpec((members, 1) + shape[2:], lambda i, info: (0, i, 0, 0))],
        outs,
        [pltpu.VMEM((2, width, 4 * rows), bf16)],
        "feed_weights",
        2 * kinds * 4 * rows * width * hidden,
    )[0]


def shards(inputs, cotangent, lengths, w_query, w_latent, w_key, w_value, w_out, gains, w_gate, w_up, w_down):
    core = lax.axis_index("section")
    z = lax.axis_index("tensor")
    d = lax.axis_index("dp")
    planes = lax.axis_size("tensor")
    dp = lax.axis_size("dp")
    seqs = lengths.shape[0]
    bucket = inputs.shape[0] // seqs
    width = inputs.shape[1]
    layers = 2
    per_seq = planes // seqs * 2
    rows = bucket // per_seq
    rank = (z % (planes // seqs)) * 2 + core
    seq = z // (planes // seqs)
    first = rank * rows
    length = lax.dynamic_index_in_dim(lengths, seq, 0, False)
    info = jnp.stack([length, first, core, d, rank, z]).astype(jnp.int32)
    live = (lax.broadcasted_iota(jnp.int32, (rows, 1), 0) + first < length).astype(f32)
    row_at = seq * bucket + first
    own_in = lax.dynamic_slice_in_dim(inputs, row_at, rows, 0)
    own_target = lax.dynamic_slice_in_dim(cotangent, row_at, rows, 0)
    latent = w_latent.shape[2] // 2
    far_group = z // (planes // 2)

    cols = w_query.shape[2]
    hidden_cols = w_gate.shape[2]
    heads_here = jnp.concatenate([w_query[0], w_key[0], w_value[0]], axis=0)
    heads_there = core_swap(heads_here)
    lat_here = w_latent[0]
    lat_there = core_swap(lat_here)
    gain_here = gains[0]
    gain_there = core_swap(gain_here)
    out_here = w_out[0]
    feed_here = [w_gate[0].T, w_up[0].T, w_down[0]]
    head_rows, out_rows, feed_rows = heads_here.shape[0], out_here.shape[0], hidden_cols

    def piece_rows(count):
        return -(-count // (2 * dp * 16)) * 16

    def piece_of(value, side):
        rows_each = piece_rows(value.shape[0])
        value = jnp.pad(value, ((0, rows_each * 2 * dp - value.shape[0]), (0, 0)))
        return lax.dynamic_slice_in_dim(value, (side * dp + d) * rows_each, rows_each, 0)

    def feed_and_out(side):
        return jnp.concatenate([piece_of(v, side) for v in [out_here] + feed_here], axis=0)

    def layers_of(mine, received):
        return [jnp.where(core == layer, mine, received) for layer in range(layers)]

    main_pieces = layers_of(feed_and_out(core), core_swap(feed_and_out(1 - core)))
    head_pieces = layers_of(piece_of(heads_here, core), core_swap(piece_of(heads_here, 1 - core)))
    head_piece, out_piece, feed_piece = piece_rows(head_rows), piece_rows(out_rows), piece_rows(feed_rows)
    over = [z_swap(main_pieces[0][:out_piece], step) for step in range(1, lax.axis_size("tensor"))]
    feed_far = z_swap(main_pieces[0][out_piece:], planes // 2)
    out_there = core_swap(tie(out_here, feed_far))
    feed_there = [core_swap(tie(v, feed_far)) for v in feed_here]
    latents_w = [jnp.where(core == layer, lat_here, lat_there) for layer in range(layers)]
    gains_all = [jnp.where(core == layer, gain_here, gain_there) for layer in range(layers)]

    def over_planes(piece):
        return [z_swap(piece, step) for step in range(1, planes)]

    def gather_near(parts, *before):
        return plane_gather(jnp.concatenate([tie(v, *before) for v in parts], axis=0))

    def gather(parts, before=(), after=()):
        near = gather_near(parts, *before)
        return near, core_swap(tie(near, *after))

    def gather_slow(parts, before=()):
        return lax.all_gather(jnp.concatenate([tie(v, *before) for v in parts], axis=0), "dp", axis=0, tiled=False)

    def by_group(value):
        return by_plane(value, far_group)

    def normalise(x, gain):
        x = x.astype(f32)
        return (x * inverse_rms(x) * gain).astype(bf16)

    def first_attention(*after):
        scalars = jnp.stack([lax.dynamic_index_in_dim(lengths, core, 0, False), z, core, far_group]).astype(jnp.int32)
        out = attend_first_call(
            scalars, inputs, lat_here, lat_there, tie(heads_here, *after), heads_there, gain_here, gain_there, bucket, per_seq
        )
        messages = []
        for way in range(per_seq):
            pairs = []
            for side in range(2):
                for plane in range(planes):
                    to = plane ^ way
                    target = (to % 2) * planes + side * (planes // seqs) + to // 2
                    pairs.append((side * planes + plane, target))
            messages.append(lax.ppermute(out[way], ("section", "tensor"), pairs))
        return out, messages

    def first_latents(*after):
        all_rows = tie(lax.dynamic_slice_in_dim(inputs, seq * bucket, bucket, 0), *after)
        lat = dot_nn(normalise(all_rows, gains_all[0][0]), latents_w[0]).astype(bf16)
        return by_group(jnp.stack([lat[:, :latent], lat[:, latent:]]))

    def attention(layer, x, pack):
        gain = gains_all[layer]
        normed = normalise(x, gain[0])
        own_lat = dot_nn(normed, latents_w[layer]).astype(bf16)
        own_lat = jnp.where(
            far_group == 1, jnp.concatenate([own_lat[:, latent:], own_lat[:, :latent]], axis=1), own_lat
        )
        far_lat = z_swap(own_lat, 1)
        lats = (own_lat, core_swap(own_lat), far_lat, core_swap(far_lat))
        mixed, lse, lat, residual, normed2 = attend_call(info, layer, x, normed, lats, pack, gain[1][None])
        return normed, lat, mixed, lse, residual, normed2

    def feed_own(layer, normed2, feed_w):
        far_normed2 = z_swap(normed2, 1)
        part, saved = feed_call(info, layer, normed2, feed_w, f32)
        return part, saved, tie(far_normed2, part)

    def feed_rest(layer, residual, part, far_normed2, feed_w):
        far_part, far_saved = feed_call(info, layer, far_normed2, feed_w, bf16)
        feed = part + z_swap(far_part, 1).astype(f32)
        return (live * (residual + feed)).astype(bf16), far_saved

    def finish_core(firsts, seconds):
        mine = jnp.where(core == 0, firsts, seconds)
        other = core_swap(jnp.where(core == 0, seconds, firsts))
        return jnp.where(core == 0, jnp.stack([mine, other]), jnp.stack([other, mine]))

    def backward(layer, grad_out, x, normed, lat, mixed, lse, residual, feed_kept, pack, feed_w, hooks):
        normed2, far_normed2, saved, far_saved = feed_kept
        gain = gains_all[layer]
        grad_res = live * grad_out.astype(f32)
        grad_feed = grad_res.astype(bf16)
        far_feed = z_swap(grad_feed, 1)
        part, *rights = feed_back_call(info, layer, grad_feed, saved, feed_w, f32)
        far_part, *far_rights = feed_back_call(info, layer, far_feed, far_saved, feed_w, bf16)
        back = z_swap(far_part, 1)
        lefts = [normed2, far_normed2, core_swap(normed2), core_swap(far_normed2)]
        lefts += [grad_feed, far_feed, core_swap(grad_feed), core_swap(far_feed)]
        rights = [rights[0], far_rights[0], core_swap(rights[1]), core_swap(far_rights[1])]
        feed_grads = feed_weights_call(info, lefts, rights, dp, hidden_cols)
        back = tie(back, feed_grads, *hooks[0]())
        grad_norm2 = part + back.astype(f32)
        grad_residual, gain_second = norm_back(residual, gain[1], grad_norm2)
        grad_residual = grad_residual + grad_res
        grad_branch = grad_residual.astype(bf16)

        feed_parts = lax.all_to_all(feed_grads, "dp", 0, 0)
        grad_norms = []
        lat_parts = []
        pack_parts_here = []
        for first_set in (2, 0):
            if first_set == 0:
                grad_branch = tie(grad_branch, grad_norms[0], *hooks[1](grad_branch))
            grad_norm, grad_lat, pack_keep, pack_send = attend_back_call(
                first_set, info, layer, grad_branch, normed, lat, pack, mixed, lse, dp
            )
            grad_norms.append(grad_norm)
            pack_parts_here.append((pack_keep, core_swap(pack_send)))
            grad_lat = grad_lat.reshape(per_seq // 2, 2, rows, latent)
            total = lax.dynamic_index_in_dim(grad_lat, core, 1, False) + core_swap(
                lax.dynamic_index_in_dim(grad_lat, 1 - core, 1, False)
            )
            near = rank // 2
            total = lax.dynamic_index_in_dim(total, near, 0, False) + z_swap(
                lax.dynamic_index_in_dim(total, 1 - near, 0, False), 1
            )
            lat_parts.append(total)
        if layer == 0:
            lat_parts[1] = tie(lat_parts[1], *hooks[2]())
        else:
            lat_parts[1] = tie(lat_parts[1], feed_parts)
        lat_own = by_group(jnp.stack(lat_parts[::-1]))
        lat_own = jnp.concatenate([lat_own[0], lat_own[1]], axis=1)
        grad_norm = grad_norms[0] + grad_norms[1] + dot_nt(lat_own, latents_w[layer])
        grad_x, gain_first = norm_back(x.astype(f32), gain[0], grad_norm)
        grad_x = (grad_x + grad_residual).astype(bf16)

        lat_w = dot_tn(normed, lat_own).astype(bf16).reshape(planes, dp, width // planes // dp * 2, latent)
        gain_g = jnp.stack([gain_first, gain_second]).astype(bf16)
        gain_g = gain_g.reshape(2, planes, dp, -1).transpose(1, 2, 0, 3).reshape(planes, dp, 1, -1)
        gain_g = jnp.pad(gain_g, ((0, 0), (0, 0), (0, 31), (0, latent - gain_g.shape[3])))
        small = jnp.swapaxes(by_plane(jnp.concatenate([lat_w, gain_g], axis=2), z), 0, 1)
        half = small.shape[2] // 2
        small_keep = lax.dynamic_slice_in_dim(small, core * half, half, 2)
        small_send = lax.dynamic_slice_in_dim(small, (1 - core) * half, half, 2)
        small_parts = (small_keep, core_swap(small_send))

        feed_sums = jnp.sum(tie(feed_parts, grad_x).astype(f32), axis=0).astype(bf16)
        pack_total = jnp.concatenate([a + b for a, b in pack_parts_here[::-1]], axis=1)
        small_total = small_parts[0] + small_parts[1]
        if layer == 0:
            pack_total = tie(pack_total, grad_x)
            small_total = tie(small_total, grad_x)
        pack_parts = lax.all_to_all(jnp.concatenate([pack_total, small_total], axis=2), "dp", 0, 0)

        def finish_feed():
            pairs = [((1 - layer) * planes + i, layer * planes + (i ^ (planes // 2))) for i in range(planes)]
            return feed_sums.astype(f32) + lax.ppermute(feed_sums, ("section", "tensor"), pairs).astype(f32)

        def finish_pack(*after):
            parts = tie(pack_parts, *after)
            sums = jnp.sum(parts.astype(f32), axis=0).astype(bf16)
            sums = sums[0::2] + z_swap(sums[1::2], 1)
            return sums[0] + z_swap(sums[1], 2)

        return grad_x, finish_feed, finish_pack

    first_out, messages = first_attention(feed_far)
    main0 = gather(over + [feed_far], (), messages)
    outs0 = (out_here, out_there) + main0 + (0, out_piece)
    at = (planes - 1) * out_piece
    feed0 = (feed_here, feed_there, [main0 + (at + k * feed_piece, feed_piece) for k in range(3)])
    lat0 = first_latents()
    mixed0, lse0, residual0, normed2_0 = attend_out_call(info, 0, tie(own_in, lat0), messages, outs0, gains_all[0][1][None])
    near_heads1 = gather_slow(over_planes(head_pieces[1]), (first_out,))
    part0, saved0, far_normed2 = feed_own(0, normed2_0, feed0)
    far_normed2 = tie(far_normed2, near_heads1)
    main_piece = tie(main_pieces[1], *messages)
    far_main = over_planes(main_piece[:out_piece]) + [z_swap(main_piece[out_piece:], planes // 2)]
    near1 = gather_near(far_main, part0)
    out0, far_saved0 = feed_rest(0, residual0, part0, far_normed2, feed0)
    kept0 = [normed2_0, far_normed2, saved0, far_saved0]
    main1 = near1, core_swap(tie(near1, out0))
    heads1 = (heads_here, heads_there, near_heads1, core_swap(near_heads1), 0, head_piece)
    outs1 = (out_here, out_there) + main1 + (0, out_piece)
    feed1 = (feed_here, feed_there, [main1 + (at + k * feed_piece, feed_piece) for k in range(3)])

    normed1, lat1, mixed1, lse1, residual1, normed2_1 = attention(1, out0, (heads1, outs1))
    part1, saved1, far_normed2 = feed_own(1, normed2_1, feed1)
    out1, far_saved1 = feed_rest(1, residual1, part1, far_normed2, feed1)
    kept1 = [normed2_1, far_normed2, saved1, far_saved1]
    far_heads = over_planes(head_pieces[0])
    near_heads0 = gather_slow(far_heads, (normed2_1,))
    heads0 = (heads_here, heads_there, near_heads0, core_swap(tie(near_heads0, out1)), 0, head_piece)

    def gather_rows(own):
        return lax.all_gather(own, "tensor", axis=0, tiled=False)

    def finish_rows(firsts, seconds):
        mine = jnp.where(core == 0, firsts, seconds)
        other = core_swap(jnp.where(core == 0, seconds, firsts))
        both = jnp.where(core == 0, jnp.stack([mine, other], axis=1), jnp.stack([other, mine], axis=1))
        return both.reshape(planes * 2 * rows, width)

    rows_out = [gather_rows(out0), gather_rows(out1)]
    grad1, finish_feed1, finish_pack1 = backward(
        1, own_target, out0, normed1, lat1, mixed1, lse1, residual1, kept1, (heads1, outs1), feed1,
        [lambda: (rows_out[0],), lambda token: ()],
    )
    normed0 = normalise(own_in, gains_all[0][0])
    later = {}

    def during_attention(token):
        later["feed"] = finish_feed1()
        return (later["feed"],)

    def after_attention():
        later["pack"] = finish_pack1()
        later["grad"] = gather_rows(grad1)
        return (later["pack"], later["grad"])

    grad0, finish_feed0, finish_pack0 = backward(
        0, grad1, own_in, normed0, lat0, mixed0, lse0, residual0, kept0, (heads0, outs0), feed0,
        [lambda: (rows_out[1],), during_attention, after_attention],
    )
    rows_grad0 = gather_rows(grad0)
    layer_outputs = finish_rows(*rows_out)
    input_grads = finish_rows(rows_grad0, later["grad"])

    feed_final0 = finish_feed0()
    feed_total = jnp.where(core == 0, feed_final0, later["feed"])
    gate_t, up_t, down_t = feed_total[:, :, :hidden_cols]
    halves = finish_core(finish_pack0(feed_final0), later["pack"]).astype(f32)
    main = (head_rows + width) // dp // 2
    query_t, key_t = halves[0, : width // dp], halves[0, width // dp : main]
    value_t, out_t = halves[1, : latent // dp], halves[1, latent // dp : main]
    small = halves[:, main:].reshape(-1, latent)
    lat_rows = width // planes // dp * 2
    lat_t = small[:lat_rows].reshape(lat_rows // 2, 2 * latent)
    gain_t = small[lat_rows, : 2 * width // planes // dp].reshape(2, -1)
    return (
        layer_outputs[None],
        input_grads[None],
        query_t[None],
        lat_t[None],
        key_t[None],
        value_t[None],
        out_t.T[None],
        gain_t[None],
        gate_t[None],
        up_t[None],
        down_t.T[None],
    )


def solution(mesh):
    placed = (
        P("dp", None),
        P("dp", None),
        P("dp"),
        P("section", None, "tensor"),
        P("section", None, None),
        P("section", None, "tensor"),
        P("section", None, "tensor"),
        P("section", "tensor", None),
        P("section", None, None),
        P("section", None, "tensor"),
        P("section", None, "tensor"),
        P("section", "tensor", None),
    )
    return jax.shard_map(
        shards,
        mesh=mesh,
        in_specs=placed,
        out_specs=(
            P("section", "dp", None),
            P("section", "dp", None),
            P("section", "dp", "tensor"),
            P("section", ("tensor", "dp"), None),
            P("section", "dp", "tensor"),
            P("section", "dp", "tensor"),
            P("section", "tensor", "dp"),
            P("section", None, ("tensor", "dp")),
            P("section", "dp", "tensor"),
            P("section", "dp", "tensor"),
            P("section", "tensor", "dp"),
        ),
        check_vma=False,
    )
```

```python
import functools

import jax
import jax.numpy as jnp
from jax import lax
from jax.experimental import pallas as pl
from jax.experimental.pallas import tpu as pltpu
from jax.sharding import PartitionSpec as P

HEAD_DIM = 64
eps = 1e-06
masked_score = -1e30
f32 = jnp.float32
bf16 = jnp.bfloat16


def dot_nn(left, right):
    return lax.dot_general(left, right, (((1,), (0,)), ((), ())), preferred_element_type=f32)


def dot_nt(left, right):
    return lax.dot_general(left, right, (((1,), (1,)), ((), ())), preferred_element_type=f32)


def dot_tn(left, right):
    return lax.dot_general(left, right, (((0,), (0,)), ((), ())), preferred_element_type=f32)


def core_swap(value):
    return lax.ppermute(value, "section", [(0, 1), (1, 0)])


def z_swap(value, step):
    count = lax.axis_size("tensor")
    return lax.ppermute(value, "tensor", [(i, i ^ step) for i in range(count)])


def tie(first, *others):
    return lax.optimization_barrier((first,) + others)[0]


def bits_of(count):
    return [1 << i for i in range(count.bit_length() - 1)]


def plane_gather(piece):
    count = lax.axis_size("dp")
    return lax.all_to_all(jnp.broadcast_to(piece[None], (count,) + piece.shape), "dp", 0, 0)


def plane_sum(parts):
    return jnp.sum(lax.all_to_all(parts, "dp", 0, 0).astype(f32), axis=0).astype(bf16)


def by_plane(values, flip_of):
    count = values.shape[0]
    for bit in bits_of(count):
        order = [k ^ bit for k in range(count)]
        flipped = jnp.stack([values[k] for k in order])
        values = jnp.where((flip_of // bit) % 2 == 1, flipped, values)
    return values


def inverse_rms(rows):
    return lax.rsqrt(jnp.mean(rows * rows, axis=-1, keepdims=True) + eps)


def norm_back(rows, gain, grad_norm):
    scale = inverse_rms(rows)
    weighted = grad_norm * gain
    inner = jnp.mean(weighted * rows, axis=-1, keepdims=True)
    grad_rows = scale * weighted - rows * scale * scale * scale * inner
    grad_gain = jnp.sum(grad_norm * rows * scale, axis=0)
    return (grad_rows, grad_gain)


LENGTH, FIRST, CORE, MEMBER, RANK, PLANE = range(6)


def kernel_call(kernel, info, arrays, grid, in_specs, out_specs, out_shape, scratch, name, flops, transcendentals=0):
    size = sum(a.size * a.dtype.itemsize for a in arrays)
    size += sum(o.size * o.dtype.itemsize for o in out_shape)
    return pl.pallas_call(
        kernel,
        grid_spec=pltpu.PrefetchScalarGridSpec(
            num_scalar_prefetch=1,
            grid=grid,
            in_specs=in_specs,
            out_specs=out_specs,
            scratch_shapes=scratch,
        ),
        out_shape=out_shape,
        compiler_params=pltpu.CompilerParams(
            dimension_semantics=("arbitrary",) * len(grid), vmem_limit_bytes=52 * 1024 * 1024
        ),
        cost_estimate=pl.CostEstimate(flops=flops, bytes_accessed=size, transcendentals=transcendentals),
        name=name,
    )(info, *arrays)


def whole(array):
    shape = array.shape
    return pl.BlockSpec(shape, lambda i, info: (0,) * len(shape))


def lead(array):
    shape = array.shape[1:]
    return pl.BlockSpec((1,) + shape, lambda i, info: (i,) + (0,) * len(shape))


def like(shape, dtype):
    return jax.ShapeDtypeStruct(shape, dtype)


class PackCopies:
    def __init__(self, info, layer, parts, held, sems):
        self.info, self.layer, self.parts, self.held, self.sems = info, layer, parts, held, sems

    def own(self, slot, there):
        for at, (part, target) in enumerate(zip(self.parts, self.held)):
            source = part[1] if there else part[0]
            rows = source.shape[0]
            yield pltpu.make_async_copy(source, target.at[slot, pl.ds(0, rows)], self.sems.at[slot, at])

    def pieces(self, slot, step):
        at = 0
        for (_, _, near, other, begin, rows), held in zip(self.parts, self.held):
            members = near.shape[0]
            source_at = pl.multiple_of(begin + (step - 1) * rows, 16)
            for key in range(members):
                for source, core in ((near, self.info[CORE]), (other, 1 - self.info[CORE])):
                    target = pl.multiple_of((core * members + key) * rows, 16)
                    yield pltpu.make_async_copy(
                        source.at[key, pl.ds(source_at, rows)],
                        held.at[slot, pl.ds(target, rows)],
                        self.sems.at[slot, at],
                    )
                    at += 1

    def each(self, step, act):
        slot = step % 2

        def run(copies):
            for copy in copies:
                act(copy)

        there = self.info[CORE] != self.layer
        pl.when((step == 0) & there)(lambda: run(self.own(slot, True)))
        pl.when((step == 0) & jnp.logical_not(there))(lambda: run(self.own(slot, False)))
        pl.when(step > 0)(lambda: run(self.pieces(slot, step)))

    def start(self, step):
        self.each(step, lambda copy: copy.start())

    def turn(self, step, first, last):
        @pl.when(step == first)
        def _():
            self.start(step)

        @pl.when(step < last)
        def _():
            self.start(step + 1)

        self.each(step, lambda copy: copy.wait())
        return [held.at[step % 2] for held in self.held]


def pack_refs(spec, refs):
    return [tuple(refs[4 * at : 4 * at + 4]) + part for at, part in enumerate(spec)]


def fill_bias(info, bias):
    keys, rows = bias.shape
    key_pos = lax.broadcasted_iota(jnp.int32, (keys, rows), 0)
    query_pos = lax.broadcasted_iota(jnp.int32, (keys, rows), 1) + info[FIRST]
    allowed = (key_pos <= query_pos) & (key_pos < info[LENGTH])
    bias[...] = jnp.where(allowed, 0.0, masked_score)


def head_parts(heads, width, latent):
    at = (0, width, width + latent, width + 2 * latent)
    return [heads[lo:hi] for lo, hi in zip(at[:-1], at[1:])]


def attend_sets(keys, values_t, query, bias, heads):
    lane_head = lax.broadcasted_iota(jnp.int32, query.shape, 1) // HEAD_DIM
    mixed, sums = [], []
    for head in range(heads):
        query_here = jnp.where(lane_head == head, query, bf16(0))
        scores = dot_nt(keys, query_here) + bias
        peak = jnp.max(scores, axis=0, keepdims=True)
        expo = jnp.exp(scores - peak)
        total = jnp.sum(expo, axis=0, keepdims=True)
        part = dot_nn(values_t[head * HEAD_DIM : (head + 1) * HEAD_DIM], expo.astype(bf16))
        mixed.append(part * (1.0 / total))
        sums.append(peak + jnp.log(total))
    return jnp.concatenate(mixed, axis=0), jnp.concatenate(sums, axis=0)


def attend_first_kernel(
    info, x, lat_here, lat_there, heads_here, heads_there, gain_here, gain_there, out, normed, query_all, keys_all, values_t_all
):
    keys_count, width = x.shape
    latent = lat_here.shape[1]
    cols = heads_here.shape[1]
    heads = cols // HEAD_DIM
    rows = keys_count // out.shape[0]
    here = info[2] == 0
    gain = jnp.where(here, gain_here[0:1], gain_there[0:1])
    pack = jnp.where(here, heads_here[...], heads_there[...])
    w_latent = jnp.where(here, lat_here[...], lat_there[...])
    for block in range(keys_count // rows):
        here = slice(block * rows, (block + 1) * rows)
        value = x[here].astype(f32)
        normed[here] = (value * inverse_rms(value) * gain).astype(bf16)
    w_query, w_key, w_value = head_parts(pack, width, latent)
    query_all[...] = dot_nn(normed[...], w_query).astype(bf16) * bf16(HEAD_DIM**-0.5)
    lat = dot_nn(normed[...], w_latent).astype(bf16)
    keys_all[...] = dot_nn(lat, w_key).astype(bf16)
    values_t_all[...] = dot_nn(lat, w_value).astype(bf16).T
    for block in range(keys_count // rows):
        first = block * rows
        end = first + rows
        key_pos = lax.broadcasted_iota(jnp.int32, (end, rows), 0)
        query_pos = lax.broadcasted_iota(jnp.int32, (end, rows), 1) + first
        bias = jnp.where((key_pos <= query_pos) & (key_pos < info[0]), 0.0, masked_score)
        mixed, sums = attend_sets(keys_all[0:end], values_t_all[:, 0:end], query_all[first:end], bias, heads)
        high = sums.astype(bf16)
        low = (sums - high.astype(f32)).astype(bf16)
        at = info[1] ^ block
        out[at, 0:rows, :] = mixed.T.astype(bf16)
        out[at, rows:, :] = jnp.concatenate([high, low, jnp.zeros((16 - 2 * heads, rows), bf16)], axis=0)


def attend_out_kernel(
    spec, layer, info, x, m0, m1, m2, m3, gain, o0, o1, o2, o3, mixed_out, lse_out, residual, normed2, sets, outs, sems
):
    step = pl.program_id(0)
    rows, width = x.shape
    heads = lse_out.shape[1]
    copies = PackCopies(info, layer, pack_refs(spec, (o0, o1, o2, o3)), [outs], sems)
    w_out = copies.turn(step, 0, pl.num_programs(0) - 1)[0]

    @pl.when(step == 0)
    def _():
        residual[...] = x[...].astype(f32)
        for key, piece in enumerate((m0, m1, m2, m3)):
            sets[key ^ info[RANK] ^ info[PLANE]] = piece[...]

    mixed = sets[step, 0:rows, :]
    tail = sets[step, rows:, :].astype(f32)
    mixed_out[0] = mixed
    lse_out[0] = tail[0:heads] + tail[heads : 2 * heads]
    residual[...] += dot_nn(mixed, w_out[0 : mixed.shape[1]])

    @pl.when(step == pl.num_programs(0) - 1)
    def _():
        full = residual[...]
        normed2[...] = (full * inverse_rms(full) * gain[...]).astype(bf16)


def attend_kernel(
    spec, layer, info, x, normed, lat0, lat1, lat2, lat3, gain, h0, h1, h2, h3, o0, o1, o2, o3,
    mixed_out, lse_out, lat_out, residual, normed2, bias, heads_held, outs_held, sems,
):
    step = pl.program_id(0)
    rows, width = normed.shape
    latent = lat_out.shape[2]
    heads = lse_out.shape[1]
    parts = pack_refs(spec, (h0, h1, h2, h3, o0, o1, o2, o3))
    copies = PackCopies(info, layer, parts, [heads_held, outs_held], sems)
    w_heads, w_out = copies.turn(step, 0, pl.num_programs(0) - 1)

    @pl.when(step == 0)
    def _():
        fill_bias(info, bias)
        residual[...] = x[...].astype(f32)
        for key, piece in enumerate((lat0, lat1, lat2, lat3)):
            at = pl.multiple_of((info[RANK] ^ key) * rows, 16)
            for group in range(2):
                lat_out[group, pl.ds(at, rows), :] = piece[:, group * latent : (group + 1) * latent]

    w_query, w_key, w_value = head_parts(w_heads, width, latent)
    lat = lat_out[step // 2]
    query = dot_nn(normed[...], w_query).astype(bf16) * bf16(HEAD_DIM**-0.5)
    keys = dot_nn(lat, w_key).astype(bf16)
    values_t = dot_nn(lat, w_value).astype(bf16).T
    mixed, sums = attend_sets(keys, values_t, query, bias[...], heads)
    lse_out[0] = sums
    mixed = mixed.T.astype(bf16)
    mixed_out[0] = mixed
    residual[...] += dot_nn(mixed, w_out[0 : mixed.shape[1]])

    @pl.when(step == pl.num_programs(0) - 1)
    def _():
        full = residual[...]
        normed2[...] = (full * inverse_rms(full) * gain[...]).astype(bf16)


def attend_back_kernel(
    first_set, spec, layer, info, grad_branch, normed, lat, mixed_in, lse_in, h0, h1, h2, h3, o0, o1, o2, o3,
    grad_norm, grad_lat, keep, send, bias, heads_held, outs_held, sems, lat_sum,
):
    step = pl.program_id(0)
    rows, width = normed.shape
    keys_count, latent = grad_lat.shape
    cols = heads_held.shape[2]
    scale = HEAD_DIM**-0.5
    members = keep.shape[0]
    parts = pack_refs(spec, (h0, h1, h2, h3, o0, o1, o2, o3))
    copies = PackCopies(info, layer, parts, [heads_held, outs_held], sems)
    w_heads, w_out = copies.turn(step + first_set, first_set, first_set + pl.num_programs(0) - 1)

    @pl.when(step == 0)
    def _():
        fill_bias(info, bias)
        grad_norm[...] = jnp.zeros_like(grad_norm)
        lat_sum[...] = jnp.zeros_like(lat_sum)

    w_query, w_key, w_value = head_parts(w_heads, width, latent)
    here = lat[0]
    query = dot_nn(normed[...], w_query).astype(bf16) * bf16(scale)
    keys = dot_nn(here, w_key).astype(bf16)
    keys_t = keys.T
    values = dot_nn(here, w_value).astype(bf16)
    mixed = mixed_in[0]
    grad_mixed = dot_nt(grad_branch[...], w_out[0:cols]).astype(bf16)
    centre = (grad_mixed.astype(f32) * mixed.astype(f32)).T
    lane_head = lax.broadcasted_iota(jnp.int32, (rows, cols), 1) // HEAD_DIM
    grad_keys = jnp.zeros((keys_count, cols), f32)
    grad_values = jnp.zeros((keys_count, cols), f32)
    grad_query_parts = []
    for head in range(cols // HEAD_DIM):
        mine = slice(head * HEAD_DIM, (head + 1) * HEAD_DIM)
        query_here = jnp.where(lane_head == head, query, bf16(0))
        grad_here = jnp.where(lane_head == head, grad_mixed, bf16(0))
        scores = dot_nt(keys, query_here) + bias[...]
        probs = jnp.exp(scores - lse_in[0, head : head + 1, :])
        grad_probs = dot_nt(values, grad_here)
        inner = jnp.sum(centre[mine], axis=0, keepdims=True)
        grad_scores = (probs * (grad_probs - inner)).astype(bf16)
        grad_values += dot_nn(probs.astype(bf16), grad_here)
        grad_keys += dot_nn(grad_scores, query_here)
        grad_query_parts.append(dot_nn(keys_t[mine], grad_scores) * scale)
    grad_keys = grad_keys.astype(bf16)
    grad_values = grad_values.astype(bf16)
    grad_query = jnp.concatenate(grad_query_parts, axis=0).T.astype(bf16)
    grad_norm[...] += dot_nt(grad_query, w_query)
    lat_sum[...] += dot_nt(grad_keys, w_key) + dot_nt(grad_values, w_value)
    halves = (
        (dot_tn(normed[...], grad_query), dot_tn(here, grad_keys)),
        (dot_tn(here, grad_values), dot_tn(grad_branch[...], mixed)),
    )
    for half, results in enumerate(halves):
        for out, wanted in ((keep, half), (send, 1 - half)):

            @pl.when(info[CORE] == wanted)
            def _(out=out, results=results):
                at = 0
                for result in results:
                    size = result.shape[0] // members
                    for member in range(members):
                        out[member, 0, at : at + size, :] = result[member * size : (member + 1) * size].astype(bf16)
                    at += size

    @pl.when(step == pl.num_programs(0) - 1)
    def _():
        grad_lat[...] = lat_sum[...].astype(bf16)


def attend_first_call(info, x, lat_here, lat_there, heads_here, heads_there, gain_here, gain_there, keys, blocks):
    width = x.shape[1]
    latent = lat_here.shape[1] // 2
    cols = heads_here.shape[1]
    outs = [like((blocks, keys // blocks + 16, cols), bf16)]
    arrays = (x, lat_here, lat_there, heads_here, heads_there, gain_here, gain_there)
    group = pl.BlockSpec((width, latent), lambda i, info: (0, info[3]))
    return kernel_call(
        attend_first_kernel,
        info,
        arrays,
        (1,),
        [pl.BlockSpec((keys, width), lambda i, info: (info[2], 0)), group, group] + [whole(v) for v in arrays[3:]],
        [whole(o) for o in outs],
        outs,
        [pltpu.VMEM((keys, width), bf16)] + [pltpu.VMEM((keys, cols), bf16)] * 2 + [pltpu.VMEM((cols, keys), bf16)],
        "attend_first",
        2 * keys * width * (cols + latent) + 4 * keys * latent * cols + 4 * keys * keys * cols * 3,
        keys * keys * 3,
    )[0]


def pack_in(*parts):
    arrays = sum((tuple(part[0:4]) for part in parts), ())
    spec = tuple(tuple(part[4:]) for part in parts)
    members = parts[0][2].shape[0]
    scratch = [pltpu.VMEM((2, 2 * members * part[5], part[0].shape[1]), bf16) for part in parts]
    scratch.append(pltpu.SemaphoreType.DMA((2, 2 * members * len(parts))))
    return arrays, spec, [pl.BlockSpec(memory_space=pl.ANY)] * len(arrays), scratch


def attend_out_call(info, layer, x, messages, outs_w, gain):
    rows, width = x.shape
    arrays, spec, specs, scratch = pack_in(outs_w)
    sets = 4
    cols = messages[0].shape[1]
    heads = cols // HEAD_DIM
    outs = [
        like((sets, rows, cols), bf16),
        like((sets, heads, rows), f32),
        like((rows, width), f32),
        like((rows, width), bf16),
    ]
    return kernel_call(
        functools.partial(attend_out_kernel, spec, layer),
        info,
        (x, *messages, gain) + arrays,
        (sets,),
        [whole(x)] + [whole(m) for m in messages] + [whole(gain)] + specs,
        [lead(outs[0]), lead(outs[1]), whole(outs[2]), whole(outs[3])],
        outs,
        [pltpu.VMEM((sets,) + messages[0].shape, bf16)] + scratch,
        "attend_out",
        2 * sets * rows * width * cols,
    )


def attend_call(info, layer, x, normed, lats, pack, gain):
    rows, width = normed.shape
    arrays, spec, specs, scratch = pack_in(*pack)
    sets = 4
    cols = arrays[0].shape[1]
    latent = lats[0].shape[1] // 2
    keys = rows * len(lats)
    heads = cols // HEAD_DIM
    outs = [
        like((sets, rows, cols), bf16),
        like((sets, heads, rows), f32),
        like((2, keys, latent), bf16),
        like((rows, width), f32),
        like((rows, width), bf16),
    ]
    return kernel_call(
        functools.partial(attend_kernel, spec, layer),
        info,
        (x, normed, *lats, gain) + arrays,
        (sets,),
        [whole(x), whole(normed)] + [whole(v) for v in lats] + [whole(gain)] + specs,
        [lead(outs[0]), lead(outs[1])] + [whole(o) for o in outs[2:]],
        outs,
        [pltpu.VMEM((keys, rows), f32)] + scratch,
        "attend",
        2 * sets * rows * (2 * keys * cols * heads + width * cols * 2) + 4 * sets * keys * latent * cols,
        sets * heads * keys * rows,
    )


def attend_back_call(first_set, info, layer, grad_branch, normed, lat, pack, mixed, lse, members):
    rows, width = normed.shape
    arrays, spec, specs, scratch = pack_in(*pack)
    cols = arrays[0].shape[1]
    piece_rows = (arrays[0].shape[0] + width) // members // 2
    sets = 2
    keys, latent = lat.shape[1:]
    heads = cols // HEAD_DIM
    group = pl.BlockSpec((1, keys, latent), lambda i, info: (first_set // 2, 0, 0))
    outs = [
        like((rows, width), f32),
        like((keys, latent), bf16),
        like((members, sets, piece_rows, cols), bf16),
        like((members, sets, piece_rows, cols), bf16),
    ]
    summed = pl.BlockSpec((members, 1, piece_rows, cols), lambda i, info: (0, i, 0, 0))
    mine = [pl.BlockSpec((1,) + v.shape[1:], lambda i, info: (i + first_set, 0, 0)) for v in (mixed, lse)]
    return kernel_call(
        functools.partial(attend_back_kernel, first_set, spec, layer),
        info,
        (grad_branch, normed, lat, mixed, lse) + arrays,
        (sets,),
        [whole(grad_branch), whole(normed), group] + mine + specs,
        [whole(outs[0]), whole(outs[1]), summed, summed],
        outs,
        [pltpu.VMEM((keys, rows), f32)] + scratch + [pltpu.VMEM((keys, latent), f32)],
        "attend_back",
        2 * sets * rows * (5 * keys * cols * heads + width * cols * 5) + 16 * sets * keys * latent * cols,
        sets * heads * keys * rows,
    )


def feed_shards(spec, layer, info, refs, weights, sems, use):
    here, there, pieces = refs[0:3], refs[3:6], refs[6:12]
    hidden = here[0].shape[0]

    def run(act, far):
        if not far:
            for wanted, sources in ((True, here), (False, there)):

                @pl.when((info[CORE] == layer) == wanted)
                def _(sources=sources):
                    for kind, source in enumerate(sources):
                        act(pltpu.make_async_copy(source, weights.at[0, kind, pl.ds(0, hidden)], sems.at[kind]))

            return
        at = 3
        for kind, (begin, rows) in enumerate(spec):
            members = pieces[2 * kind].shape[0]
            for key in range(members):
                for source, core in ((pieces[2 * kind], info[CORE]), (pieces[2 * kind + 1], 1 - info[CORE])):
                    target = pl.multiple_of((core * members + key) * rows, 16)
                    act(
                        pltpu.make_async_copy(
                            source.at[key, pl.ds(begin, rows)], weights.at[1, kind, pl.ds(target, rows)], sems.at[at]
                        )
                    )
                    at += 1

    run(lambda copy: copy.start(), False)
    run(lambda copy: copy.start(), True)
    run(lambda copy: copy.wait(), False)
    use(0, [weights[0, kind, 0:hidden] for kind in range(3)])
    run(lambda copy: copy.wait(), True)
    use(1, [weights[1, kind, 0:hidden] for kind in range(3)])


def feed_kernel(spec, layer, info, value, *refs):
    total_out, saved, weights, sems, total = refs[12:]

    def use(shard, held):
        gate = dot_nt(value[...], held[0])
        up = dot_nt(value[...], held[1])
        saved[shard, 0] = gate.astype(bf16)
        saved[shard, 1] = up.astype(bf16)
        hidden = (gate * jax.nn.sigmoid(gate) * up).astype(bf16)
        part = dot_nn(hidden, held[2])
        if shard == 0:
            total[...] = part
        else:
            total_out[...] = (total[...] + part).astype(total_out.dtype)

    feed_shards(spec, layer, info, refs[0:12], weights, sems, use)


def feed_back_kernel(spec, layer, info, value, saved, *refs):
    total_out, keep, send, weights, sems, total = refs[12:]

    width = saved.shape[3]

    def use(shard, held):
        grad_hidden = dot_nt(value[...], held[2])
        gate = saved[shard, 0].astype(f32)
        up = saved[shard, 1].astype(f32)
        sigma = jax.nn.sigmoid(gate)
        silu = gate * sigma
        grad_gate = (grad_hidden * up * sigma * (1.0 + gate * (1.0 - sigma))).astype(bf16)
        grad_up = (grad_hidden * silu).astype(bf16)
        hidden = (silu * up).astype(bf16)
        mine = info[CORE] == layer if shard == 0 else info[CORE] != layer
        for out, wanted in ((keep, mine), (send, jnp.logical_not(mine))):

            @pl.when(wanted)
            def _(out=out):
                out[0, :, 0:width] = grad_gate
                out[1, :, 0:width] = grad_up
                out[2, :, 0:width] = hidden

        part = dot_nn(grad_gate, held[0]) + dot_nn(grad_up, held[1])
        if shard == 0:
            total[...] = part
        else:
            total_out[...] = (total[...] + part).astype(total_out.dtype)

    feed_shards(spec, layer, info, refs[0:12], weights, sems, use)


def feed_weights_kernel(hidden, info, *refs):
    lefts, rights, out, turned = refs[0:8], refs[8:12], refs[12], refs[13]
    kind = pl.program_id(0)
    rows = lefts[0].shape[0]
    members, _, size, lanes = out.shape

    @pl.when(kind == 0)
    def _():
        for at in range(2):
            for block in range(4):
                turned[at, :, block * rows : (block + 1) * rows] = lefts[4 * at + block][...].T

    right = jnp.concatenate([r[0] for r in rights], axis=0)
    left = turned[kind // 2]
    for first in range(0, hidden, 256):
        end = min(first + 256, hidden)
        result = dot_nn(left, right[:, first:end]).astype(bf16)
        for member in range(members):
            out[member, 0, :, first:end] = result[member * size : (member + 1) * size]
    out[:, :, :, hidden:] = jnp.zeros((members, 1, size, lanes - hidden), bf16)


def whole_lanes(count):
    return -(-count // 128) * 128


def feed_in(feed_w):
    here, there, pieces = feed_w
    arrays = (*here, *there, *sum((part[0:2] for part in pieces), ()))
    spec = tuple(part[2:4] for part in pieces)
    members, _, width = pieces[0][0].shape
    scratch = [
        pltpu.VMEM((2, 3, 2 * members * pieces[0][3], width), bf16),
        pltpu.SemaphoreType.DMA((3 + 6 * members,)),
    ]
    return arrays, spec, [pl.BlockSpec(memory_space=pl.ANY)] * len(arrays), scratch


def feed_call(info, layer, value, feed_w, dtype):
    rows, width = value.shape
    arrays, spec, specs, scratch = feed_in(feed_w)
    hidden = arrays[0].shape[0]
    outs = [like((rows, width), dtype), like((2, 2, rows, hidden), bf16)]
    return kernel_call(
        functools.partial(feed_kernel, spec, layer),
        info,
        (value,) + arrays,
        (1,),
        [whole(value)] + specs,
        [whole(o) for o in outs],
        outs,
        scratch + [pltpu.VMEM((rows, width), f32)],
        "feed",
        2 * 2 * 3 * rows * width * hidden,
    )


def feed_back_call(info, layer, value, saved, feed_w, dtype):
    rows, width = value.shape
    arrays, spec, specs, scratch = feed_in(feed_w)
    hidden = arrays[0].shape[0]
    outs = [like((rows, width), dtype)] + [like((3, rows, whole_lanes(hidden)), bf16)] * 2
    return kernel_call(
        functools.partial(feed_back_kernel, spec, layer),
        info,
        (value, saved) + arrays,
        (1,),
        [whole(value), whole(saved)] + specs,
        [whole(o) for o in outs],
        outs,
        scratch + [pltpu.VMEM((rows, width), f32)],
        "feed_back",
        2 * 2 * 3 * rows * width * hidden,
    )


def feed_weights_call(info, lefts, rights, members, hidden):
    rows, width = lefts[0].shape
    kinds, _, lanes = rights[0].shape
    shape = (members, kinds, width // members, lanes)
    outs = [like(shape, bf16)]
    return kernel_call(
        functools.partial(feed_weights_kernel, hidden),
        info,
        (*lefts, *rights),
        (kinds,),
        [whole(v) for v in lefts] + [lead(r) for r in rights],
        [pl.BlockSpec((members, 1) + shape[2:], lambda i, info: (0, i, 0, 0))],
        outs,
        [pltpu.VMEM((2, width, 4 * rows), bf16)],
        "feed_weights",
        2 * kinds * 4 * rows * width * hidden,
    )[0]


def shards(inputs, cotangent, lengths, w_query, w_latent, w_key, w_value, w_out, gains, w_gate, w_up, w_down):
    core = lax.axis_index("section")
    z = lax.axis_index("tensor")
    d = lax.axis_index("dp")
    planes = lax.axis_size("tensor")
    dp = lax.axis_size("dp")
    seqs = lengths.shape[0]
    bucket = inputs.shape[0] // seqs
    width = inputs.shape[1]
    layers = 2
    per_seq = planes // seqs * 2
    rows = bucket // per_seq
    rank = (z % (planes // seqs)) * 2 + core
    seq = z // (planes // seqs)
    first = rank * rows
    length = lax.dynamic_index_in_dim(lengths, seq, 0, False)
    info = jnp.stack([length, first, core, d, rank, z]).astype(jnp.int32)
    live = (lax.broadcasted_iota(jnp.int32, (rows, 1), 0) + first < length).astype(f32)
    row_at = seq * bucket + first
    own_in = lax.dynamic_slice_in_dim(inputs, row_at, rows, 0)
    own_target = lax.dynamic_slice_in_dim(cotangent, row_at, rows, 0)
    latent = w_latent.shape[2] // 2
    far_group = z // (planes // 2)

    cols = w_query.shape[2]
    hidden_cols = w_gate.shape[2]
    heads_here = jnp.concatenate([w_query[0], w_key[0], w_value[0]], axis=0)
    heads_there = core_swap(heads_here)
    lat_here = w_latent[0]
    lat_there = core_swap(lat_here)
    gain_here = gains[0]
    gain_there = core_swap(gain_here)
    out_here = w_out[0]
    feed_here = [w_gate[0].T, w_up[0].T, w_down[0]]
    head_rows, out_rows, feed_rows = heads_here.shape[0], out_here.shape[0], hidden_cols

    def piece_rows(count):
        return -(-count // (2 * dp * 16)) * 16

    def piece_of(value, side):
        rows_each = piece_rows(value.shape[0])
        value = jnp.pad(value, ((0, rows_each * 2 * dp - value.shape[0]), (0, 0)))
        return lax.dynamic_slice_in_dim(value, (side * dp + d) * rows_each, rows_each, 0)

    def feed_and_out(side):
        return jnp.concatenate([piece_of(v, side) for v in [out_here] + feed_here], axis=0)

    def layers_of(mine, received):
        return [jnp.where(core == layer, mine, received) for layer in range(layers)]

    main_pieces = layers_of(feed_and_out(core), core_swap(feed_and_out(1 - core)))
    head_pieces = layers_of(piece_of(heads_here, core), core_swap(piece_of(heads_here, 1 - core)))
    head_piece, out_piece, feed_piece = piece_rows(head_rows), piece_rows(out_rows), piece_rows(feed_rows)
    out_pieces = jnp.concatenate([piece[:out_piece] for piece in main_pieces], axis=0)
    feed_far = z_swap(jnp.concatenate([out_pieces, main_pieces[0][out_piece:]], axis=0), planes // 2)
    out_far = [z_swap(out_pieces, 1), feed_far[: 2 * out_piece], z_swap(out_pieces, 3)]
    out_far = [[v[layer * out_piece : (layer + 1) * out_piece] for v in out_far] for layer in range(layers)]
    feed_far = feed_far[2 * out_piece :]
    out_there = core_swap(tie(out_here, feed_far))
    feed_there = [core_swap(tie(v, feed_far)) for v in feed_here]
    latents_w = [jnp.where(core == layer, lat_here, lat_there) for layer in range(layers)]
    gains_all = [jnp.where(core == layer, gain_here, gain_there) for layer in range(layers)]

    def over_planes(piece):
        return [z_swap(piece, step) for step in range(1, planes)]

    def gather_near(parts, *before):
        return plane_gather(jnp.concatenate([tie(v, *before) for v in parts], axis=0))

    def gather(parts, before=(), after=()):
        near = gather_near(parts, *before)
        return near, core_swap(tie(near, *after))

    def gather_slow(parts, before=()):
        return lax.all_gather(jnp.concatenate([tie(v, *before) for v in parts], axis=0), "dp", axis=0, tiled=False)

    def by_group(value):
        return by_plane(value, far_group)

    def normalise(x, gain):
        x = x.astype(f32)
        return (x * inverse_rms(x) * gain).astype(bf16)

    def first_attention(*after):
        scalars = jnp.stack([lax.dynamic_index_in_dim(lengths, core, 0, False), z, core, far_group]).astype(jnp.int32)
        out = attend_first_call(
            scalars, inputs, lat_here, lat_there, tie(heads_here, *after), heads_there, gain_here, gain_there, bucket, per_seq
        )
        messages = []
        for way in range(per_seq):
            pairs = []
            for side in range(2):
                for plane in range(planes):
                    to = plane ^ way
                    target = (to % 2) * planes + side * (planes // seqs) + to // 2
                    pairs.append((side * planes + plane, target))
            messages.append(lax.ppermute(out[way], ("section", "tensor"), pairs))
        return out, messages

    def first_latents(*after):
        all_rows = tie(lax.dynamic_slice_in_dim(inputs, seq * bucket, bucket, 0), *after)
        lat = dot_nn(normalise(all_rows, gains_all[0][0]), latents_w[0]).astype(bf16)
        return by_group(jnp.stack([lat[:, :latent], lat[:, latent:]]))

    def attention(layer, x, pack):
        gain = gains_all[layer]
        normed = normalise(x, gain[0])
        own_lat = dot_nn(normed, latents_w[layer]).astype(bf16)
        own_lat = jnp.where(
            far_group == 1, jnp.concatenate([own_lat[:, latent:], own_lat[:, :latent]], axis=1), own_lat
        )
        far_lat = z_swap(own_lat, 1)
        lats = (own_lat, core_swap(own_lat), far_lat, core_swap(far_lat))
        mixed, lse, lat, residual, normed2 = attend_call(info, layer, x, normed, lats, pack, gain[1][None])
        return normed, lat, mixed, lse, residual, normed2

    def feed_own(layer, normed2, feed_w):
        far_normed2 = z_swap(normed2, 1)
        part, saved = feed_call(info, layer, normed2, feed_w, f32)
        return part, saved, tie(far_normed2, part)

    def feed_rest(layer, residual, part, far_normed2, feed_w):
        far_part, far_saved = feed_call(info, layer, far_normed2, feed_w, bf16)
        feed = part + z_swap(far_part, 1).astype(f32)
        return (live * (residual + feed)).astype(bf16), far_saved

    def finish_core(firsts, seconds):
        mine = jnp.where(core == 0, firsts, seconds)
        other = core_swap(jnp.where(core == 0, seconds, firsts))
        return jnp.where(core == 0, jnp.stack([mine, other]), jnp.stack([other, mine]))

    def backward(layer, grad_out, x, normed, lat, mixed, lse, residual, feed_kept, pack, feed_w, hooks):
        normed2, far_normed2, saved, far_saved = feed_kept
        gain = gains_all[layer]
        grad_res = live * grad_out.astype(f32)
        grad_feed = grad_res.astype(bf16)
        far_feed = z_swap(grad_feed, 1)
        part, *rights = feed_back_call(info, layer, grad_feed, saved, feed_w, f32)
        far_part, *far_rights = feed_back_call(info, layer, far_feed, far_saved, feed_w, bf16)
        back = z_swap(far_part, 1)
        lefts = [normed2, far_normed2, core_swap(normed2), core_swap(far_normed2)]
        lefts += [grad_feed, far_feed, core_swap(grad_feed), core_swap(far_feed)]
        rights = [rights[0], far_rights[0], core_swap(rights[1]), core_swap(far_rights[1])]
        lefts[0] = tie(lefts[0], *hooks[3]())
        feed_grads = feed_weights_call(info, lefts, rights, dp, hidden_cols)
        back = tie(back, feed_grads, *hooks[0]())
        grad_norm2 = part + back.astype(f32)
        grad_residual, gain_second = norm_back(residual, gain[1], grad_norm2)
        grad_residual = grad_residual + grad_res
        grad_branch = grad_residual.astype(bf16)

        feed_parts = lax.all_to_all(feed_grads, "dp", 0, 0)
        grad_norms = []
        lat_parts = []
        pack_parts_here = []
        for first_set in (2, 0):
            if first_set == 0:
                grad_branch = tie(grad_branch, grad_norms[0], *hooks[1](grad_branch))
            grad_norm, grad_lat, pack_keep, pack_send = attend_back_call(
                first_set, info, layer, grad_branch, normed, lat, pack, mixed, lse, dp
            )
            grad_norms.append(grad_norm)
            pack_parts_here.append((pack_keep, core_swap(pack_send)))
            grad_lat = grad_lat.reshape(per_seq // 2, 2, rows, latent)
            total = lax.dynamic_index_in_dim(grad_lat, core, 1, False) + core_swap(
                lax.dynamic_index_in_dim(grad_lat, 1 - core, 1, False)
            )
            near = rank // 2
            total = lax.dynamic_index_in_dim(total, near, 0, False) + z_swap(
                lax.dynamic_index_in_dim(total, 1 - near, 0, False), 1
            )
            lat_parts.append(total)
        lat_parts[1] = tie(lat_parts[1], feed_parts, *hooks[2]())
        lat_own = by_group(jnp.stack(lat_parts[::-1]))
        lat_own = jnp.concatenate([lat_own[0], lat_own[1]], axis=1)
        grad_norm = grad_norms[0] + grad_norms[1] + dot_nt(lat_own, latents_w[layer])
        grad_x, gain_first = norm_back(x.astype(f32), gain[0], grad_norm)
        grad_x = (grad_x + grad_residual).astype(bf16)

        lat_w = dot_tn(normed, lat_own).astype(bf16).reshape(planes, dp, width // planes // dp * 2, latent)
        gain_g = jnp.stack([gain_first, gain_second]).astype(bf16)
        gain_g = gain_g.reshape(2, planes, dp, -1).transpose(1, 2, 0, 3).reshape(planes, dp, 1, -1)
        gain_g = jnp.pad(gain_g, ((0, 0), (0, 0), (0, 31), (0, latent - gain_g.shape[3])))
        small = jnp.swapaxes(by_plane(jnp.concatenate([lat_w, gain_g], axis=2), z), 0, 1)
        half = small.shape[2] // 2
        small_keep = lax.dynamic_slice_in_dim(small, core * half, half, 2)
        small_send = lax.dynamic_slice_in_dim(small, (1 - core) * half, half, 2)
        small_parts = (small_keep, core_swap(small_send))

        feed_sums = jnp.sum(tie(feed_parts, grad_x).astype(f32), axis=0).astype(bf16)
        if layer == 0:
            pack_parts_here = [(a, tie(b, grad_x)) for a, b in pack_parts_here]
        pack_total = jnp.concatenate([a + b for a, b in pack_parts_here[::-1]], axis=1)
        small_total = small_parts[0] + small_parts[1]
        pack_parts = lax.all_to_all(jnp.concatenate([pack_total, small_total], axis=2), "dp", 0, 0)

        def finish_feed():
            pairs = [((1 - layer) * planes + i, layer * planes + (i ^ (planes // 2))) for i in range(planes)]
            return feed_sums.astype(f32) + lax.ppermute(feed_sums, ("section", "tensor"), pairs).astype(f32)

        def finish_pack(*after):
            parts = tie(pack_parts, *after)
            sums = jnp.sum(parts.astype(f32), axis=0).astype(bf16)
            sums = sums[0::2] + z_swap(sums[1::2], 1)
            return sums[0] + z_swap(sums[1], 2)

        return grad_x, pack_parts, finish_feed, finish_pack

    lat0 = first_latents()
    first_out, messages = first_attention(feed_far, lat0)
    main0 = gather(out_far[0] + [feed_far], (), messages)
    outs0 = (out_here, out_there) + main0 + (0, out_piece)
    at = (planes - 1) * out_piece
    feed0 = (feed_here, feed_there, [main0 + (at + k * feed_piece, feed_piece) for k in range(3)])
    mixed0, lse0, residual0, normed2_0 = attend_out_call(info, 0, own_in, messages, outs0, gains_all[0][1][None])
    near_heads1 = gather_slow(over_planes(head_pieces[1]), (first_out,))
    part0, saved0, far_normed2 = feed_own(0, normed2_0, feed0)
    far_normed2 = tie(far_normed2, near_heads1)
    feed_far1 = z_swap(tie(main_pieces[1][out_piece:], *messages), planes // 2)
    near1 = gather_near(out_far[1] + [feed_far1], part0)
    out0, far_saved0 = feed_rest(0, residual0, part0, far_normed2, feed0)
    kept0 = [normed2_0, far_normed2, saved0, far_saved0]
    main1 = near1, core_swap(tie(near1, out0))
    heads1 = (heads_here, heads_there, near_heads1, core_swap(near_heads1), 0, head_piece)
    outs1 = (out_here, out_there) + main1 + (0, out_piece)
    feed1 = (feed_here, feed_there, [main1 + (at + k * feed_piece, feed_piece) for k in range(3)])

    normed1, lat1, mixed1, lse1, residual1, normed2_1 = attention(1, out0, (heads1, outs1))
    part1, saved1, far_normed2 = feed_own(1, normed2_1, feed1)
    out1, far_saved1 = feed_rest(1, residual1, part1, far_normed2, feed1)
    kept1 = [normed2_1, far_normed2, saved1, far_saved1]
    def gather_rows(own):
        return lax.all_gather(own, "tensor", axis=0, tiled=False)

    def finish_rows(firsts, seconds):
        mine = jnp.where(core == 0, firsts, seconds)
        other = core_swap(jnp.where(core == 0, seconds, firsts))
        both = jnp.where(core == 0, jnp.stack([mine, other], axis=1), jnp.stack([other, mine], axis=1))
        return both.reshape(planes * 2 * rows, width)

    rows_out = [gather_rows(out0), gather_rows(out1)]
    near_heads0 = gather_slow(over_planes(head_pieces[0]), (out0,))
    heads0 = (heads_here, heads_there, near_heads0, core_swap(tie(near_heads0, out1)), 0, head_piece)
    grad1, pack_parts1, finish_feed1, finish_pack1 = backward(
        1, own_target, out0, normed1, lat1, mixed1, lse1, residual1, kept1, (heads1, outs1), feed1,
        [lambda: (rows_out[0],), lambda token: (), lambda: (rows_out[1],), lambda: ()],
    )
    normed0 = normalise(own_in, gains_all[0][0])
    later = {}

    def during_attention(token):
        later["feed"] = finish_feed1()
        return (later["feed"],)

    def after_attention():
        later["pack"] = finish_pack1()
        later["grad"] = gather_rows(grad1)
        return (later["pack"], later["grad"])

    grad0, _, finish_feed0, finish_pack0 = backward(
        0, grad1, own_in, normed0, lat0, mixed0, lse0, residual0, kept0, (heads0, outs0), feed0,
        [lambda: (), during_attention, after_attention, lambda: (pack_parts1,)],
    )
    rows_grad0 = gather_rows(grad0)
    layer_outputs = finish_rows(*rows_out)
    input_grads = finish_rows(rows_grad0, later["grad"])

    feed_final0 = finish_feed0()
    feed_total = jnp.where(core == 0, feed_final0, later["feed"])
    gate_t, up_t, down_t = feed_total[:, :, :hidden_cols]
    halves = finish_core(finish_pack0(feed_final0), later["pack"]).astype(f32)
    main = (head_rows + width) // dp // 2
    query_t, key_t = halves[0, : width // dp], halves[0, width // dp : main]
    value_t, out_t = halves[1, : latent // dp], halves[1, latent // dp : main]
    small = halves[:, main:].reshape(-1, latent)
    lat_rows = width // planes // dp * 2
    lat_t = small[:lat_rows].reshape(lat_rows // 2, 2 * latent)
    gain_t = small[lat_rows, : 2 * width // planes // dp].reshape(2, -1)
    return (
        layer_outputs[None],
        input_grads[None],
        query_t[None],
        lat_t[None],
        key_t[None],
        value_t[None],
        out_t.T[None],
        gain_t[None],
        gate_t[None],
        up_t[None],
        down_t.T[None],
    )


def solution(mesh):
    placed = (
        P("dp", None),
        P("dp", None),
        P("dp"),
        P("section", None, "tensor"),
        P("section", None, None),
        P("section", None, "tensor"),
        P("section", None, "tensor"),
        P("section", "tensor", None),
        P("section", None, None),
        P("section", None, "tensor"),
        P("section", None, "tensor"),
        P("section", "tensor", None),
    )
    return jax.shard_map(
        shards,
        mesh=mesh,
        in_specs=placed,
        out_specs=(
            P("section", "dp", None),
            P("section", "dp", None),
            P("section", "dp", "tensor"),
            P("section", ("tensor", "dp"), None),
            P("section", "dp", "tensor"),
            P("section", "dp", "tensor"),
            P("section", "tensor", "dp"),
            P("section", None, ("tensor", "dp")),
            P("section", "dp", "tensor"),
            P("section", "dp", "tensor"),
            P("section", "tensor", "dp"),
        ),
        check_vma=False,
    )
```

```python
import functools

import jax
import jax.numpy as jnp
from jax import lax
from jax.experimental import pallas as pl
from jax.experimental.pallas import tpu as pltpu
from jax.sharding import PartitionSpec as P

HEAD_DIM = 64
eps = 1e-06
masked_score = -1e30
f32 = jnp.float32
bf16 = jnp.bfloat16


def dot_nn(left, right):
    return lax.dot_general(left, right, (((1,), (0,)), ((), ())), preferred_element_type=f32)


def dot_nt(left, right):
    return lax.dot_general(left, right, (((1,), (1,)), ((), ())), preferred_element_type=f32)


def dot_tn(left, right):
    return lax.dot_general(left, right, (((0,), (0,)), ((), ())), preferred_element_type=f32)


def core_swap(value):
    return lax.ppermute(value, "section", [(0, 1), (1, 0)])


def z_swap(value, step):
    count = lax.axis_size("tensor")
    return lax.ppermute(value, "tensor", [(i, i ^ step) for i in range(count)])


def tie(first, *others):
    return lax.optimization_barrier((first,) + others)[0]


def bits_of(count):
    return [1 << i for i in range(count.bit_length() - 1)]


def plane_gather(piece):
    count = lax.axis_size("dp")
    return lax.all_to_all(jnp.broadcast_to(piece[None], (count,) + piece.shape), "dp", 0, 0)


def plane_sum(parts):
    return jnp.sum(lax.all_to_all(parts, "dp", 0, 0).astype(f32), axis=0).astype(bf16)


def by_plane(values, flip_of):
    count = values.shape[0]
    for bit in bits_of(count):
        order = [k ^ bit for k in range(count)]
        flipped = jnp.stack([values[k] for k in order])
        values = jnp.where((flip_of // bit) % 2 == 1, flipped, values)
    return values


def inverse_rms(rows):
    return lax.rsqrt(jnp.mean(rows * rows, axis=-1, keepdims=True) + eps)


def norm_back(rows, gain, grad_norm):
    scale = inverse_rms(rows)
    weighted = grad_norm * gain
    inner = jnp.mean(weighted * rows, axis=-1, keepdims=True)
    grad_rows = scale * weighted - rows * scale * scale * scale * inner
    grad_gain = jnp.sum(grad_norm * rows * scale, axis=0)
    return (grad_rows, grad_gain)


LENGTH, FIRST, CORE, MEMBER, RANK, PLANE = range(6)


def kernel_call(kernel, info, arrays, grid, in_specs, out_specs, out_shape, scratch, name, flops, transcendentals=0):
    size = sum(a.size * a.dtype.itemsize for a in arrays)
    size += sum(o.size * o.dtype.itemsize for o in out_shape)
    return pl.pallas_call(
        kernel,
        grid_spec=pltpu.PrefetchScalarGridSpec(
            num_scalar_prefetch=1,
            grid=grid,
            in_specs=in_specs,
            out_specs=out_specs,
            scratch_shapes=scratch,
        ),
        out_shape=out_shape,
        compiler_params=pltpu.CompilerParams(
            dimension_semantics=("arbitrary",) * len(grid), vmem_limit_bytes=52 * 1024 * 1024
        ),
        cost_estimate=pl.CostEstimate(flops=flops, bytes_accessed=size, transcendentals=transcendentals),
        name=name,
    )(info, *arrays)


def whole(array):
    shape = array.shape
    return pl.BlockSpec(shape, lambda i, info: (0,) * len(shape))


def lead(array):
    shape = array.shape[1:]
    return pl.BlockSpec((1,) + shape, lambda i, info: (i,) + (0,) * len(shape))


def like(shape, dtype):
    return jax.ShapeDtypeStruct(shape, dtype)


class PackCopies:
    def __init__(self, info, layer, parts, held, sems):
        self.info, self.layer, self.parts, self.held, self.sems = info, layer, parts, held, sems

    def own(self, slot, there):
        for at, (part, target) in enumerate(zip(self.parts, self.held)):
            source = part[1] if there else part[0]
            rows = source.shape[0]
            yield pltpu.make_async_copy(source, target.at[slot, pl.ds(0, rows)], self.sems.at[slot, at])

    def pieces(self, slot, step):
        at = 0
        for (_, _, near, other, begin, rows), held in zip(self.parts, self.held):
            members = near.shape[0]
            source_at = pl.multiple_of(begin + (step - 1) * rows, 16)
            for key in range(members):
                for source, core in ((near, self.info[CORE]), (other, 1 - self.info[CORE])):
                    target = pl.multiple_of((core * members + key) * rows, 16)
                    yield pltpu.make_async_copy(
                        source.at[key, pl.ds(source_at, rows)],
                        held.at[slot, pl.ds(target, rows)],
                        self.sems.at[slot, at],
                    )
                    at += 1

    def each(self, step, act):
        slot = step % 2

        def run(copies):
            for copy in copies:
                act(copy)

        there = self.info[CORE] != self.layer
        pl.when((step == 0) & there)(lambda: run(self.own(slot, True)))
        pl.when((step == 0) & jnp.logical_not(there))(lambda: run(self.own(slot, False)))
        pl.when(step > 0)(lambda: run(self.pieces(slot, step)))

    def start(self, step):
        self.each(step, lambda copy: copy.start())

    def turn(self, step, first, last):
        @pl.when(step == first)
        def _():
            self.start(step)

        @pl.when(step < last)
        def _():
            self.start(step + 1)

        self.each(step, lambda copy: copy.wait())
        return [held.at[step % 2] for held in self.held]


def pack_refs(spec, refs):
    return [tuple(refs[4 * at : 4 * at + 4]) + part for at, part in enumerate(spec)]


def fill_bias(info, bias):
    keys, rows = bias.shape
    key_pos = lax.broadcasted_iota(jnp.int32, (keys, rows), 0)
    query_pos = lax.broadcasted_iota(jnp.int32, (keys, rows), 1) + info[FIRST]
    allowed = (key_pos <= query_pos) & (key_pos < info[LENGTH])
    bias[...] = jnp.where(allowed, 0.0, masked_score)


def head_parts(heads, width, latent):
    at = (0, width, width + latent, width + 2 * latent)
    return [heads[lo:hi] for lo, hi in zip(at[:-1], at[1:])]


def attend_sets(keys, values_t, query, bias, heads):
    lane_head = lax.broadcasted_iota(jnp.int32, query.shape, 1) // HEAD_DIM
    mixed, sums = [], []
    for head in range(heads):
        query_here = jnp.where(lane_head == head, query, bf16(0))
        scores = dot_nt(keys, query_here) + bias
        peak = jnp.max(scores, axis=0, keepdims=True)
        expo = jnp.exp(scores - peak)
        total = jnp.sum(expo, axis=0, keepdims=True)
        part = dot_nn(values_t[head * HEAD_DIM : (head + 1) * HEAD_DIM], expo.astype(bf16))
        mixed.append(part * (1.0 / total))
        sums.append(peak + jnp.log(total))
    return jnp.concatenate(mixed, axis=0), jnp.concatenate(sums, axis=0)


def attend_first_kernel(
    info, x, lat_here, lat_there, heads_here, heads_there, gain_here, gain_there, out, normed, query_all, keys_all, values_t_all
):
    keys_count, width = x.shape
    latent = lat_here.shape[1]
    cols = heads_here.shape[1]
    heads = cols // HEAD_DIM
    rows = keys_count // out.shape[0]
    here = info[2] == 0
    gain = jnp.where(here, gain_here[0:1], gain_there[0:1])
    pack = jnp.where(here, heads_here[...], heads_there[...])
    w_latent = jnp.where(here, lat_here[...], lat_there[...])
    for block in range(keys_count // rows):
        here = slice(block * rows, (block + 1) * rows)
        value = x[here].astype(f32)
        normed[here] = (value * inverse_rms(value) * gain).astype(bf16)
    w_query, w_key, w_value = head_parts(pack, width, latent)
    query_all[...] = dot_nn(normed[...], w_query).astype(bf16) * bf16(HEAD_DIM**-0.5)
    lat = dot_nn(normed[...], w_latent).astype(bf16)
    keys_all[...] = dot_nn(lat, w_key).astype(bf16)
    values_t_all[...] = dot_nn(lat, w_value).astype(bf16).T
    for block in range(keys_count // rows):
        first = block * rows
        end = first + rows
        key_pos = lax.broadcasted_iota(jnp.int32, (end, rows), 0)
        query_pos = lax.broadcasted_iota(jnp.int32, (end, rows), 1) + first
        bias = jnp.where((key_pos <= query_pos) & (key_pos < info[0]), 0.0, masked_score)
        mixed, sums = attend_sets(keys_all[0:end], values_t_all[:, 0:end], query_all[first:end], bias, heads)
        high = sums.astype(bf16)
        low = (sums - high.astype(f32)).astype(bf16)
        at = info[1] ^ block
        out[at, 0:rows, :] = mixed.T.astype(bf16)
        out[at, rows:, :] = jnp.concatenate([high, low, jnp.zeros((16 - 2 * heads, rows), bf16)], axis=0)


def attend_out_kernel(
    spec, layer, info, x, m0, m1, m2, m3, gain, o0, o1, o2, o3, mixed_out, lse_out, residual, normed2, sets, outs, sems
):
    step = pl.program_id(0)
    rows, width = x.shape
    heads = lse_out.shape[1]
    copies = PackCopies(info, layer, pack_refs(spec, (o0, o1, o2, o3)), [outs], sems)
    w_out = copies.turn(step, 0, pl.num_programs(0) - 1)[0]

    @pl.when(step == 0)
    def _():
        residual[...] = x[...].astype(f32)
        for key, piece in enumerate((m0, m1, m2, m3)):
            sets[key ^ info[RANK] ^ info[PLANE]] = piece[...]

    mixed = sets[step, 0:rows, :]
    tail = sets[step, rows:, :].astype(f32)
    mixed_out[0] = mixed
    lse_out[0] = tail[0:heads] + tail[heads : 2 * heads]
    residual[...] += dot_nn(mixed, w_out[0 : mixed.shape[1]])

    @pl.when(step == pl.num_programs(0) - 1)
    def _():
        full = residual[...]
        normed2[...] = (full * inverse_rms(full) * gain[...]).astype(bf16)


def attend_kernel(
    spec, layer, info, x, normed, lat0, lat1, lat2, lat3, gain, h0, h1, h2, h3, o0, o1, o2, o3,
    mixed_out, lse_out, lat_out, residual, normed2, bias, heads_held, outs_held, sems,
):
    step = pl.program_id(0)
    rows, width = normed.shape
    latent = lat_out.shape[2]
    heads = lse_out.shape[1]
    parts = pack_refs(spec, (h0, h1, h2, h3, o0, o1, o2, o3))
    copies = PackCopies(info, layer, parts, [heads_held, outs_held], sems)
    w_heads, w_out = copies.turn(step, 0, pl.num_programs(0) - 1)

    @pl.when(step == 0)
    def _():
        fill_bias(info, bias)
        residual[...] = x[...].astype(f32)
        for key, piece in enumerate((lat0, lat1, lat2, lat3)):
            at = pl.multiple_of((info[RANK] ^ key) * rows, 16)
            for group in range(2):
                lat_out[group, pl.ds(at, rows), :] = piece[:, group * latent : (group + 1) * latent]

    w_query, w_key, w_value = head_parts(w_heads, width, latent)
    lat = lat_out[step // 2]
    query = dot_nn(normed[...], w_query).astype(bf16) * bf16(HEAD_DIM**-0.5)
    keys = dot_nn(lat, w_key).astype(bf16)
    values_t = dot_nn(lat, w_value).astype(bf16).T
    mixed, sums = attend_sets(keys, values_t, query, bias[...], heads)
    lse_out[0] = sums
    mixed = mixed.T.astype(bf16)
    mixed_out[0] = mixed
    residual[...] += dot_nn(mixed, w_out[0 : mixed.shape[1]])

    @pl.when(step == pl.num_programs(0) - 1)
    def _():
        full = residual[...]
        normed2[...] = (full * inverse_rms(full) * gain[...]).astype(bf16)


def attend_back_kernel(
    first_set, spec, layer, info, grad_branch, normed, lat, mixed_in, lse_in, h0, h1, h2, h3, o0, o1, o2, o3,
    grad_norm, grad_lat, keep, send, bias, heads_held, outs_held, sems, lat_sum,
):
    step = pl.program_id(0)
    rows, width = normed.shape
    keys_count, latent = grad_lat.shape
    cols = heads_held.shape[2]
    scale = HEAD_DIM**-0.5
    members = keep.shape[0]
    parts = pack_refs(spec, (h0, h1, h2, h3, o0, o1, o2, o3))
    copies = PackCopies(info, layer, parts, [heads_held, outs_held], sems)
    w_heads, w_out = copies.turn(step + first_set, first_set, first_set + pl.num_programs(0) - 1)

    @pl.when(step == 0)
    def _():
        fill_bias(info, bias)
        grad_norm[...] = jnp.zeros_like(grad_norm)
        lat_sum[...] = jnp.zeros_like(lat_sum)

    w_query, w_key, w_value = head_parts(w_heads, width, latent)
    here = lat[0]
    query = dot_nn(normed[...], w_query).astype(bf16) * bf16(scale)
    keys = dot_nn(here, w_key).astype(bf16)
    keys_t = keys.T
    values = dot_nn(here, w_value).astype(bf16)
    mixed = mixed_in[0]
    grad_mixed = dot_nt(grad_branch[...], w_out[0:cols]).astype(bf16)
    centre = (grad_mixed.astype(f32) * mixed.astype(f32)).T
    lane_head = lax.broadcasted_iota(jnp.int32, (rows, cols), 1) // HEAD_DIM
    grad_keys = jnp.zeros((keys_count, cols), f32)
    grad_values = jnp.zeros((keys_count, cols), f32)
    grad_query_parts = []
    for head in range(cols // HEAD_DIM):
        mine = slice(head * HEAD_DIM, (head + 1) * HEAD_DIM)
        query_here = jnp.where(lane_head == head, query, bf16(0))
        grad_here = jnp.where(lane_head == head, grad_mixed, bf16(0))
        scores = dot_nt(keys, query_here) + bias[...]
        probs = jnp.exp(scores - lse_in[0, head : head + 1, :])
        grad_probs = dot_nt(values, grad_here)
        inner = jnp.sum(centre[mine], axis=0, keepdims=True)
        grad_scores = (probs * (grad_probs - inner)).astype(bf16)
        grad_values += dot_nn(probs.astype(bf16), grad_here)
        grad_keys += dot_nn(grad_scores, query_here)
        grad_query_parts.append(dot_nn(keys_t[mine], grad_scores) * scale)
    grad_keys = grad_keys.astype(bf16)
    grad_values = grad_values.astype(bf16)
    grad_query = jnp.concatenate(grad_query_parts, axis=0).T.astype(bf16)
    grad_norm[...] += dot_nt(grad_query, w_query)
    lat_sum[...] += dot_nt(grad_keys, w_key) + dot_nt(grad_values, w_value)
    halves = (
        (dot_tn(normed[...], grad_query), dot_tn(here, grad_keys)),
        (dot_tn(here, grad_values), dot_tn(grad_branch[...], mixed)),
    )
    for half, results in enumerate(halves):
        for out, wanted in ((keep, half), (send, 1 - half)):

            @pl.when(info[CORE] == wanted)
            def _(out=out, results=results):
                at = 0
                for result in results:
                    size = result.shape[0] // members
                    for member in range(members):
                        out[member, 0, at : at + size, :] = result[member * size : (member + 1) * size].astype(bf16)
                    at += size

    @pl.when(step == pl.num_programs(0) - 1)
    def _():
        grad_lat[...] = lat_sum[...].astype(bf16)


def attend_first_call(info, x, lat_here, lat_there, heads_here, heads_there, gain_here, gain_there, keys, blocks):
    width = x.shape[1]
    latent = lat_here.shape[1] // 2
    cols = heads_here.shape[1]
    outs = [like((blocks, keys // blocks + 16, cols), bf16)]
    arrays = (x, lat_here, lat_there, heads_here, heads_there, gain_here, gain_there)
    group = pl.BlockSpec((width, latent), lambda i, info: (0, info[3]))
    return kernel_call(
        attend_first_kernel,
        info,
        arrays,
        (1,),
        [pl.BlockSpec((keys, width), lambda i, info: (info[2], 0)), group, group] + [whole(v) for v in arrays[3:]],
        [whole(o) for o in outs],
        outs,
        [pltpu.VMEM((keys, width), bf16)] + [pltpu.VMEM((keys, cols), bf16)] * 2 + [pltpu.VMEM((cols, keys), bf16)],
        "attend_first",
        2 * keys * width * (cols + latent) + 4 * keys * latent * cols + 4 * keys * keys * cols * 3,
        keys * keys * 3,
    )[0]


def pack_in(*parts):
    arrays = sum((tuple(part[0:4]) for part in parts), ())
    spec = tuple(tuple(part[4:]) for part in parts)
    members = parts[0][2].shape[0]
    scratch = [pltpu.VMEM((2, 2 * members * part[5], part[0].shape[1]), bf16) for part in parts]
    scratch.append(pltpu.SemaphoreType.DMA((2, 2 * members * len(parts))))
    return arrays, spec, [pl.BlockSpec(memory_space=pl.ANY)] * len(arrays), scratch


def attend_out_call(info, layer, x, messages, outs_w, gain):
    rows, width = x.shape
    arrays, spec, specs, scratch = pack_in(outs_w)
    sets = 4
    cols = messages[0].shape[1]
    heads = cols // HEAD_DIM
    outs = [
        like((sets, rows, cols), bf16),
        like((sets, heads, rows), f32),
        like((rows, width), f32),
        like((rows, width), bf16),
    ]
    return kernel_call(
        functools.partial(attend_out_kernel, spec, layer),
        info,
        (x, *messages, gain) + arrays,
        (sets,),
        [whole(x)] + [whole(m) for m in messages] + [whole(gain)] + specs,
        [lead(outs[0]), lead(outs[1]), whole(outs[2]), whole(outs[3])],
        outs,
        [pltpu.VMEM((sets,) + messages[0].shape, bf16)] + scratch,
        "attend_out",
        2 * sets * rows * width * cols,
    )


def attend_call(info, layer, x, normed, lats, pack, gain):
    rows, width = normed.shape
    arrays, spec, specs, scratch = pack_in(*pack)
    sets = 4
    cols = arrays[0].shape[1]
    latent = lats[0].shape[1] // 2
    keys = rows * len(lats)
    heads = cols // HEAD_DIM
    outs = [
        like((sets, rows, cols), bf16),
        like((sets, heads, rows), f32),
        like((2, keys, latent), bf16),
        like((rows, width), f32),
        like((rows, width), bf16),
    ]
    return kernel_call(
        functools.partial(attend_kernel, spec, layer),
        info,
        (x, normed, *lats, gain) + arrays,
        (sets,),
        [whole(x), whole(normed)] + [whole(v) for v in lats] + [whole(gain)] + specs,
        [lead(outs[0]), lead(outs[1])] + [whole(o) for o in outs[2:]],
        outs,
        [pltpu.VMEM((keys, rows), f32)] + scratch,
        "attend",
        2 * sets * rows * (2 * keys * cols * heads + width * cols * 2) + 4 * sets * keys * latent * cols,
        sets * heads * keys * rows,
    )


def attend_back_call(first_set, info, layer, grad_branch, normed, lat, pack, mixed, lse, members):
    rows, width = normed.shape
    arrays, spec, specs, scratch = pack_in(*pack)
    cols = arrays[0].shape[1]
    piece_rows = (arrays[0].shape[0] + width) // members // 2
    sets = 2
    keys, latent = lat.shape[1:]
    heads = cols // HEAD_DIM
    group = pl.BlockSpec((1, keys, latent), lambda i, info: (first_set // 2, 0, 0))
    outs = [
        like((rows, width), f32),
        like((keys, latent), bf16),
        like((members, sets, piece_rows, cols), bf16),
        like((members, sets, piece_rows, cols), bf16),
    ]
    summed = pl.BlockSpec((members, 1, piece_rows, cols), lambda i, info: (0, i, 0, 0))
    mine = [pl.BlockSpec((1,) + v.shape[1:], lambda i, info: (i + first_set, 0, 0)) for v in (mixed, lse)]
    return kernel_call(
        functools.partial(attend_back_kernel, first_set, spec, layer),
        info,
        (grad_branch, normed, lat, mixed, lse) + arrays,
        (sets,),
        [whole(grad_branch), whole(normed), group] + mine + specs,
        [whole(outs[0]), whole(outs[1]), summed, summed],
        outs,
        [pltpu.VMEM((keys, rows), f32)] + scratch + [pltpu.VMEM((keys, latent), f32)],
        "attend_back",
        2 * sets * rows * (5 * keys * cols * heads + width * cols * 5) + 16 * sets * keys * latent * cols,
        sets * heads * keys * rows,
    )


def feed_shards(spec, layer, info, refs, weights, sems, use):
    here, there, pieces = refs[0:3], refs[3:6], refs[6:12]
    hidden = here[0].shape[0]

    def run(act, far):
        if not far:
            for wanted, sources in ((True, here), (False, there)):

                @pl.when((info[CORE] == layer) == wanted)
                def _(sources=sources):
                    for kind, source in enumerate(sources):
                        act(pltpu.make_async_copy(source, weights.at[0, kind, pl.ds(0, hidden)], sems.at[kind]))

            return
        at = 3
        for kind, (begin, rows) in enumerate(spec):
            members = pieces[2 * kind].shape[0]
            for key in range(members):
                for source, core in ((pieces[2 * kind], info[CORE]), (pieces[2 * kind + 1], 1 - info[CORE])):
                    target = pl.multiple_of((core * members + key) * rows, 16)
                    act(
                        pltpu.make_async_copy(
                            source.at[key, pl.ds(begin, rows)], weights.at[1, kind, pl.ds(target, rows)], sems.at[at]
                        )
                    )
                    at += 1

    run(lambda copy: copy.start(), False)
    run(lambda copy: copy.start(), True)
    run(lambda copy: copy.wait(), False)
    use(0, [weights[0, kind, 0:hidden] for kind in range(3)])
    run(lambda copy: copy.wait(), True)
    use(1, [weights[1, kind, 0:hidden] for kind in range(3)])


def feed_kernel(spec, layer, info, value, *refs):
    total_out, saved, weights, sems, total = refs[12:]

    def use(shard, held):
        gate = dot_nt(value[...], held[0])
        up = dot_nt(value[...], held[1])
        saved[shard, 0] = gate.astype(bf16)
        saved[shard, 1] = up.astype(bf16)
        hidden = (gate * jax.nn.sigmoid(gate) * up).astype(bf16)
        part = dot_nn(hidden, held[2])
        if shard == 0:
            total[...] = part
        else:
            total_out[...] = (total[...] + part).astype(total_out.dtype)

    feed_shards(spec, layer, info, refs[0:12], weights, sems, use)


def feed_back_kernel(spec, layer, info, value, saved, *refs):
    total_out, keep, send, weights, sems, total = refs[12:]

    width = saved.shape[3]

    def use(shard, held):
        grad_hidden = dot_nt(value[...], held[2])
        gate = saved[shard, 0].astype(f32)
        up = saved[shard, 1].astype(f32)
        sigma = jax.nn.sigmoid(gate)
        silu = gate * sigma
        grad_gate = (grad_hidden * up * sigma * (1.0 + gate * (1.0 - sigma))).astype(bf16)
        grad_up = (grad_hidden * silu).astype(bf16)
        hidden = (silu * up).astype(bf16)
        mine = info[CORE] == layer if shard == 0 else info[CORE] != layer
        for out, wanted in ((keep, mine), (send, jnp.logical_not(mine))):

            @pl.when(wanted)
            def _(out=out):
                out[0, :, 0:width] = grad_gate
                out[1, :, 0:width] = grad_up
                out[2, :, 0:width] = hidden

        part = dot_nn(grad_gate, held[0]) + dot_nn(grad_up, held[1])
        if shard == 0:
            total[...] = part
        else:
            total_out[...] = (total[...] + part).astype(total_out.dtype)

    feed_shards(spec, layer, info, refs[0:12], weights, sems, use)


def feed_weights_kernel(hidden, info, *refs):
    lefts, rights, out, turned = refs[0:8], refs[8:12], refs[12], refs[13]
    kind = pl.program_id(0)
    rows = lefts[0].shape[0]
    members, _, size, lanes = out.shape

    @pl.when(kind == 0)
    def _():
        for at in range(2):
            for block in range(4):
                turned[at, :, block * rows : (block + 1) * rows] = lefts[4 * at + block][...].T

    right = jnp.concatenate([r[0] for r in rights], axis=0)
    left = turned[kind // 2]
    for first in range(0, hidden, 256):
        end = min(first + 256, hidden)
        result = dot_nn(left, right[:, first:end]).astype(bf16)
        for member in range(members):
            out[member, 0, :, first:end] = result[member * size : (member + 1) * size]
    out[:, :, :, hidden:] = jnp.zeros((members, 1, size, lanes - hidden), bf16)


def whole_lanes(count):
    return -(-count // 128) * 128


def feed_in(feed_w):
    here, there, pieces = feed_w
    arrays = (*here, *there, *sum((part[0:2] for part in pieces), ()))
    spec = tuple(part[2:4] for part in pieces)
    members, _, width = pieces[0][0].shape
    scratch = [
        pltpu.VMEM((2, 3, 2 * members * pieces[0][3], width), bf16),
        pltpu.SemaphoreType.DMA((3 + 6 * members,)),
    ]
    return arrays, spec, [pl.BlockSpec(memory_space=pl.ANY)] * len(arrays), scratch


def feed_call(info, layer, value, feed_w, dtype):
    rows, width = value.shape
    arrays, spec, specs, scratch = feed_in(feed_w)
    hidden = arrays[0].shape[0]
    outs = [like((rows, width), dtype), like((2, 2, rows, hidden), bf16)]
    return kernel_call(
        functools.partial(feed_kernel, spec, layer),
        info,
        (value,) + arrays,
        (1,),
        [whole(value)] + specs,
        [whole(o) for o in outs],
        outs,
        scratch + [pltpu.VMEM((rows, width), f32)],
        "feed",
        2 * 2 * 3 * rows * width * hidden,
    )


def feed_back_call(info, layer, value, saved, feed_w, dtype):
    rows, width = value.shape
    arrays, spec, specs, scratch = feed_in(feed_w)
    hidden = arrays[0].shape[0]
    outs = [like((rows, width), dtype)] + [like((3, rows, whole_lanes(hidden)), bf16)] * 2
    return kernel_call(
        functools.partial(feed_back_kernel, spec, layer),
        info,
        (value, saved) + arrays,
        (1,),
        [whole(value), whole(saved)] + specs,
        [whole(o) for o in outs],
        outs,
        scratch + [pltpu.VMEM((rows, width), f32)],
        "feed_back",
        2 * 2 * 3 * rows * width * hidden,
    )


def feed_weights_call(info, lefts, rights, members, hidden):
    rows, width = lefts[0].shape
    kinds, _, lanes = rights[0].shape
    shape = (members, kinds, width // members, lanes)
    outs = [like(shape, bf16)]
    return kernel_call(
        functools.partial(feed_weights_kernel, hidden),
        info,
        (*lefts, *rights),
        (kinds,),
        [whole(v) for v in lefts] + [lead(r) for r in rights],
        [pl.BlockSpec((members, 1) + shape[2:], lambda i, info: (0, i, 0, 0))],
        outs,
        [pltpu.VMEM((2, width, 4 * rows), bf16)],
        "feed_weights",
        2 * kinds * 4 * rows * width * hidden,
    )[0]


def rows_kernel(info, first, first_other, second, second_other, out, held, sems):
    planes, rows, _ = first.shape
    for core, sources in ((0, (first, first_other)), (1, (second_other, second))):

        @pl.when(info[CORE] == core)
        def _(sources=sources):
            copies = [pltpu.make_async_copy(v, held.at[:, at], sems.at[0, at]) for at, v in enumerate(sources)]
            for copy in copies:
                copy.start()
            for copy in copies:
                copy.wait()

    whole_copy = pltpu.make_async_copy(held, out, sems.at[1, 0])
    whole_copy.start()
    whole_copy.wait()


def rows_call(info, *arrays):
    planes, rows, width = arrays[0].shape
    shape = (planes, 2, rows, width)
    out = kernel_call(
        rows_kernel,
        info,
        arrays,
        (1,),
        [pl.BlockSpec(memory_space=pl.ANY)] * 4,
        [pl.BlockSpec(memory_space=pl.ANY)],
        [like(shape, bf16)],
        [pltpu.VMEM(shape, bf16), pltpu.SemaphoreType.DMA((2, 2))],
        "rows",
        0,
    )[0]
    return out.reshape(planes * 2 * rows, width)


def shards(inputs, cotangent, lengths, w_query, w_latent, w_key, w_value, w_out, gains, w_gate, w_up, w_down):
    core = lax.axis_index("section")
    z = lax.axis_index("tensor")
    d = lax.axis_index("dp")
    planes = lax.axis_size("tensor")
    dp = lax.axis_size("dp")
    seqs = lengths.shape[0]
    bucket = inputs.shape[0] // seqs
    width = inputs.shape[1]
    layers = 2
    per_seq = planes // seqs * 2
    rows = bucket // per_seq
    rank = (z % (planes // seqs)) * 2 + core
    seq = z // (planes // seqs)
    first = rank * rows
    length = lax.dynamic_index_in_dim(lengths, seq, 0, False)
    info = jnp.stack([length, first, core, d, rank, z]).astype(jnp.int32)
    live = (lax.broadcasted_iota(jnp.int32, (rows, 1), 0) + first < length).astype(f32)
    row_at = seq * bucket + first
    own_in = lax.dynamic_slice_in_dim(inputs, row_at, rows, 0)
    own_target = lax.dynamic_slice_in_dim(cotangent, row_at, rows, 0)
    latent = w_latent.shape[2] // 2
    far_group = z // (planes // 2)

    cols = w_query.shape[2]
    hidden_cols = w_gate.shape[2]
    heads_here = jnp.concatenate([w_query[0], w_key[0], w_value[0]], axis=0)
    heads_there = core_swap(heads_here)
    lat_here = w_latent[0]
    lat_there = core_swap(lat_here)
    gain_here = gains[0]
    gain_there = core_swap(gain_here)
    out_here = w_out[0]
    feed_here = [w_gate[0].T, w_up[0].T, w_down[0]]
    head_rows, out_rows, feed_rows = heads_here.shape[0], out_here.shape[0], hidden_cols

    def piece_rows(count):
        return -(-count // (2 * dp * 16)) * 16

    def piece_of(value, side):
        rows_each = piece_rows(value.shape[0])
        value = jnp.pad(value, ((0, rows_each * 2 * dp - value.shape[0]), (0, 0)))
        return lax.dynamic_slice_in_dim(value, (side * dp + d) * rows_each, rows_each, 0)

    def feed_and_out(side):
        return jnp.concatenate([piece_of(v, side) for v in [out_here] + feed_here], axis=0)

    def layers_of(mine, received):
        return [jnp.where(core == layer, mine, received) for layer in range(layers)]

    main_pieces = layers_of(feed_and_out(core), core_swap(feed_and_out(1 - core)))
    head_pieces = layers_of(piece_of(heads_here, core), core_swap(piece_of(heads_here, 1 - core)))
    head_piece, out_piece, feed_piece = piece_rows(head_rows), piece_rows(out_rows), piece_rows(feed_rows)
    out_far = [z_swap(main_pieces[0][:out_piece], step) for step in range(1, planes)]
    feed_far = z_swap(main_pieces[0][out_piece:], planes // 2)
    out_there = core_swap(tie(out_here, feed_far))
    feed_there = [core_swap(tie(v, feed_far)) for v in feed_here]
    latents_w = [jnp.where(core == layer, lat_here, lat_there) for layer in range(layers)]
    gains_all = [jnp.where(core == layer, gain_here, gain_there) for layer in range(layers)]

    def over_planes(piece):
        return [z_swap(piece, step) for step in range(1, planes)]

    def gather_near(parts, *before):
        return plane_gather(jnp.concatenate([tie(v, *before) for v in parts], axis=0))

    def gather(parts, before=(), after=()):
        near = gather_near(parts, *before)
        return near, core_swap(tie(near, *after))

    def gather_slow(parts, before=()):
        return lax.all_gather(jnp.concatenate([tie(v, *before) for v in parts], axis=0), "dp", axis=0, tiled=False)

    def by_group(value):
        return by_plane(value, far_group)

    def normalise(x, gain):
        x = x.astype(f32)
        return (x * inverse_rms(x) * gain).astype(bf16)

    def first_attention(*after):
        scalars = jnp.stack([lax.dynamic_index_in_dim(lengths, core, 0, False), z, core, far_group]).astype(jnp.int32)
        out = attend_first_call(
            scalars, inputs, lat_here, lat_there, tie(heads_here, *after), heads_there, gain_here, gain_there, bucket, per_seq
        )
        messages = []
        for way in range(per_seq):
            pairs = []
            for side in range(2):
                for plane in range(planes):
                    to = plane ^ way
                    target = (to % 2) * planes + side * (planes // seqs) + to // 2
                    pairs.append((side * planes + plane, target))
            messages.append(lax.ppermute(out[way], ("section", "tensor"), pairs))
        return out, messages

    def first_latents(*after):
        all_rows = tie(lax.dynamic_slice_in_dim(inputs, seq * bucket, bucket, 0), *after)
        lat = dot_nn(normalise(all_rows, gains_all[0][0]), latents_w[0]).astype(bf16)
        return by_group(jnp.stack([lat[:, :latent], lat[:, latent:]]))

    def attention(layer, x, pack):
        gain = gains_all[layer]
        normed = normalise(x, gain[0])
        own_lat = dot_nn(normed, latents_w[layer]).astype(bf16)
        own_lat = jnp.where(
            far_group == 1, jnp.concatenate([own_lat[:, latent:], own_lat[:, :latent]], axis=1), own_lat
        )
        far_lat = z_swap(own_lat, 1)
        lats = (own_lat, core_swap(own_lat), far_lat, core_swap(far_lat))
        mixed, lse, lat, residual, normed2 = attend_call(info, layer, x, normed, lats, pack, gain[1][None])
        return normed, lat, mixed, lse, residual, normed2

    def feed_own(layer, normed2, feed_w):
        far_normed2 = z_swap(normed2, 1)
        part, saved = feed_call(info, layer, normed2, feed_w, f32)
        return part, saved, tie(far_normed2, part)

    def feed_rest(layer, residual, part, far_normed2, feed_w):
        far_part, far_saved = feed_call(info, layer, far_normed2, feed_w, bf16)
        feed = part + z_swap(far_part, 1).astype(f32)
        return (live * (residual + feed)).astype(bf16), far_saved

    def finish_core(firsts, seconds):
        mine = jnp.where(core == 0, firsts, seconds)
        other = core_swap(jnp.where(core == 0, seconds, firsts))
        return jnp.where(core == 0, jnp.stack([mine, other]), jnp.stack([other, mine]))

    def backward(layer, grad_out, x, normed, lat, mixed, lse, residual, feed_kept, pack, feed_w, hooks):
        normed2, far_normed2, saved, far_saved = feed_kept
        gain = gains_all[layer]
        grad_res = live * grad_out.astype(f32)
        grad_feed = grad_res.astype(bf16)
        far_feed = z_swap(grad_feed, 1)
        part, *rights = feed_back_call(info, layer, grad_feed, saved, feed_w, f32)
        far_part, *far_rights = feed_back_call(info, layer, far_feed, far_saved, feed_w, bf16)
        back = z_swap(far_part, 1)
        lefts = [normed2, far_normed2, core_swap(normed2), core_swap(far_normed2)]
        lefts += [grad_feed, far_feed, core_swap(grad_feed), core_swap(far_feed)]
        rights = [rights[0], far_rights[0], core_swap(rights[1]), core_swap(far_rights[1])]
        lefts[0] = tie(lefts[0], *hooks[3]())
        feed_grads = feed_weights_call(info, lefts, rights, dp, hidden_cols)
        back = tie(back, feed_grads, *hooks[0]())
        grad_norm2 = part + back.astype(f32)
        grad_residual, gain_second = norm_back(residual, gain[1], grad_norm2)
        grad_residual = grad_residual + grad_res
        grad_branch = grad_residual.astype(bf16)

        feed_parts = lax.all_to_all(feed_grads, "dp", 0, 0)
        grad_norms = []
        lat_parts = []
        pack_parts_here = []
        for first_set in (2, 0):
            if first_set == 0:
                grad_branch = tie(grad_branch, grad_norms[0], *hooks[1](grad_branch))
            grad_norm, grad_lat, pack_keep, pack_send = attend_back_call(
                first_set, info, layer, grad_branch, normed, lat, pack, mixed, lse, dp
            )
            grad_norms.append(grad_norm)
            pack_parts_here.append((pack_keep, core_swap(pack_send)))
            grad_lat = grad_lat.reshape(per_seq // 2, 2, rows, latent)
            total = lax.dynamic_index_in_dim(grad_lat, core, 1, False) + core_swap(
                lax.dynamic_index_in_dim(grad_lat, 1 - core, 1, False)
            )
            near = rank // 2
            total = lax.dynamic_index_in_dim(total, near, 0, False) + z_swap(
                lax.dynamic_index_in_dim(total, 1 - near, 0, False), 1
            )
            lat_parts.append(total)
        if layer == 0:
            feed_sums = jnp.sum(feed_parts.astype(f32), axis=0).astype(bf16)
            lat_parts[1] = tie(lat_parts[1], feed_sums, *hooks[2]())
        else:
            lat_parts[1] = tie(lat_parts[1], feed_parts, *hooks[2]())
        lat_own = by_group(jnp.stack(lat_parts[::-1]))
        lat_own = jnp.concatenate([lat_own[0], lat_own[1]], axis=1)
        grad_norm = grad_norms[0] + grad_norms[1] + dot_nt(lat_own, latents_w[layer])
        grad_x, gain_first = norm_back(x.astype(f32), gain[0], grad_norm)
        grad_x = (grad_x + grad_residual).astype(bf16)

        lat_w = dot_tn(normed, lat_own).astype(bf16).reshape(planes, dp, width // planes // dp * 2, latent)
        gain_g = jnp.stack([gain_first, gain_second]).astype(bf16)
        gain_g = gain_g.reshape(2, planes, dp, -1).transpose(1, 2, 0, 3).reshape(planes, dp, 1, -1)
        gain_g = jnp.pad(gain_g, ((0, 0), (0, 0), (0, 31), (0, latent - gain_g.shape[3])))
        small = jnp.swapaxes(by_plane(jnp.concatenate([lat_w, gain_g], axis=2), z), 0, 1)
        half = small.shape[2] // 2
        small_keep = lax.dynamic_slice_in_dim(small, core * half, half, 2)
        small_send = lax.dynamic_slice_in_dim(small, (1 - core) * half, half, 2)
        small_parts = (small_keep, core_swap(small_send))

        if layer == 1:
            feed_sums = jnp.sum(tie(feed_parts, grad_x).astype(f32), axis=0).astype(bf16)
        if layer == 0:
            pack_parts_here = [(a, tie(b, grad_x)) for a, b in pack_parts_here]
        pack_total = jnp.concatenate([a + b for a, b in pack_parts_here[::-1]], axis=1)
        small_total = small_parts[0] + small_parts[1]
        pack_parts = lax.all_to_all(jnp.concatenate([pack_total, small_total], axis=2), "dp", 0, 0)

        def finish_feed():
            pairs = [((1 - layer) * planes + i, layer * planes + (i ^ (planes // 2))) for i in range(planes)]
            far = lax.ppermute(feed_sums, ("section", "tensor"), pairs)
            return feed_sums.astype(f32) + far.astype(f32), far

        def finish_pack(*after):
            parts = tie(pack_parts, *after)
            sums = jnp.sum(parts.astype(f32), axis=0).astype(bf16)
            sums = sums[0::2] + z_swap(sums[1::2], 1)
            return sums[0] + z_swap(sums[1], 2)

        return grad_x, pack_parts, finish_feed, finish_pack

    lat0 = first_latents()
    first_out, messages = first_attention(feed_far, lat0)
    main0 = gather(out_far + [feed_far], (), messages)
    outs0 = (out_here, out_there) + main0 + (0, out_piece)
    at = (planes - 1) * out_piece
    feed0 = (feed_here, feed_there, [main0 + (at + k * feed_piece, feed_piece) for k in range(3)])
    mixed0, lse0, residual0, normed2_0 = attend_out_call(info, 0, own_in, messages, outs0, gains_all[0][1][None])
    near_heads1 = gather_slow(over_planes(head_pieces[1]), (first_out,))
    part0, saved0, far_normed2 = feed_own(0, normed2_0, feed0)
    far_normed2 = tie(far_normed2, near_heads1)
    main_piece = tie(main_pieces[1], *messages)
    far_main = over_planes(main_piece[:out_piece]) + [z_swap(main_piece[out_piece:], planes // 2)]
    near1 = gather_near(far_main, part0)
    out0, far_saved0 = feed_rest(0, residual0, part0, far_normed2, feed0)
    kept0 = [normed2_0, far_normed2, saved0, far_saved0]
    main1 = near1, core_swap(tie(near1, out0))
    heads1 = (heads_here, heads_there, near_heads1, core_swap(near_heads1), 0, head_piece)
    outs1 = (out_here, out_there) + main1 + (0, out_piece)
    feed1 = (feed_here, feed_there, [main1 + (at + k * feed_piece, feed_piece) for k in range(3)])

    normed1, lat1, mixed1, lse1, residual1, normed2_1 = attention(1, out0, (heads1, outs1))
    part1, saved1, far_normed2 = feed_own(1, normed2_1, feed1)
    out1, far_saved1 = feed_rest(1, residual1, part1, far_normed2, feed1)
    kept1 = [normed2_1, far_normed2, saved1, far_saved1]
    def gather_rows(own):
        return lax.all_gather(own, "tensor", axis=0, tiled=False)

    def to_core(layer, found):
        return found, lax.ppermute(found, "section", [(1 - layer, layer)])

    rows_out = [gather_rows(out0), gather_rows(out1)]
    near_heads0 = gather_slow(over_planes(tie(head_pieces[0], normed2_1)), (part1,))
    heads0 = (heads_here, heads_there, near_heads0, core_swap(tie(near_heads0, out1)), 0, head_piece)
    grad1, pack_parts1, finish_feed1, finish_pack1 = backward(
        1, own_target, out0, normed1, lat1, mixed1, lse1, residual1, kept1, (heads1, outs1), feed1,
        [lambda: (rows_out[0],), lambda token: (), lambda: (rows_out[1],), lambda: ()],
    )
    normed0 = normalise(own_in, gains_all[0][0])
    later = {}

    def before_weights():
        later["feed"], far = finish_feed1()
        return (pack_parts1, far)

    def during_attention(token):
        return ()

    def after_attention():
        later["pack"] = finish_pack1()
        later["grad"] = gather_rows(grad1)
        return (later["pack"], later["grad"])

    grad0, _, finish_feed0, finish_pack0 = backward(
        0, grad1, own_in, normed0, lat0, mixed0, lse0, residual0, kept0, (heads0, outs0), feed0,
        [lambda: (), during_attention, after_attention, before_weights],
    )
    rows_grad0 = gather_rows(grad0)
    layer_outputs = rows_call(info, *to_core(0, rows_out[0]), *to_core(1, rows_out[1]))
    input_grads = rows_call(info, *to_core(0, rows_grad0), *to_core(1, later["grad"]))

    feed_final0, feed_far0 = finish_feed0()
    feed_total = jnp.where(core == 0, feed_final0, later["feed"])
    gate_t, up_t, down_t = feed_total[:, :, :hidden_cols]
    halves = finish_core(finish_pack0(), later["pack"]).astype(f32)
    main = (head_rows + width) // dp // 2
    query_t, key_t = halves[0, : width // dp], halves[0, width // dp : main]
    value_t, out_t = halves[1, : latent // dp], halves[1, latent // dp : main]
    small = halves[:, main:].reshape(-1, latent)
    lat_rows = width // planes // dp * 2
    lat_t = small[:lat_rows].reshape(lat_rows // 2, 2 * latent)
    gain_t = small[lat_rows, : 2 * width // planes // dp].reshape(2, -1)
    return (
        layer_outputs[None],
        input_grads[None],
        query_t[None],
        lat_t[None],
        key_t[None],
        value_t[None],
        out_t.T[None],
        gain_t[None],
        gate_t[None],
        up_t[None],
        down_t.T[None],
    )


def solution(mesh):
    placed = (
        P("dp", None),
        P("dp", None),
        P("dp"),
        P("section", None, "tensor"),
        P("section", None, None),
        P("section", None, "tensor"),
        P("section", None, "tensor"),
        P("section", "tensor", None),
        P("section", None, None),
        P("section", None, "tensor"),
        P("section", None, "tensor"),
        P("section", "tensor", None),
    )
    return jax.shard_map(
        shards,
        mesh=mesh,
        in_specs=placed,
        out_specs=(
            P("section", "dp", None),
            P("section", "dp", None),
            P("section", "dp", "tensor"),
            P("section", ("tensor", "dp"), None),
            P("section", "dp", "tensor"),
            P("section", "dp", "tensor"),
            P("section", "tensor", "dp"),
            P("section", None, ("tensor", "dp")),
            P("section", "dp", "tensor"),
            P("section", "dp", "tensor"),
            P("section", "tensor", "dp"),
        ),
        check_vma=False,
    )
```

```python
import functools

import jax
import jax.numpy as jnp
from jax import lax
from jax.experimental import pallas as pl
from jax.experimental.pallas import tpu as pltpu
from jax.sharding import PartitionSpec as P

HEAD_DIM = 64
eps = 1e-06
masked_score = -1e30
f32 = jnp.float32
bf16 = jnp.bfloat16


def dot_nn(left, right):
    return lax.dot_general(left, right, (((1,), (0,)), ((), ())), preferred_element_type=f32)


def dot_nt(left, right):
    return lax.dot_general(left, right, (((1,), (1,)), ((), ())), preferred_element_type=f32)


def dot_tn(left, right):
    return lax.dot_general(left, right, (((0,), (0,)), ((), ())), preferred_element_type=f32)


def core_swap(value):
    return lax.ppermute(value, "section", [(0, 1), (1, 0)])


def z_swap(value, step):
    count = lax.axis_size("tensor")
    return lax.ppermute(value, "tensor", [(i, i ^ step) for i in range(count)])


def tie(first, *others):
    return lax.optimization_barrier((first,) + others)[0]


def bits_of(count):
    return [1 << i for i in range(count.bit_length() - 1)]


def plane_gather(piece):
    count = lax.axis_size("dp")
    return lax.all_to_all(jnp.broadcast_to(piece[None], (count,) + piece.shape), "dp", 0, 0)


def plane_sum(parts):
    return jnp.sum(lax.all_to_all(parts, "dp", 0, 0).astype(f32), axis=0).astype(bf16)


def by_plane(values, flip_of):
    count = values.shape[0]
    for bit in bits_of(count):
        order = [k ^ bit for k in range(count)]
        flipped = jnp.stack([values[k] for k in order])
        values = jnp.where((flip_of // bit) % 2 == 1, flipped, values)
    return values


def inverse_rms(rows):
    return lax.rsqrt(jnp.mean(rows * rows, axis=-1, keepdims=True) + eps)


def norm_back(rows, gain, grad_norm):
    scale = inverse_rms(rows)
    weighted = grad_norm * gain
    inner = jnp.mean(weighted * rows, axis=-1, keepdims=True)
    grad_rows = scale * weighted - rows * scale * scale * scale * inner
    grad_gain = jnp.sum(grad_norm * rows * scale, axis=0)
    return (grad_rows, grad_gain)


LENGTH, FIRST, CORE, MEMBER, RANK, PLANE = range(6)


def kernel_call(kernel, info, arrays, grid, in_specs, out_specs, out_shape, scratch, name, flops, transcendentals=0):
    size = sum(a.size * a.dtype.itemsize for a in arrays)
    size += sum(o.size * o.dtype.itemsize for o in out_shape)
    return pl.pallas_call(
        kernel,
        grid_spec=pltpu.PrefetchScalarGridSpec(
            num_scalar_prefetch=1,
            grid=grid,
            in_specs=in_specs,
            out_specs=out_specs,
            scratch_shapes=scratch,
        ),
        out_shape=out_shape,
        compiler_params=pltpu.CompilerParams(
            dimension_semantics=("arbitrary",) * len(grid), vmem_limit_bytes=52 * 1024 * 1024
        ),
        cost_estimate=pl.CostEstimate(flops=flops, bytes_accessed=size, transcendentals=transcendentals),
        name=name,
    )(info, *arrays)


def whole(array):
    shape = array.shape
    return pl.BlockSpec(shape, lambda i, info: (0,) * len(shape))


def lead(array):
    shape = array.shape[1:]
    return pl.BlockSpec((1,) + shape, lambda i, info: (i,) + (0,) * len(shape))


def like(shape, dtype):
    return jax.ShapeDtypeStruct(shape, dtype)


class PackCopies:
    def __init__(self, info, layer, parts, held, sems):
        self.info, self.layer, self.parts, self.held, self.sems = info, layer, parts, held, sems

    def own(self, slot, there):
        for at, (part, target) in enumerate(zip(self.parts, self.held)):
            source = part[1] if there else part[0]
            rows = source.shape[0]
            yield pltpu.make_async_copy(source, target.at[slot, pl.ds(0, rows)], self.sems.at[slot, at])

    def pieces(self, slot, step):
        at = 0
        for (_, _, near, other, begin, rows), held in zip(self.parts, self.held):
            members = near.shape[0]
            source_at = pl.multiple_of(begin + (step - 1) * rows, 16)
            for key in range(members):
                for source, core in ((near, self.info[CORE]), (other, 1 - self.info[CORE])):
                    target = pl.multiple_of((core * members + key) * rows, 16)
                    yield pltpu.make_async_copy(
                        source.at[key, pl.ds(source_at, rows)],
                        held.at[slot, pl.ds(target, rows)],
                        self.sems.at[slot, at],
                    )
                    at += 1

    def each(self, step, act):
        slot = step % 2

        def run(copies):
            for copy in copies:
                act(copy)

        there = self.info[CORE] != self.layer
        pl.when((step == 0) & there)(lambda: run(self.own(slot, True)))
        pl.when((step == 0) & jnp.logical_not(there))(lambda: run(self.own(slot, False)))
        pl.when(step > 0)(lambda: run(self.pieces(slot, step)))

    def start(self, step):
        self.each(step, lambda copy: copy.start())

    def turn(self, step, first, last):
        @pl.when(step == first)
        def _():
            self.start(step)

        @pl.when(step < last)
        def _():
            self.start(step + 1)

        self.each(step, lambda copy: copy.wait())
        return [held.at[step % 2] for held in self.held]


def pack_refs(spec, refs):
    return [tuple(refs[4 * at : 4 * at + 4]) + part for at, part in enumerate(spec)]


def fill_bias(info, bias):
    keys, rows = bias.shape
    key_pos = lax.broadcasted_iota(jnp.int32, (keys, rows), 0)
    query_pos = lax.broadcasted_iota(jnp.int32, (keys, rows), 1) + info[FIRST]
    allowed = (key_pos <= query_pos) & (key_pos < info[LENGTH])
    bias[...] = jnp.where(allowed, 0.0, masked_score)


def head_parts(heads, width, latent):
    at = (0, width, width + latent, width + 2 * latent)
    return [heads[lo:hi] for lo, hi in zip(at[:-1], at[1:])]


def attend_sets(keys, values_t, query, bias, heads):
    lane_head = lax.broadcasted_iota(jnp.int32, query.shape, 1) // HEAD_DIM
    mixed, sums = [], []
    for head in range(heads):
        query_here = jnp.where(lane_head == head, query, bf16(0))
        scores = dot_nt(keys, query_here) + bias
        peak = jnp.max(scores, axis=0, keepdims=True)
        expo = jnp.exp(scores - peak)
        total = jnp.sum(expo, axis=0, keepdims=True)
        part = dot_nn(values_t[head * HEAD_DIM : (head + 1) * HEAD_DIM], expo.astype(bf16))
        mixed.append(part * (1.0 / total))
        sums.append(peak + jnp.log(total))
    return jnp.concatenate(mixed, axis=0), jnp.concatenate(sums, axis=0)


def attend_first_kernel(
    info, x, lat_here, lat_there, heads_here, heads_there, gain_here, gain_there, out, normed, query_all, keys_all, values_t_all
):
    keys_count, width = x.shape
    latent = lat_here.shape[1]
    cols = heads_here.shape[1]
    heads = cols // HEAD_DIM
    rows = keys_count // out.shape[0]
    here = info[2] == 0
    gain = jnp.where(here, gain_here[0:1], gain_there[0:1])
    pack = jnp.where(here, heads_here[...], heads_there[...])
    w_latent = jnp.where(here, lat_here[...], lat_there[...])
    for block in range(keys_count // rows):
        here = slice(block * rows, (block + 1) * rows)
        value = x[here].astype(f32)
        normed[here] = (value * inverse_rms(value) * gain).astype(bf16)
    w_query, w_key, w_value = head_parts(pack, width, latent)
    query_all[...] = dot_nn(normed[...], w_query).astype(bf16) * bf16(HEAD_DIM**-0.5)
    lat = dot_nn(normed[...], w_latent).astype(bf16)
    keys_all[...] = dot_nn(lat, w_key).astype(bf16)
    values_t_all[...] = dot_nn(lat, w_value).astype(bf16).T
    for block in range(keys_count // rows):
        first = block * rows
        end = first + rows
        key_pos = lax.broadcasted_iota(jnp.int32, (end, rows), 0)
        query_pos = lax.broadcasted_iota(jnp.int32, (end, rows), 1) + first
        bias = jnp.where((key_pos <= query_pos) & (key_pos < info[0]), 0.0, masked_score)
        mixed, sums = attend_sets(keys_all[0:end], values_t_all[:, 0:end], query_all[first:end], bias, heads)
        high = sums.astype(bf16)
        low = (sums - high.astype(f32)).astype(bf16)
        at = info[1] ^ block
        out[at, 0:rows, :] = mixed.T.astype(bf16)
        out[at, rows:, :] = jnp.concatenate([high, low, jnp.zeros((16 - 2 * heads, rows), bf16)], axis=0)


def attend_out_kernel(
    spec, layer, info, x, m0, m1, m2, m3, gain, o0, o1, o2, o3, mixed_out, lse_out, residual, normed2, sets, outs, sems
):
    step = pl.program_id(0)
    rows, width = x.shape
    heads = lse_out.shape[1]
    copies = PackCopies(info, layer, pack_refs(spec, (o0, o1, o2, o3)), [outs], sems)
    w_out = copies.turn(step, 0, pl.num_programs(0) - 1)[0]

    @pl.when(step == 0)
    def _():
        residual[...] = x[...].astype(f32)
        for key, piece in enumerate((m0, m1, m2, m3)):
            sets[key ^ info[RANK] ^ info[PLANE]] = piece[...]

    mixed = sets[step, 0:rows, :]
    tail = sets[step, rows:, :].astype(f32)
    mixed_out[0] = mixed
    lse_out[0] = tail[0:heads] + tail[heads : 2 * heads]
    residual[...] += dot_nn(mixed, w_out[0 : mixed.shape[1]])

    @pl.when(step == pl.num_programs(0) - 1)
    def _():
        full = residual[...]
        normed2[...] = (full * inverse_rms(full) * gain[...]).astype(bf16)


def attend_kernel(
    spec, layer, info, x, normed, lat0, lat1, lat2, lat3, gain, h0, h1, h2, h3, o0, o1, o2, o3,
    mixed_out, lse_out, lat_out, residual, normed2, bias, heads_held, outs_held, sems,
):
    step = pl.program_id(0)
    rows, width = normed.shape
    latent = lat_out.shape[2]
    heads = lse_out.shape[1]
    parts = pack_refs(spec, (h0, h1, h2, h3, o0, o1, o2, o3))
    copies = PackCopies(info, layer, parts, [heads_held, outs_held], sems)
    w_heads, w_out = copies.turn(step, 0, pl.num_programs(0) - 1)

    @pl.when(step == 0)
    def _():
        fill_bias(info, bias)
        residual[...] = x[...].astype(f32)
        for key, piece in enumerate((lat0, lat1, lat2, lat3)):
            at = pl.multiple_of((info[RANK] ^ key) * rows, 16)
            for group in range(2):
                lat_out[group, pl.ds(at, rows), :] = piece[:, group * latent : (group + 1) * latent]

    w_query, w_key, w_value = head_parts(w_heads, width, latent)
    lat = lat_out[step // 2]
    query = dot_nn(normed[...], w_query).astype(bf16) * bf16(HEAD_DIM**-0.5)
    keys = dot_nn(lat, w_key).astype(bf16)
    values_t = dot_nn(lat, w_value).astype(bf16).T
    mixed, sums = attend_sets(keys, values_t, query, bias[...], heads)
    lse_out[0] = sums
    mixed = mixed.T.astype(bf16)
    mixed_out[0] = mixed
    residual[...] += dot_nn(mixed, w_out[0 : mixed.shape[1]])

    @pl.when(step == pl.num_programs(0) - 1)
    def _():
        full = residual[...]
        normed2[...] = (full * inverse_rms(full) * gain[...]).astype(bf16)


def attend_back_kernel(
    first_set, spec, layer, info, grad_branch, normed, lat, mixed_in, lse_in, h0, h1, h2, h3, o0, o1, o2, o3,
    grad_norm, grad_lat, keep, send, bias, heads_held, outs_held, sems, lat_sum,
):
    step = pl.program_id(0)
    rows, width = normed.shape
    keys_count, latent = grad_lat.shape
    cols = heads_held.shape[2]
    scale = HEAD_DIM**-0.5
    members = keep.shape[0]
    parts = pack_refs(spec, (h0, h1, h2, h3, o0, o1, o2, o3))
    copies = PackCopies(info, layer, parts, [heads_held, outs_held], sems)
    w_heads, w_out = copies.turn(step + first_set, first_set, first_set + pl.num_programs(0) - 1)

    @pl.when(step == 0)
    def _():
        fill_bias(info, bias)
        grad_norm[...] = jnp.zeros_like(grad_norm)
        lat_sum[...] = jnp.zeros_like(lat_sum)

    w_query, w_key, w_value = head_parts(w_heads, width, latent)
    here = lat[0]
    query = dot_nn(normed[...], w_query).astype(bf16) * bf16(scale)
    keys = dot_nn(here, w_key).astype(bf16)
    keys_t = keys.T
    values = dot_nn(here, w_value).astype(bf16)
    mixed = mixed_in[0]
    grad_mixed = dot_nt(grad_branch[...], w_out[0:cols]).astype(bf16)
    centre = (grad_mixed.astype(f32) * mixed.astype(f32)).T
    lane_head = lax.broadcasted_iota(jnp.int32, (rows, cols), 1) // HEAD_DIM
    grad_keys = jnp.zeros((keys_count, cols), f32)
    grad_values = jnp.zeros((keys_count, cols), f32)
    grad_query_parts = []
    for head in range(cols // HEAD_DIM):
        mine = slice(head * HEAD_DIM, (head + 1) * HEAD_DIM)
        query_here = jnp.where(lane_head == head, query, bf16(0))
        grad_here = jnp.where(lane_head == head, grad_mixed, bf16(0))
        scores = dot_nt(keys, query_here) + bias[...]
        probs = jnp.exp(scores - lse_in[0, head : head + 1, :])
        grad_probs = dot_nt(values, grad_here)
        inner = jnp.sum(centre[mine], axis=0, keepdims=True)
        grad_scores = (probs * (grad_probs - inner)).astype(bf16)
        grad_values += dot_nn(probs.astype(bf16), grad_here)
        grad_keys += dot_nn(grad_scores, query_here)
        grad_query_parts.append(dot_nn(keys_t[mine], grad_scores) * scale)
    grad_keys = grad_keys.astype(bf16)
    grad_values = grad_values.astype(bf16)
    grad_query = jnp.concatenate(grad_query_parts, axis=0).T.astype(bf16)
    grad_norm[...] += dot_nt(grad_query, w_query)
    lat_sum[...] += dot_nt(grad_keys, w_key) + dot_nt(grad_values, w_value)
    halves = (
        (dot_tn(normed[...], grad_query), dot_tn(here, grad_keys)),
        (dot_tn(here, grad_values), dot_tn(grad_branch[...], mixed)),
    )
    for half, results in enumerate(halves):
        for out, wanted in ((keep, half), (send, 1 - half)):

            @pl.when(info[CORE] == wanted)
            def _(out=out, results=results):
                at = 0
                for result in results:
                    size = result.shape[0] // members
                    for member in range(members):
                        out[member, 0, at : at + size, :] = result[member * size : (member + 1) * size].astype(bf16)
                    at += size

    @pl.when(step == pl.num_programs(0) - 1)
    def _():
        grad_lat[...] = lat_sum[...].astype(bf16)


def attend_first_call(info, x, lat_here, lat_there, heads_here, heads_there, gain_here, gain_there, keys, blocks):
    width = x.shape[1]
    latent = lat_here.shape[1] // 2
    cols = heads_here.shape[1]
    outs = [like((blocks, keys // blocks + 16, cols), bf16)]
    arrays = (x, lat_here, lat_there, heads_here, heads_there, gain_here, gain_there)
    group = pl.BlockSpec((width, latent), lambda i, info: (0, info[3]))
    return kernel_call(
        attend_first_kernel,
        info,
        arrays,
        (1,),
        [pl.BlockSpec((keys, width), lambda i, info: (info[2], 0)), group, group] + [whole(v) for v in arrays[3:]],
        [whole(o) for o in outs],
        outs,
        [pltpu.VMEM((keys, width), bf16)] + [pltpu.VMEM((keys, cols), bf16)] * 2 + [pltpu.VMEM((cols, keys), bf16)],
        "attend_first",
        2 * keys * width * (cols + latent) + 4 * keys * latent * cols + 4 * keys * keys * cols * 3,
        keys * keys * 3,
    )[0]


def pack_in(*parts):
    arrays = sum((tuple(part[0:4]) for part in parts), ())
    spec = tuple(tuple(part[4:]) for part in parts)
    members = parts[0][2].shape[0]
    scratch = [pltpu.VMEM((2, 2 * members * part[5], part[0].shape[1]), bf16) for part in parts]
    scratch.append(pltpu.SemaphoreType.DMA((2, 2 * members * len(parts))))
    return arrays, spec, [pl.BlockSpec(memory_space=pl.ANY)] * len(arrays), scratch


def attend_out_call(info, layer, x, messages, outs_w, gain):
    rows, width = x.shape
    arrays, spec, specs, scratch = pack_in(outs_w)
    sets = 4
    cols = messages[0].shape[1]
    heads = cols // HEAD_DIM
    outs = [
        like((sets, rows, cols), bf16),
        like((sets, heads, rows), f32),
        like((rows, width), f32),
        like((rows, width), bf16),
    ]
    return kernel_call(
        functools.partial(attend_out_kernel, spec, layer),
        info,
        (x, *messages, gain) + arrays,
        (sets,),
        [whole(x)] + [whole(m) for m in messages] + [whole(gain)] + specs,
        [lead(outs[0]), lead(outs[1]), whole(outs[2]), whole(outs[3])],
        outs,
        [pltpu.VMEM((sets,) + messages[0].shape, bf16)] + scratch,
        "attend_out",
        2 * sets * rows * width * cols,
    )


def attend_call(info, layer, x, normed, lats, pack, gain):
    rows, width = normed.shape
    arrays, spec, specs, scratch = pack_in(*pack)
    sets = 4
    cols = arrays[0].shape[1]
    latent = lats[0].shape[1] // 2
    keys = rows * len(lats)
    heads = cols // HEAD_DIM
    outs = [
        like((sets, rows, cols), bf16),
        like((sets, heads, rows), f32),
        like((2, keys, latent), bf16),
        like((rows, width), f32),
        like((rows, width), bf16),
    ]
    return kernel_call(
        functools.partial(attend_kernel, spec, layer),
        info,
        (x, normed, *lats, gain) + arrays,
        (sets,),
        [whole(x), whole(normed)] + [whole(v) for v in lats] + [whole(gain)] + specs,
        [lead(outs[0]), lead(outs[1])] + [whole(o) for o in outs[2:]],
        outs,
        [pltpu.VMEM((keys, rows), f32)] + scratch,
        "attend",
        2 * sets * rows * (2 * keys * cols * heads + width * cols * 2) + 4 * sets * keys * latent * cols,
        sets * heads * keys * rows,
    )


def attend_back_call(first_set, info, layer, grad_branch, normed, lat, pack, mixed, lse, members):
    rows, width = normed.shape
    arrays, spec, specs, scratch = pack_in(*pack)
    cols = arrays[0].shape[1]
    piece_rows = (arrays[0].shape[0] + width) // members // 2
    sets = 2
    keys, latent = lat.shape[1:]
    heads = cols // HEAD_DIM
    group = pl.BlockSpec((1, keys, latent), lambda i, info: (first_set // 2, 0, 0))
    outs = [
        like((rows, width), f32),
        like((keys, latent), bf16),
        like((members, sets, piece_rows, cols), bf16),
        like((members, sets, piece_rows, cols), bf16),
    ]
    summed = pl.BlockSpec((members, 1, piece_rows, cols), lambda i, info: (0, i, 0, 0))
    mine = [pl.BlockSpec((1,) + v.shape[1:], lambda i, info: (i + first_set, 0, 0)) for v in (mixed, lse)]
    return kernel_call(
        functools.partial(attend_back_kernel, first_set, spec, layer),
        info,
        (grad_branch, normed, lat, mixed, lse) + arrays,
        (sets,),
        [whole(grad_branch), whole(normed), group] + mine + specs,
        [whole(outs[0]), whole(outs[1]), summed, summed],
        outs,
        [pltpu.VMEM((keys, rows), f32)] + scratch + [pltpu.VMEM((keys, latent), f32)],
        "attend_back",
        2 * sets * rows * (5 * keys * cols * heads + width * cols * 5) + 16 * sets * keys * latent * cols,
        sets * heads * keys * rows,
    )


def feed_shards(spec, layer, info, refs, weights, sems, use):
    here, there, pieces = refs[0:3], refs[3:6], refs[6:12]
    hidden = here[0].shape[0]

    def run(act, far):
        if not far:
            for wanted, sources in ((True, here), (False, there)):

                @pl.when((info[CORE] == layer) == wanted)
                def _(sources=sources):
                    for kind, source in enumerate(sources):
                        act(pltpu.make_async_copy(source, weights.at[0, kind, pl.ds(0, hidden)], sems.at[kind]))

            return
        at = 3
        for kind, (begin, rows) in enumerate(spec):
            members = pieces[2 * kind].shape[0]
            for key in range(members):
                for source, core in ((pieces[2 * kind], info[CORE]), (pieces[2 * kind + 1], 1 - info[CORE])):
                    target = pl.multiple_of((core * members + key) * rows, 16)
                    act(
                        pltpu.make_async_copy(
                            source.at[key, pl.ds(begin, rows)], weights.at[1, kind, pl.ds(target, rows)], sems.at[at]
                        )
                    )
                    at += 1

    run(lambda copy: copy.start(), False)
    run(lambda copy: copy.start(), True)
    run(lambda copy: copy.wait(), False)
    use(0, [weights[0, kind, 0:hidden] for kind in range(3)])
    run(lambda copy: copy.wait(), True)
    use(1, [weights[1, kind, 0:hidden] for kind in range(3)])


def feed_kernel(spec, layer, info, value, *refs):
    total_out, saved, weights, sems, total = refs[12:]

    def use(shard, held):
        gate = dot_nt(value[...], held[0])
        up = dot_nt(value[...], held[1])
        saved[shard, 0] = gate.astype(bf16)
        saved[shard, 1] = up.astype(bf16)
        hidden = (gate * jax.nn.sigmoid(gate) * up).astype(bf16)
        part = dot_nn(hidden, held[2])
        if shard == 0:
            total[...] = part
        else:
            total_out[...] = (total[...] + part).astype(total_out.dtype)

    feed_shards(spec, layer, info, refs[0:12], weights, sems, use)


def feed_back_kernel(spec, layer, info, value, saved, *refs):
    total_out, keep, send, weights, sems, total = refs[12:]

    width = saved.shape[3]

    def use(shard, held):
        grad_hidden = dot_nt(value[...], held[2])
        gate = saved[shard, 0].astype(f32)
        up = saved[shard, 1].astype(f32)
        sigma = jax.nn.sigmoid(gate)
        silu = gate * sigma
        grad_gate = (grad_hidden * up * sigma * (1.0 + gate * (1.0 - sigma))).astype(bf16)
        grad_up = (grad_hidden * silu).astype(bf16)
        hidden = (silu * up).astype(bf16)
        mine = info[CORE] == layer if shard == 0 else info[CORE] != layer
        for out, wanted in ((keep, mine), (send, jnp.logical_not(mine))):

            @pl.when(wanted)
            def _(out=out):
                out[0, :, 0:width] = grad_gate
                out[1, :, 0:width] = grad_up
                out[2, :, 0:width] = hidden

        part = dot_nn(grad_gate, held[0]) + dot_nn(grad_up, held[1])
        if shard == 0:
            total[...] = part
        else:
            total_out[...] = (total[...] + part).astype(total_out.dtype)

    feed_shards(spec, layer, info, refs[0:12], weights, sems, use)


def feed_weights_kernel(hidden, info, *refs):
    lefts, rights, out, turned = refs[0:8], refs[8:12], refs[12], refs[13]
    kind = pl.program_id(0)
    rows = lefts[0].shape[0]
    members, _, size, lanes = out.shape

    @pl.when(kind == 0)
    def _():
        for at in range(2):
            for block in range(4):
                turned[at, :, block * rows : (block + 1) * rows] = lefts[4 * at + block][...].T

    right = jnp.concatenate([r[0] for r in rights], axis=0)
    left = turned[kind // 2]
    for first in range(0, hidden, 256):
        end = min(first + 256, hidden)
        result = dot_nn(left, right[:, first:end]).astype(bf16)
        for member in range(members):
            out[member, 0, :, first:end] = result[member * size : (member + 1) * size]
    out[:, :, :, hidden:] = jnp.zeros((members, 1, size, lanes - hidden), bf16)


def whole_lanes(count):
    return -(-count // 128) * 128


def feed_in(feed_w):
    here, there, pieces = feed_w
    arrays = (*here, *there, *sum((part[0:2] for part in pieces), ()))
    spec = tuple(part[2:4] for part in pieces)
    members, _, width = pieces[0][0].shape
    scratch = [
        pltpu.VMEM((2, 3, 2 * members * pieces[0][3], width), bf16),
        pltpu.SemaphoreType.DMA((3 + 6 * members,)),
    ]
    return arrays, spec, [pl.BlockSpec(memory_space=pl.ANY)] * len(arrays), scratch


def feed_call(info, layer, value, feed_w, dtype):
    rows, width = value.shape
    arrays, spec, specs, scratch = feed_in(feed_w)
    hidden = arrays[0].shape[0]
    outs = [like((rows, width), dtype), like((2, 2, rows, hidden), bf16)]
    return kernel_call(
        functools.partial(feed_kernel, spec, layer),
        info,
        (value,) + arrays,
        (1,),
        [whole(value)] + specs,
        [whole(o) for o in outs],
        outs,
        scratch + [pltpu.VMEM((rows, width), f32)],
        "feed",
        2 * 2 * 3 * rows * width * hidden,
    )


def feed_back_call(info, layer, value, saved, feed_w, dtype):
    rows, width = value.shape
    arrays, spec, specs, scratch = feed_in(feed_w)
    hidden = arrays[0].shape[0]
    outs = [like((rows, width), dtype)] + [like((3, rows, whole_lanes(hidden)), bf16)] * 2
    return kernel_call(
        functools.partial(feed_back_kernel, spec, layer),
        info,
        (value, saved) + arrays,
        (1,),
        [whole(value), whole(saved)] + specs,
        [whole(o) for o in outs],
        outs,
        scratch + [pltpu.VMEM((rows, width), f32)],
        "feed_back",
        2 * 2 * 3 * rows * width * hidden,
    )


def feed_weights_call(info, lefts, rights, members, hidden):
    rows, width = lefts[0].shape
    kinds, _, lanes = rights[0].shape
    shape = (members, kinds, width // members, lanes)
    outs = [like(shape, bf16)]
    return kernel_call(
        functools.partial(feed_weights_kernel, hidden),
        info,
        (*lefts, *rights),
        (kinds,),
        [whole(v) for v in lefts] + [lead(r) for r in rights],
        [pl.BlockSpec((members, 1) + shape[2:], lambda i, info: (0, i, 0, 0))],
        outs,
        [pltpu.VMEM((2, width, 4 * rows), bf16)],
        "feed_weights",
        2 * kinds * 4 * rows * width * hidden,
    )[0]


def rows_kernel(info, first, first_other, second, second_other, out, held, sems):
    planes, rows, _ = first.shape
    for core, sources in ((0, (first, first_other)), (1, (second_other, second))):

        @pl.when(info[CORE] == core)
        def _(sources=sources):
            copies = [pltpu.make_async_copy(v, held.at[:, at], sems.at[0, at]) for at, v in enumerate(sources)]
            for copy in copies:
                copy.start()
            for copy in copies:
                copy.wait()

    whole_copy = pltpu.make_async_copy(held, out, sems.at[1, 0])
    whole_copy.start()
    whole_copy.wait()


def rows_call(info, *arrays):
    planes, rows, width = arrays[0].shape
    shape = (planes, 2, rows, width)
    out = kernel_call(
        rows_kernel,
        info,
        arrays,
        (1,),
        [pl.BlockSpec(memory_space=pl.ANY)] * 4,
        [pl.BlockSpec(memory_space=pl.ANY)],
        [like(shape, bf16)],
        [pltpu.VMEM(shape, bf16), pltpu.SemaphoreType.DMA((2, 2))],
        "rows",
        0,
    )[0]
    return out.reshape(planes * 2 * rows, width)


def shards(inputs, cotangent, lengths, w_query, w_latent, w_key, w_value, w_out, gains, w_gate, w_up, w_down):
    core = lax.axis_index("section")
    z = lax.axis_index("tensor")
    d = lax.axis_index("dp")
    planes = lax.axis_size("tensor")
    dp = lax.axis_size("dp")
    seqs = lengths.shape[0]
    bucket = inputs.shape[0] // seqs
    width = inputs.shape[1]
    layers = 2
    per_seq = planes // seqs * 2
    rows = bucket // per_seq
    rank = (z % (planes // seqs)) * 2 + core
    seq = z // (planes // seqs)
    first = rank * rows
    length = lax.dynamic_index_in_dim(lengths, seq, 0, False)
    info = jnp.stack([length, first, core, d, rank, z]).astype(jnp.int32)
    live = (lax.broadcasted_iota(jnp.int32, (rows, 1), 0) + first < length).astype(f32)
    row_at = seq * bucket + first
    own_in = lax.dynamic_slice_in_dim(inputs, row_at, rows, 0)
    own_target = lax.dynamic_slice_in_dim(cotangent, row_at, rows, 0)
    latent = w_latent.shape[2] // 2
    far_group = z // (planes // 2)

    cols = w_query.shape[2]
    hidden_cols = w_gate.shape[2]
    heads_here = jnp.concatenate([w_query[0], w_key[0], w_value[0]], axis=0)
    heads_there = core_swap(heads_here)
    lat_here = w_latent[0]
    lat_there = core_swap(lat_here)
    gain_here = gains[0]
    gain_there = core_swap(gain_here)
    out_here = w_out[0]
    feed_here = [w_gate[0].T, w_up[0].T, w_down[0]]
    head_rows, out_rows, feed_rows = heads_here.shape[0], out_here.shape[0], hidden_cols

    def piece_rows(count):
        return -(-count // (2 * dp * 16)) * 16

    def piece_of(value, side):
        rows_each = piece_rows(value.shape[0])
        value = jnp.pad(value, ((0, rows_each * 2 * dp - value.shape[0]), (0, 0)))
        return lax.dynamic_slice_in_dim(value, (side * dp + d) * rows_each, rows_each, 0)

    def feed_and_out(side):
        return jnp.concatenate([piece_of(v, side) for v in [out_here] + feed_here], axis=0)

    def layers_of(mine, received):
        return [jnp.where(core == layer, mine, received) for layer in range(layers)]

    main_pieces = layers_of(feed_and_out(core), core_swap(feed_and_out(1 - core)))
    head_pieces = layers_of(piece_of(heads_here, core), core_swap(piece_of(heads_here, 1 - core)))
    head_piece, out_piece, feed_piece = piece_rows(head_rows), piece_rows(out_rows), piece_rows(feed_rows)
    out_far = [z_swap(main_pieces[0][:out_piece], step) for step in range(1, planes)]
    feed_far = z_swap(main_pieces[0][out_piece:], planes // 2)
    out_there = core_swap(out_here)
    feed_there = [core_swap(v) for v in feed_here]
    latents_w = [jnp.where(core == layer, lat_here, lat_there) for layer in range(layers)]
    gains_all = [jnp.where(core == layer, gain_here, gain_there) for layer in range(layers)]

    def over_planes(piece):
        return [z_swap(piece, step) for step in range(1, planes)]

    def gather_near(parts, *before):
        return plane_gather(jnp.concatenate([tie(v, *before) for v in parts], axis=0))

    def gather(parts, before=(), after=()):
        near = gather_near(parts, *before)
        return near, core_swap(tie(near, *after))

    def gather_slow(parts, before=()):
        return lax.all_gather(jnp.concatenate([tie(v, *before) for v in parts], axis=0), "dp", axis=0, tiled=False)

    def by_group(value):
        return by_plane(value, far_group)

    def normalise(x, gain):
        x = x.astype(f32)
        return (x * inverse_rms(x) * gain).astype(bf16)

    def first_attention(*after):
        scalars = jnp.stack([lax.dynamic_index_in_dim(lengths, core, 0, False), z, core, far_group]).astype(jnp.int32)
        out = attend_first_call(
            scalars, inputs, lat_here, lat_there, tie(heads_here, *after), heads_there, gain_here, gain_there, bucket, per_seq
        )
        messages = []
        for way in range(per_seq):
            pairs = []
            for side in range(2):
                for plane in range(planes):
                    to = plane ^ way
                    target = (to % 2) * planes + side * (planes // seqs) + to // 2
                    pairs.append((side * planes + plane, target))
            messages.append(lax.ppermute(out[way], ("section", "tensor"), pairs))
        return out, messages

    def first_latents(*after):
        all_rows = tie(lax.dynamic_slice_in_dim(inputs, seq * bucket, bucket, 0), *after)
        lat = dot_nn(normalise(all_rows, gains_all[0][0]), latents_w[0]).astype(bf16)
        return by_group(jnp.stack([lat[:, :latent], lat[:, latent:]]))

    def attention(layer, x, pack):
        gain = gains_all[layer]
        normed = normalise(x, gain[0])
        own_lat = dot_nn(normed, latents_w[layer]).astype(bf16)
        own_lat = jnp.where(
            far_group == 1, jnp.concatenate([own_lat[:, latent:], own_lat[:, :latent]], axis=1), own_lat
        )
        far_lat = z_swap(own_lat, 1)
        lats = (own_lat, core_swap(own_lat), far_lat, core_swap(far_lat))
        mixed, lse, lat, residual, normed2 = attend_call(info, layer, x, normed, lats, pack, gain[1][None])
        return normed, lat, mixed, lse, residual, normed2

    def feed_own(layer, normed2, feed_w):
        far_normed2 = z_swap(normed2, 1)
        part, saved = feed_call(info, layer, normed2, feed_w, f32)
        return part, saved, tie(far_normed2, part)

    def feed_rest(layer, residual, part, far_normed2, feed_w):
        far_part, far_saved = feed_call(info, layer, far_normed2, feed_w, bf16)
        feed = part + z_swap(far_part, 1).astype(f32)
        return (live * (residual + feed)).astype(bf16), far_saved

    def finish_core(firsts, seconds):
        mine = jnp.where(core == 0, firsts, seconds)
        other = core_swap(jnp.where(core == 0, seconds, firsts))
        return jnp.where(core == 0, jnp.stack([mine, other]), jnp.stack([other, mine]))

    def backward(layer, grad_out, x, normed, lat, mixed, lse, residual, feed_kept, pack, feed_w, hooks):
        normed2, far_normed2, saved, far_saved = feed_kept
        gain = gains_all[layer]
        grad_res = live * grad_out.astype(f32)
        grad_feed = grad_res.astype(bf16)
        far_feed = z_swap(grad_feed, 1)
        part, *rights = feed_back_call(info, layer, grad_feed, saved, feed_w, f32)
        far_part, *far_rights = feed_back_call(info, layer, far_feed, far_saved, feed_w, bf16)
        back = z_swap(far_part, 1)
        lefts = [normed2, far_normed2, core_swap(normed2), core_swap(far_normed2)]
        lefts += [grad_feed, far_feed, core_swap(grad_feed), core_swap(far_feed)]
        rights = [rights[0], far_rights[0], core_swap(rights[1]), core_swap(far_rights[1])]
        lefts[0] = tie(lefts[0], *hooks[3]())
        feed_grads = feed_weights_call(info, lefts, rights, dp, hidden_cols)
        back = tie(back, feed_grads, *hooks[0]())
        grad_norm2 = part + back.astype(f32)
        grad_residual, gain_second = norm_back(residual, gain[1], grad_norm2)
        grad_residual = grad_residual + grad_res
        grad_branch = grad_residual.astype(bf16)

        feed_parts = lax.all_to_all(feed_grads, "dp", 0, 0)
        grad_norms = []
        lat_parts = []
        pack_parts_here = []
        for first_set in (2, 0):
            if first_set == 0:
                grad_branch = tie(grad_branch, grad_norms[0], *hooks[1](grad_branch))
            grad_norm, grad_lat, pack_keep, pack_send = attend_back_call(
                first_set, info, layer, grad_branch, normed, lat, pack, mixed, lse, dp
            )
            grad_norms.append(grad_norm)
            pack_parts_here.append((pack_keep, core_swap(pack_send)))
            grad_lat = grad_lat.reshape(per_seq // 2, 2, rows, latent)
            total = lax.dynamic_index_in_dim(grad_lat, core, 1, False) + core_swap(
                lax.dynamic_index_in_dim(grad_lat, 1 - core, 1, False)
            )
            near = rank // 2
            total = lax.dynamic_index_in_dim(total, near, 0, False) + z_swap(
                lax.dynamic_index_in_dim(total, 1 - near, 0, False), 1
            )
            lat_parts.append(total)
        if layer == 0:
            feed_sums = jnp.sum(feed_parts.astype(f32), axis=0).astype(bf16)
            lat_parts[1] = tie(lat_parts[1], feed_sums, *hooks[2]())
        else:
            lat_parts[1] = tie(lat_parts[1], feed_parts, *hooks[2]())
        lat_own = by_group(jnp.stack(lat_parts[::-1]))
        lat_own = jnp.concatenate([lat_own[0], lat_own[1]], axis=1)
        grad_norm = grad_norms[0] + grad_norms[1] + dot_nt(lat_own, latents_w[layer])
        grad_x, gain_first = norm_back(x.astype(f32), gain[0], grad_norm)
        grad_x = (grad_x + grad_residual).astype(bf16)

        lat_w = dot_tn(normed, lat_own).astype(bf16).reshape(planes, dp, width // planes // dp * 2, latent)
        gain_g = jnp.stack([gain_first, gain_second]).astype(bf16)
        gain_g = gain_g.reshape(2, planes, dp, -1).transpose(1, 2, 0, 3).reshape(planes, dp, 1, -1)
        gain_g = jnp.pad(gain_g, ((0, 0), (0, 0), (0, 31), (0, latent - gain_g.shape[3])))
        small = jnp.swapaxes(by_plane(jnp.concatenate([lat_w, gain_g], axis=2), z), 0, 1)
        half = small.shape[2] // 2
        small_keep = lax.dynamic_slice_in_dim(small, core * half, half, 2)
        small_send = lax.dynamic_slice_in_dim(small, (1 - core) * half, half, 2)
        small_parts = (small_keep, core_swap(small_send))

        if layer == 1:
            feed_sums = jnp.sum(tie(feed_parts, grad_x).astype(f32), axis=0).astype(bf16)
        if layer == 0:
            pack_parts_here = [(a, tie(b, grad_x)) for a, b in pack_parts_here]
        pack_total = jnp.concatenate([a + b for a, b in pack_parts_here[::-1]], axis=1)
        small_total = small_parts[0] + small_parts[1]
        pack_parts = lax.all_to_all(jnp.concatenate([pack_total, small_total], axis=2), "dp", 0, 0)

        def finish_feed():
            pairs = [((1 - layer) * planes + i, layer * planes + (i ^ (planes // 2))) for i in range(planes)]
            far = lax.ppermute(feed_sums, ("section", "tensor"), pairs)
            return feed_sums.astype(f32) + far.astype(f32), far

        def finish_pack(*after):
            parts = tie(pack_parts, *after)
            sums = jnp.sum(parts.astype(f32), axis=0).astype(bf16)
            sums = sums[0::2] + z_swap(sums[1::2], 1)
            return sums[0] + z_swap(sums[1], 2)

        return grad_x, pack_parts, finish_feed, finish_pack

    lat0 = first_latents()
    first_out, messages = first_attention(feed_far, lat0, out_there, *feed_there)
    main0 = gather(out_far + [feed_far], (), messages)
    outs0 = (out_here, out_there) + main0 + (0, out_piece)
    at = (planes - 1) * out_piece
    feed0 = (feed_here, feed_there, [main0 + (at + k * feed_piece, feed_piece) for k in range(3)])
    mixed0, lse0, residual0, normed2_0 = attend_out_call(info, 0, own_in, messages, outs0, gains_all[0][1][None])
    near_heads1 = gather_slow(over_planes(head_pieces[1]), (first_out,))
    part0, saved0, far_normed2 = feed_own(0, normed2_0, feed0)
    far_normed2 = tie(far_normed2, near_heads1)
    main_piece = tie(main_pieces[1], *messages)
    far_main = over_planes(main_piece[:out_piece]) + [z_swap(main_piece[out_piece:], planes // 2)]
    near1 = gather_near(far_main, part0)
    out0, far_saved0 = feed_rest(0, residual0, part0, far_normed2, feed0)
    kept0 = [normed2_0, far_normed2, saved0, far_saved0]
    main1 = near1, core_swap(tie(near1, out0))
    heads1 = (heads_here, heads_there, near_heads1, core_swap(near_heads1), 0, head_piece)
    outs1 = (out_here, out_there) + main1 + (0, out_piece)
    feed1 = (feed_here, feed_there, [main1 + (at + k * feed_piece, feed_piece) for k in range(3)])

    normed1, lat1, mixed1, lse1, residual1, normed2_1 = attention(1, out0, (heads1, outs1))
    part1, saved1, far_normed2 = feed_own(1, normed2_1, feed1)
    out1, far_saved1 = feed_rest(1, residual1, part1, far_normed2, feed1)
    kept1 = [normed2_1, far_normed2, saved1, far_saved1]
    def gather_rows(own):
        return lax.all_gather(own, "tensor", axis=0, tiled=False)

    def to_core(layer, found):
        return found, lax.ppermute(found, "section", [(1 - layer, layer)])

    rows_out = [gather_rows(out0), gather_rows(out1)]
    near_heads0 = gather_slow(over_planes(tie(head_pieces[0], normed2_1)), (part1,))
    heads0 = (heads_here, heads_there, near_heads0, core_swap(tie(near_heads0, out1)), 0, head_piece)
    grad1, pack_parts1, finish_feed1, finish_pack1 = backward(
        1, own_target, out0, normed1, lat1, mixed1, lse1, residual1, kept1, (heads1, outs1), feed1,
        [lambda: (rows_out[0],), lambda token: (), lambda: (rows_out[1],), lambda: ()],
    )
    normed0 = normalise(own_in, gains_all[0][0])
    later = {}

    def before_weights():
        later["feed"], far = finish_feed1()
        return (pack_parts1, far)

    def during_attention(token):
        return ()

    def after_attention():
        later["pack"] = finish_pack1()
        later["grad"] = gather_rows(grad1)
        return (later["pack"], later["grad"])

    grad0, _, finish_feed0, finish_pack0 = backward(
        0, grad1, own_in, normed0, lat0, mixed0, lse0, residual0, kept0, (heads0, outs0), feed0,
        [lambda: (), during_attention, after_attention, before_weights],
    )
    rows_grad0 = gather_rows(grad0)
    layer_outputs = rows_call(info, *to_core(0, rows_out[0]), *to_core(1, rows_out[1]))
    input_grads = rows_call(info, *to_core(0, rows_grad0), *to_core(1, later["grad"]))

    feed_final0, feed_far0 = finish_feed0()
    feed_total = jnp.where(core == 0, feed_final0, later["feed"])
    gate_t, up_t, down_t = feed_total[:, :, :hidden_cols]
    halves = finish_core(finish_pack0(), later["pack"]).astype(f32)
    main = (head_rows + width) // dp // 2
    query_t, key_t = halves[0, : width // dp], halves[0, width // dp : main]
    value_t, out_t = halves[1, : latent // dp], halves[1, latent // dp : main]
    small = halves[:, main:].reshape(-1, latent)
    lat_rows = width // planes // dp * 2
    lat_t = small[:lat_rows].reshape(lat_rows // 2, 2 * latent)
    gain_t = small[lat_rows, : 2 * width // planes // dp].reshape(2, -1)
    return (
        layer_outputs[None],
        input_grads[None],
        query_t[None],
        lat_t[None],
        key_t[None],
        value_t[None],
        out_t.T[None],
        gain_t[None],
        gate_t[None],
        up_t[None],
        down_t.T[None],
    )


def solution(mesh):
    placed = (
        P("dp", None),
        P("dp", None),
        P("dp"),
        P("section", None, "tensor"),
        P("section", None, None),
        P("section", None, "tensor"),
        P("section", None, "tensor"),
        P("section", "tensor", None),
        P("section", None, None),
        P("section", None, "tensor"),
        P("section", None, "tensor"),
        P("section", "tensor", None),
    )
    return jax.shard_map(
        shards,
        mesh=mesh,
        in_specs=placed,
        out_specs=(
            P("section", "dp", None),
            P("section", "dp", None),
            P("section", "dp", "tensor"),
            P("section", ("tensor", "dp"), None),
            P("section", "dp", "tensor"),
            P("section", "dp", "tensor"),
            P("section", "tensor", "dp"),
            P("section", None, ("tensor", "dp")),
            P("section", "dp", "tensor"),
            P("section", "dp", "tensor"),
            P("section", "tensor", "dp"),
        ),
        check_vma=False,
    )
```

```python
import functools

import jax
import jax.numpy as jnp
from jax import lax
from jax.experimental import pallas as pl
from jax.experimental.pallas import tpu as pltpu
from jax.sharding import PartitionSpec as P

HEAD_DIM = 64
eps = 1e-06
masked_score = -1e30
f32 = jnp.float32
bf16 = jnp.bfloat16


def dot_nn(left, right):
    return lax.dot_general(left, right, (((1,), (0,)), ((), ())), preferred_element_type=f32)


def dot_nt(left, right):
    return lax.dot_general(left, right, (((1,), (1,)), ((), ())), preferred_element_type=f32)


def dot_tn(left, right):
    return lax.dot_general(left, right, (((0,), (0,)), ((), ())), preferred_element_type=f32)


def core_swap(value):
    return lax.ppermute(value, "section", [(0, 1), (1, 0)])


def z_swap(value, step):
    count = lax.axis_size("tensor")
    return lax.ppermute(value, "tensor", [(i, i ^ step) for i in range(count)])


def tie(first, *others):
    return lax.optimization_barrier((first,) + others)[0]


def bits_of(count):
    return [1 << i for i in range(count.bit_length() - 1)]


def plane_gather(piece):
    count = lax.axis_size("dp")
    return lax.all_to_all(jnp.broadcast_to(piece[None], (count,) + piece.shape), "dp", 0, 0)


def plane_sum(parts):
    return jnp.sum(lax.all_to_all(parts, "dp", 0, 0).astype(f32), axis=0).astype(bf16)


def by_plane(values, flip_of):
    count = values.shape[0]
    for bit in bits_of(count):
        order = [k ^ bit for k in range(count)]
        flipped = jnp.stack([values[k] for k in order])
        values = jnp.where((flip_of // bit) % 2 == 1, flipped, values)
    return values


def inverse_rms(rows):
    return lax.rsqrt(jnp.mean(rows * rows, axis=-1, keepdims=True) + eps)


def norm_back(rows, gain, grad_norm):
    scale = inverse_rms(rows)
    weighted = grad_norm * gain
    inner = jnp.mean(weighted * rows, axis=-1, keepdims=True)
    grad_rows = scale * weighted - rows * scale * scale * scale * inner
    grad_gain = jnp.sum(grad_norm * rows * scale, axis=0)
    return (grad_rows, grad_gain)


LENGTH, FIRST, CORE, MEMBER, RANK, PLANE = range(6)


def kernel_call(kernel, info, arrays, grid, in_specs, out_specs, out_shape, scratch, name, flops, transcendentals=0):
    size = sum(a.size * a.dtype.itemsize for a in arrays)
    size += sum(o.size * o.dtype.itemsize for o in out_shape)
    return pl.pallas_call(
        kernel,
        grid_spec=pltpu.PrefetchScalarGridSpec(
            num_scalar_prefetch=1,
            grid=grid,
            in_specs=in_specs,
            out_specs=out_specs,
            scratch_shapes=scratch,
        ),
        out_shape=out_shape,
        compiler_params=pltpu.CompilerParams(
            dimension_semantics=("arbitrary",) * len(grid), vmem_limit_bytes=52 * 1024 * 1024
        ),
        cost_estimate=pl.CostEstimate(flops=flops, bytes_accessed=size, transcendentals=transcendentals),
        name=name,
    )(info, *arrays)


def whole(array):
    shape = array.shape
    return pl.BlockSpec(shape, lambda i, info: (0,) * len(shape))


def lead(array):
    shape = array.shape[1:]
    return pl.BlockSpec((1,) + shape, lambda i, info: (i,) + (0,) * len(shape))


def like(shape, dtype):
    return jax.ShapeDtypeStruct(shape, dtype)


class PackCopies:
    def __init__(self, info, layer, parts, held, sems):
        self.info, self.layer, self.parts, self.held, self.sems = info, layer, parts, held, sems

    def own(self, slot, there):
        for at, (part, target) in enumerate(zip(self.parts, self.held)):
            source = part[1] if there else part[0]
            rows = source.shape[0]
            yield pltpu.make_async_copy(source, target.at[slot, pl.ds(0, rows)], self.sems.at[slot, at])

    def pieces(self, slot, step):
        at = 0
        for (_, _, near, other, begin, rows), held in zip(self.parts, self.held):
            members = near.shape[0]
            source_at = pl.multiple_of(begin + (step - 1) * rows, 16)
            for key in range(members):
                for source, core in ((near, self.info[CORE]), (other, 1 - self.info[CORE])):
                    target = pl.multiple_of((core * members + key) * rows, 16)
                    yield pltpu.make_async_copy(
                        source.at[key, pl.ds(source_at, rows)],
                        held.at[slot, pl.ds(target, rows)],
                        self.sems.at[slot, at],
                    )
                    at += 1

    def each(self, step, act):
        slot = step % 2

        def run(copies):
            for copy in copies:
                act(copy)

        there = self.info[CORE] != self.layer
        pl.when((step == 0) & there)(lambda: run(self.own(slot, True)))
        pl.when((step == 0) & jnp.logical_not(there))(lambda: run(self.own(slot, False)))
        pl.when(step > 0)(lambda: run(self.pieces(slot, step)))

    def start(self, step):
        self.each(step, lambda copy: copy.start())

    def turn(self, step, first, last):
        @pl.when(step == first)
        def _():
            self.start(step)

        @pl.when(step < last)
        def _():
            self.start(step + 1)

        self.each(step, lambda copy: copy.wait())
        return [held.at[step % 2] for held in self.held]


def pack_refs(spec, refs):
    return [tuple(refs[4 * at : 4 * at + 4]) + part for at, part in enumerate(spec)]


def fill_bias(info, bias):
    keys, rows = bias.shape
    key_pos = lax.broadcasted_iota(jnp.int32, (keys, rows), 0)
    query_pos = lax.broadcasted_iota(jnp.int32, (keys, rows), 1) + info[FIRST]
    allowed = (key_pos <= query_pos) & (key_pos < info[LENGTH])
    bias[...] = jnp.where(allowed, 0.0, masked_score)


def head_parts(heads, width, latent):
    at = (0, width, width + latent, width + 2 * latent)
    return [heads[lo:hi] for lo, hi in zip(at[:-1], at[1:])]


def attend_sets(keys, values_t, query, bias, heads):
    lane_head = lax.broadcasted_iota(jnp.int32, query.shape, 1) // HEAD_DIM
    mixed, sums = [], []
    for head in range(heads):
        query_here = jnp.where(lane_head == head, query, bf16(0))
        scores = dot_nt(keys, query_here) + bias
        peak = jnp.max(scores, axis=0, keepdims=True)
        expo = jnp.exp(scores - peak)
        total = jnp.sum(expo, axis=0, keepdims=True)
        part = dot_nn(values_t[head * HEAD_DIM : (head + 1) * HEAD_DIM], expo.astype(bf16))
        mixed.append(part * (1.0 / total))
        sums.append(peak + jnp.log(total))
    return jnp.concatenate(mixed, axis=0), jnp.concatenate(sums, axis=0)


def attend_first_kernel(
    info, x, lat_here, lat_there, heads_here, heads_there, gain_here, gain_there, out, normed, query_all, keys_all, values_t_all
):
    keys_count, width = x.shape
    latent = lat_here.shape[1]
    cols = heads_here.shape[1]
    heads = cols // HEAD_DIM
    rows = keys_count // out.shape[0]
    here = info[2] == 0
    gain = jnp.where(here, gain_here[0:1], gain_there[0:1])
    pack = jnp.where(here, heads_here[...], heads_there[...])
    w_latent = jnp.where(here, lat_here[...], lat_there[...])
    for block in range(keys_count // rows):
        here = slice(block * rows, (block + 1) * rows)
        value = x[here].astype(f32)
        normed[here] = (value * inverse_rms(value) * gain).astype(bf16)
    w_query, w_key, w_value = head_parts(pack, width, latent)
    query_all[...] = dot_nn(normed[...], w_query).astype(bf16) * bf16(HEAD_DIM**-0.5)
    lat = dot_nn(normed[...], w_latent).astype(bf16)
    keys_all[...] = dot_nn(lat, w_key).astype(bf16)
    values_t_all[...] = dot_nn(lat, w_value).astype(bf16).T
    for block in range(keys_count // rows):
        first = block * rows
        end = first + rows
        key_pos = lax.broadcasted_iota(jnp.int32, (end, rows), 0)
        query_pos = lax.broadcasted_iota(jnp.int32, (end, rows), 1) + first
        bias = jnp.where((key_pos <= query_pos) & (key_pos < info[0]), 0.0, masked_score)
        mixed, sums = attend_sets(keys_all[0:end], values_t_all[:, 0:end], query_all[first:end], bias, heads)
        high = sums.astype(bf16)
        low = (sums - high.astype(f32)).astype(bf16)
        at = info[1] ^ block
        out[at, 0:rows, :] = mixed.T.astype(bf16)
        out[at, rows:, :] = jnp.concatenate([high, low, jnp.zeros((16 - 2 * heads, rows), bf16)], axis=0)


def attend_out_kernel(
    spec, layer, info, x, m0, m1, m2, m3, gain, o0, o1, o2, o3, mixed_out, lse_out, residual, normed2, sets, outs, sems
):
    step = pl.program_id(0)
    rows, width = x.shape
    heads = lse_out.shape[1]
    copies = PackCopies(info, layer, pack_refs(spec, (o0, o1, o2, o3)), [outs], sems)
    w_out = copies.turn(step, 0, pl.num_programs(0) - 1)[0]

    @pl.when(step == 0)
    def _():
        residual[...] = x[...].astype(f32)
        for key, piece in enumerate((m0, m1, m2, m3)):
            sets[key ^ info[RANK] ^ info[PLANE]] = piece[...]

    mixed = sets[step, 0:rows, :]
    tail = sets[step, rows:, :].astype(f32)
    mixed_out[0] = mixed
    lse_out[0] = tail[0:heads] + tail[heads : 2 * heads]
    residual[...] += dot_nn(mixed, w_out[0 : mixed.shape[1]])

    @pl.when(step == pl.num_programs(0) - 1)
    def _():
        full = residual[...]
        normed2[...] = (full * inverse_rms(full) * gain[...]).astype(bf16)


def attend_kernel(
    spec, layer, info, x, normed, lat0, lat1, lat2, lat3, gain, h0, h1, h2, h3, o0, o1, o2, o3,
    mixed_out, lse_out, lat_out, residual, normed2, bias, heads_held, outs_held, sems,
):
    step = pl.program_id(0)
    rows, width = normed.shape
    latent = lat_out.shape[2]
    heads = lse_out.shape[1]
    parts = pack_refs(spec, (h0, h1, h2, h3, o0, o1, o2, o3))
    copies = PackCopies(info, layer, parts, [heads_held, outs_held], sems)
    w_heads, w_out = copies.turn(step, 0, pl.num_programs(0) - 1)

    @pl.when(step == 0)
    def _():
        fill_bias(info, bias)
        residual[...] = x[...].astype(f32)
        for key, piece in enumerate((lat0, lat1, lat2, lat3)):
            at = pl.multiple_of((info[RANK] ^ key) * rows, 16)
            for group in range(2):
                lat_out[group, pl.ds(at, rows), :] = piece[:, group * latent : (group + 1) * latent]

    w_query, w_key, w_value = head_parts(w_heads, width, latent)
    lat = lat_out[step // 2]
    query = dot_nn(normed[...], w_query).astype(bf16) * bf16(HEAD_DIM**-0.5)
    keys = dot_nn(lat, w_key).astype(bf16)
    values_t = dot_nn(lat, w_value).astype(bf16).T
    mixed, sums = attend_sets(keys, values_t, query, bias[...], heads)
    lse_out[0] = sums
    mixed = mixed.T.astype(bf16)
    mixed_out[0] = mixed
    residual[...] += dot_nn(mixed, w_out[0 : mixed.shape[1]])

    @pl.when(step == pl.num_programs(0) - 1)
    def _():
        full = residual[...]
        normed2[...] = (full * inverse_rms(full) * gain[...]).astype(bf16)


def attend_back_kernel(
    first_set, spec, layer, info, grad_branch, normed, lat, mixed_in, lse_in, h0, h1, h2, h3, o0, o1, o2, o3,
    grad_norm, grad_lat, keep, send, bias, heads_held, outs_held, sems, lat_sum,
):
    step = pl.program_id(0)
    rows, width = normed.shape
    keys_count, latent = grad_lat.shape
    cols = heads_held.shape[2]
    scale = HEAD_DIM**-0.5
    members = keep.shape[0]
    parts = pack_refs(spec, (h0, h1, h2, h3, o0, o1, o2, o3))
    copies = PackCopies(info, layer, parts, [heads_held, outs_held], sems)
    w_heads, w_out = copies.turn(step + first_set, first_set, first_set + pl.num_programs(0) - 1)

    @pl.when(step == 0)
    def _():
        fill_bias(info, bias)
        grad_norm[...] = jnp.zeros_like(grad_norm)
        lat_sum[...] = jnp.zeros_like(lat_sum)

    w_query, w_key, w_value = head_parts(w_heads, width, latent)
    here = lat[0]
    query = dot_nn(normed[...], w_query).astype(bf16) * bf16(scale)
    keys = dot_nn(here, w_key).astype(bf16)
    keys_t = keys.T
    values = dot_nn(here, w_value).astype(bf16)
    mixed = mixed_in[0]
    grad_mixed = dot_nt(grad_branch[...], w_out[0:cols]).astype(bf16)
    centre = (grad_mixed.astype(f32) * mixed.astype(f32)).T
    lane_head = lax.broadcasted_iota(jnp.int32, (rows, cols), 1) // HEAD_DIM
    grad_keys = jnp.zeros((keys_count, cols), f32)
    grad_values = jnp.zeros((keys_count, cols), f32)
    grad_query_parts = []
    for head in range(cols // HEAD_DIM):
        mine = slice(head * HEAD_DIM, (head + 1) * HEAD_DIM)
        query_here = jnp.where(lane_head == head, query, bf16(0))
        grad_here = jnp.where(lane_head == head, grad_mixed, bf16(0))
        scores = dot_nt(keys, query_here) + bias[...]
        probs = jnp.exp(scores - lse_in[0, head : head + 1, :])
        grad_probs = dot_nt(values, grad_here)
        inner = jnp.sum(centre[mine], axis=0, keepdims=True)
        grad_scores = (probs * (grad_probs - inner)).astype(bf16)
        grad_values += dot_nn(probs.astype(bf16), grad_here)
        grad_keys += dot_nn(grad_scores, query_here)
        grad_query_parts.append(dot_nn(keys_t[mine], grad_scores) * scale)
    grad_keys = grad_keys.astype(bf16)
    grad_values = grad_values.astype(bf16)
    grad_query = jnp.concatenate(grad_query_parts, axis=0).T.astype(bf16)
    grad_norm[...] += dot_nt(grad_query, w_query)
    lat_sum[...] += dot_nt(grad_keys, w_key) + dot_nt(grad_values, w_value)
    halves = (
        (dot_tn(normed[...], grad_query), dot_tn(here, grad_keys)),
        (dot_tn(here, grad_values), dot_tn(grad_branch[...], mixed)),
    )
    for half, results in enumerate(halves):
        for out, wanted in ((keep, half), (send, 1 - half)):

            @pl.when(info[CORE] == wanted)
            def _(out=out, results=results):
                at = 0
                for result in results:
                    size = result.shape[0] // members
                    for member in range(members):
                        out[member, 0, at : at + size, :] = result[member * size : (member + 1) * size].astype(bf16)
                    at += size

    @pl.when(step == pl.num_programs(0) - 1)
    def _():
        grad_lat[...] = lat_sum[...].astype(bf16)


def attend_first_call(info, x, lat_here, lat_there, heads_here, heads_there, gain_here, gain_there, keys, blocks):
    width = x.shape[1]
    latent = lat_here.shape[1] // 2
    cols = heads_here.shape[1]
    outs = [like((blocks, keys // blocks + 16, cols), bf16)]
    arrays = (x, lat_here, lat_there, heads_here, heads_there, gain_here, gain_there)
    group = pl.BlockSpec((width, latent), lambda i, info: (0, info[3]))
    return kernel_call(
        attend_first_kernel,
        info,
        arrays,
        (1,),
        [pl.BlockSpec((keys, width), lambda i, info: (info[2], 0)), group, group] + [whole(v) for v in arrays[3:]],
        [whole(o) for o in outs],
        outs,
        [pltpu.VMEM((keys, width), bf16)] + [pltpu.VMEM((keys, cols), bf16)] * 2 + [pltpu.VMEM((cols, keys), bf16)],
        "attend_first",
        2 * keys * width * (cols + latent) + 4 * keys * latent * cols + 4 * keys * keys * cols * 3,
        keys * keys * 3,
    )[0]


def pack_in(*parts):
    arrays = sum((tuple(part[0:4]) for part in parts), ())
    spec = tuple(tuple(part[4:]) for part in parts)
    members = parts[0][2].shape[0]
    scratch = [pltpu.VMEM((2, 2 * members * part[5], part[0].shape[1]), bf16) for part in parts]
    scratch.append(pltpu.SemaphoreType.DMA((2, 2 * members * len(parts))))
    return arrays, spec, [pl.BlockSpec(memory_space=pl.ANY)] * len(arrays), scratch


def attend_out_call(info, layer, x, messages, outs_w, gain):
    rows, width = x.shape
    arrays, spec, specs, scratch = pack_in(outs_w)
    sets = 4
    cols = messages[0].shape[1]
    heads = cols // HEAD_DIM
    outs = [
        like((sets, rows, cols), bf16),
        like((sets, heads, rows), f32),
        like((rows, width), f32),
        like((rows, width), bf16),
    ]
    return kernel_call(
        functools.partial(attend_out_kernel, spec, layer),
        info,
        (x, *messages, gain) + arrays,
        (sets,),
        [whole(x)] + [whole(m) for m in messages] + [whole(gain)] + specs,
        [lead(outs[0]), lead(outs[1]), whole(outs[2]), whole(outs[3])],
        outs,
        [pltpu.VMEM((sets,) + messages[0].shape, bf16)] + scratch,
        "attend_out",
        2 * sets * rows * width * cols,
    )


def attend_call(info, layer, x, normed, lats, pack, gain):
    rows, width = normed.shape
    arrays, spec, specs, scratch = pack_in(*pack)
    sets = 4
    cols = arrays[0].shape[1]
    latent = lats[0].shape[1] // 2
    keys = rows * len(lats)
    heads = cols // HEAD_DIM
    outs = [
        like((sets, rows, cols), bf16),
        like((sets, heads, rows), f32),
        like((2, keys, latent), bf16),
        like((rows, width), f32),
        like((rows, width), bf16),
    ]
    return kernel_call(
        functools.partial(attend_kernel, spec, layer),
        info,
        (x, normed, *lats, gain) + arrays,
        (sets,),
        [whole(x), whole(normed)] + [whole(v) for v in lats] + [whole(gain)] + specs,
        [lead(outs[0]), lead(outs[1])] + [whole(o) for o in outs[2:]],
        outs,
        [pltpu.VMEM((keys, rows), f32)] + scratch,
        "attend",
        2 * sets * rows * (2 * keys * cols * heads + width * cols * 2) + 4 * sets * keys * latent * cols,
        sets * heads * keys * rows,
    )


def attend_back_call(first_set, info, layer, grad_branch, normed, lat, pack, mixed, lse, members):
    rows, width = normed.shape
    arrays, spec, specs, scratch = pack_in(*pack)
    cols = arrays[0].shape[1]
    piece_rows = (arrays[0].shape[0] + width) // members // 2
    sets = 2
    keys, latent = lat.shape[1:]
    heads = cols // HEAD_DIM
    group = pl.BlockSpec((1, keys, latent), lambda i, info: (first_set // 2, 0, 0))
    outs = [
        like((rows, width), f32),
        like((keys, latent), bf16),
        like((members, sets, piece_rows, cols), bf16),
        like((members, sets, piece_rows, cols), bf16),
    ]
    summed = pl.BlockSpec((members, 1, piece_rows, cols), lambda i, info: (0, i, 0, 0))
    mine = [pl.BlockSpec((1,) + v.shape[1:], lambda i, info: (i + first_set, 0, 0)) for v in (mixed, lse)]
    return kernel_call(
        functools.partial(attend_back_kernel, first_set, spec, layer),
        info,
        (grad_branch, normed, lat, mixed, lse) + arrays,
        (sets,),
        [whole(grad_branch), whole(normed), group] + mine + specs,
        [whole(outs[0]), whole(outs[1]), summed, summed],
        outs,
        [pltpu.VMEM((keys, rows), f32)] + scratch + [pltpu.VMEM((keys, latent), f32)],
        "attend_back",
        2 * sets * rows * (5 * keys * cols * heads + width * cols * 5) + 16 * sets * keys * latent * cols,
        sets * heads * keys * rows,
    )


def feed_shards(spec, layer, info, refs, weights, sems, use):
    here, there, pieces = refs[0:3], refs[3:6], refs[6:12]
    hidden = here[0].shape[0]

    def run(act, far):
        if not far:
            for wanted, sources in ((True, here), (False, there)):

                @pl.when((info[CORE] == layer) == wanted)
                def _(sources=sources):
                    for kind, source in enumerate(sources):
                        act(pltpu.make_async_copy(source, weights.at[0, kind, pl.ds(0, hidden)], sems.at[kind]))

            return
        at = 3
        for kind, (begin, rows) in enumerate(spec):
            members = pieces[2 * kind].shape[0]
            for key in range(members):
                for source, core in ((pieces[2 * kind], info[CORE]), (pieces[2 * kind + 1], 1 - info[CORE])):
                    target = pl.multiple_of((core * members + key) * rows, 16)
                    act(
                        pltpu.make_async_copy(
                            source.at[key, pl.ds(begin, rows)], weights.at[1, kind, pl.ds(target, rows)], sems.at[at]
                        )
                    )
                    at += 1

    run(lambda copy: copy.start(), False)
    run(lambda copy: copy.start(), True)
    run(lambda copy: copy.wait(), False)
    use(0, [weights[0, kind, 0:hidden] for kind in range(3)])
    run(lambda copy: copy.wait(), True)
    use(1, [weights[1, kind, 0:hidden] for kind in range(3)])


def feed_kernel(spec, layer, info, value, *refs):
    total_out, saved, weights, sems, total = refs[12:]

    def use(shard, held):
        gate = dot_nt(value[...], held[0])
        up = dot_nt(value[...], held[1])
        saved[shard, 0] = gate.astype(bf16)
        saved[shard, 1] = up.astype(bf16)
        hidden = (gate * jax.nn.sigmoid(gate) * up).astype(bf16)
        part = dot_nn(hidden, held[2])
        if shard == 0:
            total[...] = part
        else:
            total_out[...] = (total[...] + part).astype(total_out.dtype)

    feed_shards(spec, layer, info, refs[0:12], weights, sems, use)


def feed_back_kernel(spec, layer, info, value, saved, *refs):
    total_out, keep, send, weights, sems, total = refs[12:]

    width = saved.shape[3]

    def use(shard, held):
        grad_hidden = dot_nt(value[...], held[2])
        gate = saved[shard, 0].astype(f32)
        up = saved[shard, 1].astype(f32)
        sigma = jax.nn.sigmoid(gate)
        silu = gate * sigma
        grad_gate = (grad_hidden * up * sigma * (1.0 + gate * (1.0 - sigma))).astype(bf16)
        grad_up = (grad_hidden * silu).astype(bf16)
        hidden = (silu * up).astype(bf16)
        mine = info[CORE] == layer if shard == 0 else info[CORE] != layer
        for out, wanted in ((keep, mine), (send, jnp.logical_not(mine))):

            @pl.when(wanted)
            def _(out=out):
                out[0, :, 0:width] = grad_gate
                out[1, :, 0:width] = grad_up
                out[2, :, 0:width] = hidden

        part = dot_nn(grad_gate, held[0]) + dot_nn(grad_up, held[1])
        if shard == 0:
            total[...] = part
        else:
            total_out[...] = (total[...] + part).astype(total_out.dtype)

    feed_shards(spec, layer, info, refs[0:12], weights, sems, use)


def feed_weights_kernel(hidden, info, *refs):
    lefts, rights, out, turned = refs[0:8], refs[8:12], refs[12], refs[13]
    kind = pl.program_id(0)
    rows = lefts[0].shape[0]
    members, _, size, lanes = out.shape

    @pl.when(kind == 0)
    def _():
        for at in range(2):
            for block in range(4):
                turned[at, :, block * rows : (block + 1) * rows] = lefts[4 * at + block][...].T

    right = jnp.concatenate([r[0] for r in rights], axis=0)
    left = turned[kind // 2]
    for first in range(0, hidden, 256):
        end = min(first + 256, hidden)
        result = dot_nn(left, right[:, first:end]).astype(bf16)
        for member in range(members):
            out[member, 0, :, first:end] = result[member * size : (member + 1) * size]
    out[:, :, :, hidden:] = jnp.zeros((members, 1, size, lanes - hidden), bf16)


def whole_lanes(count):
    return -(-count // 128) * 128


def feed_in(feed_w):
    here, there, pieces = feed_w
    arrays = (*here, *there, *sum((part[0:2] for part in pieces), ()))
    spec = tuple(part[2:4] for part in pieces)
    members, _, width = pieces[0][0].shape
    scratch = [
        pltpu.VMEM((2, 3, 2 * members * pieces[0][3], width), bf16),
        pltpu.SemaphoreType.DMA((3 + 6 * members,)),
    ]
    return arrays, spec, [pl.BlockSpec(memory_space=pl.ANY)] * len(arrays), scratch


def feed_call(info, layer, value, feed_w, dtype):
    rows, width = value.shape
    arrays, spec, specs, scratch = feed_in(feed_w)
    hidden = arrays[0].shape[0]
    outs = [like((rows, width), dtype), like((2, 2, rows, hidden), bf16)]
    return kernel_call(
        functools.partial(feed_kernel, spec, layer),
        info,
        (value,) + arrays,
        (1,),
        [whole(value)] + specs,
        [whole(o) for o in outs],
        outs,
        scratch + [pltpu.VMEM((rows, width), f32)],
        "feed",
        2 * 2 * 3 * rows * width * hidden,
    )


def feed_back_call(info, layer, value, saved, feed_w, dtype):
    rows, width = value.shape
    arrays, spec, specs, scratch = feed_in(feed_w)
    hidden = arrays[0].shape[0]
    outs = [like((rows, width), dtype)] + [like((3, rows, whole_lanes(hidden)), bf16)] * 2
    return kernel_call(
        functools.partial(feed_back_kernel, spec, layer),
        info,
        (value, saved) + arrays,
        (1,),
        [whole(value), whole(saved)] + specs,
        [whole(o) for o in outs],
        outs,
        scratch + [pltpu.VMEM((rows, width), f32)],
        "feed_back",
        2 * 2 * 3 * rows * width * hidden,
    )


def feed_weights_call(info, lefts, rights, members, hidden):
    rows, width = lefts[0].shape
    kinds, _, lanes = rights[0].shape
    shape = (members, kinds, width // members, lanes)
    outs = [like(shape, bf16)]
    return kernel_call(
        functools.partial(feed_weights_kernel, hidden),
        info,
        (*lefts, *rights),
        (kinds,),
        [whole(v) for v in lefts] + [lead(r) for r in rights],
        [pl.BlockSpec((members, 1) + shape[2:], lambda i, info: (0, i, 0, 0))],
        outs,
        [pltpu.VMEM((2, width, 4 * rows), bf16)],
        "feed_weights",
        2 * kinds * 4 * rows * width * hidden,
    )[0]


def rows_kernel(info, first, first_other, second, second_other, out, held, sems):
    planes, rows, _ = first.shape
    for core, sources in ((0, (first, first_other)), (1, (second_other, second))):

        @pl.when(info[CORE] == core)
        def _(sources=sources):
            copies = [pltpu.make_async_copy(v, held.at[:, at], sems.at[0, at]) for at, v in enumerate(sources)]
            for copy in copies:
                copy.start()
            for copy in copies:
                copy.wait()

    whole_copy = pltpu.make_async_copy(held, out, sems.at[1, 0])
    whole_copy.start()
    whole_copy.wait()


def rows_call(info, *arrays):
    planes, rows, width = arrays[0].shape
    shape = (planes, 2, rows, width)
    out = kernel_call(
        rows_kernel,
        info,
        arrays,
        (1,),
        [pl.BlockSpec(memory_space=pl.ANY)] * 4,
        [pl.BlockSpec(memory_space=pl.ANY)],
        [like(shape, bf16)],
        [pltpu.VMEM(shape, bf16), pltpu.SemaphoreType.DMA((2, 2))],
        "rows",
        0,
    )[0]
    return out.reshape(planes * 2 * rows, width)


def shards(inputs, cotangent, lengths, w_query, w_latent, w_key, w_value, w_out, gains, w_gate, w_up, w_down):
    core = lax.axis_index("section")
    z = lax.axis_index("tensor")
    d = lax.axis_index("dp")
    planes = lax.axis_size("tensor")
    dp = lax.axis_size("dp")
    seqs = lengths.shape[0]
    bucket = inputs.shape[0] // seqs
    width = inputs.shape[1]
    layers = 2
    per_seq = planes // seqs * 2
    rows = bucket // per_seq
    rank = (z % (planes // seqs)) * 2 + core
    seq = z // (planes // seqs)
    first = rank * rows
    length = lax.dynamic_index_in_dim(lengths, seq, 0, False)
    info = jnp.stack([length, first, core, d, rank, z]).astype(jnp.int32)
    live = (lax.broadcasted_iota(jnp.int32, (rows, 1), 0) + first < length).astype(f32)
    row_at = seq * bucket + first
    own_in = lax.dynamic_slice_in_dim(inputs, row_at, rows, 0)
    own_target = lax.dynamic_slice_in_dim(cotangent, row_at, rows, 0)
    latent = w_latent.shape[2] // 2
    far_group = z // (planes // 2)

    cols = w_query.shape[2]
    hidden_cols = w_gate.shape[2]
    heads_here = jnp.concatenate([w_query[0], w_key[0], w_value[0]], axis=0)
    heads_there = core_swap(heads_here)
    lat_here = w_latent[0]
    lat_there = core_swap(lat_here)
    gain_here = gains[0]
    gain_there = core_swap(gain_here)
    out_here = w_out[0]
    feed_here = [w_gate[0].T, w_up[0].T, w_down[0]]
    head_rows, out_rows, feed_rows = heads_here.shape[0], out_here.shape[0], hidden_cols

    def piece_rows(count):
        return -(-count // (2 * dp * 16)) * 16

    def piece_of(value, side):
        rows_each = piece_rows(value.shape[0])
        value = jnp.pad(value, ((0, rows_each * 2 * dp - value.shape[0]), (0, 0)))
        return lax.dynamic_slice_in_dim(value, (side * dp + d) * rows_each, rows_each, 0)

    def feed_and_out(side):
        return jnp.concatenate([piece_of(v, side) for v in [out_here] + feed_here], axis=0)

    def layers_of(mine, received):
        return [jnp.where(core == layer, mine, received) for layer in range(layers)]

    main_pieces = layers_of(feed_and_out(core), core_swap(feed_and_out(1 - core)))
    head_pieces = layers_of(piece_of(heads_here, core), core_swap(piece_of(heads_here, 1 - core)))
    head_piece, out_piece, feed_piece = piece_rows(head_rows), piece_rows(out_rows), piece_rows(feed_rows)
    out_far = [z_swap(main_pieces[0][:out_piece], step) for step in range(1, planes)]
    feed_far = z_swap(main_pieces[0][out_piece:], planes // 2)
    out_there = core_swap(out_here)
    feed_there = [core_swap(v) for v in feed_here]
    latents_w = [jnp.where(core == layer, lat_here, lat_there) for layer in range(layers)]
    gains_all = [jnp.where(core == layer, gain_here, gain_there) for layer in range(layers)]

    def over_planes(piece):
        return [z_swap(piece, step) for step in range(1, planes)]

    def gather_near(parts, *before):
        return plane_gather(jnp.concatenate([tie(v, *before) for v in parts], axis=0))

    def gather(parts, before=(), after=()):
        near = gather_near(parts, *before)
        return near, core_swap(tie(near, *after))

    def gather_slow(parts, before=()):
        return lax.all_gather(jnp.concatenate([tie(v, *before) for v in parts], axis=0), "dp", axis=0, tiled=False)

    def by_group(value):
        return by_plane(value, far_group)

    def normalise(x, gain):
        x = x.astype(f32)
        return (x * inverse_rms(x) * gain).astype(bf16)

    def first_attention(*after):
        scalars = jnp.stack([lax.dynamic_index_in_dim(lengths, core, 0, False), z, core, far_group]).astype(jnp.int32)
        out = attend_first_call(
            scalars, inputs, lat_here, lat_there, tie(heads_here, *after), heads_there, gain_here, gain_there, bucket, per_seq
        )
        messages = []
        for way in range(per_seq):
            pairs = []
            for side in range(2):
                for plane in range(planes):
                    to = plane ^ way
                    target = (to % 2) * planes + side * (planes // seqs) + to // 2
                    pairs.append((side * planes + plane, target))
            messages.append(lax.ppermute(out[way], ("section", "tensor"), pairs))
        return out, messages

    def first_latents(*after):
        all_rows = tie(lax.dynamic_slice_in_dim(inputs, seq * bucket, bucket, 0), *after)
        lat = dot_nn(normalise(all_rows, gains_all[0][0]), latents_w[0]).astype(bf16)
        return by_group(jnp.stack([lat[:, :latent], lat[:, latent:]]))

    def attention(layer, x, pack):
        gain = gains_all[layer]
        normed = normalise(x, gain[0])
        own_lat = dot_nn(normed, latents_w[layer]).astype(bf16)
        own_lat = jnp.where(
            far_group == 1, jnp.concatenate([own_lat[:, latent:], own_lat[:, :latent]], axis=1), own_lat
        )
        far_lat = z_swap(own_lat, 1)
        lats = (own_lat, core_swap(own_lat), far_lat, core_swap(far_lat))
        mixed, lse, lat, residual, normed2 = attend_call(info, layer, x, normed, lats, pack, gain[1][None])
        return normed, lat, mixed, lse, residual, normed2

    def feed_own(layer, normed2, feed_w):
        far_normed2 = z_swap(normed2, 1)
        part, saved = feed_call(info, layer, normed2, feed_w, f32)
        return part, saved, tie(far_normed2, part)

    def feed_rest(layer, residual, part, far_normed2, feed_w):
        far_part, far_saved = feed_call(info, layer, far_normed2, feed_w, bf16)
        feed = part + z_swap(far_part, 1).astype(f32)
        return (live * (residual + feed)).astype(bf16), far_saved

    def finish_core(firsts, seconds):
        mine = jnp.where(core == 0, firsts, seconds)
        other = core_swap(jnp.where(core == 0, seconds, firsts))
        return jnp.where(core == 0, jnp.stack([mine, other]), jnp.stack([other, mine]))

    def backward(layer, grad_out, x, normed, lat, mixed, lse, residual, feed_kept, pack, feed_w, hooks):
        normed2, far_normed2, saved, far_saved = feed_kept
        gain = gains_all[layer]
        grad_res = live * grad_out.astype(f32)
        grad_feed = grad_res.astype(bf16)
        far_feed = z_swap(grad_feed, 1)
        part, *rights = feed_back_call(info, layer, grad_feed, saved, feed_w, f32)
        far_part, *far_rights = feed_back_call(info, layer, far_feed, far_saved, feed_w, bf16)
        back = z_swap(far_part, 1)
        lefts = [normed2, far_normed2, core_swap(normed2), core_swap(far_normed2)]
        lefts += [grad_feed, far_feed, core_swap(grad_feed), core_swap(far_feed)]
        rights = [rights[0], far_rights[0], core_swap(rights[1]), core_swap(far_rights[1])]
        lefts[0] = tie(lefts[0], *hooks[3]())
        feed_grads = feed_weights_call(info, lefts, rights, dp, hidden_cols)
        back = tie(back, feed_grads, *hooks[0]())
        grad_norm2 = part + back.astype(f32)
        grad_residual, gain_second = norm_back(residual, gain[1], grad_norm2)
        grad_residual = grad_residual + grad_res
        grad_branch = grad_residual.astype(bf16)

        feed_parts = lax.all_to_all(feed_grads, "dp", 0, 0)
        grad_norms = []
        lat_parts = []
        pack_parts_here = []
        for first_set in (2, 0):
            if first_set == 0:
                grad_branch = tie(grad_branch, grad_norms[0], *hooks[1](grad_branch))
            grad_norm, grad_lat, pack_keep, pack_send = attend_back_call(
                first_set, info, layer, grad_branch, normed, lat, pack, mixed, lse, dp
            )
            grad_norms.append(grad_norm)
            pack_parts_here.append((pack_keep, core_swap(pack_send)))
            grad_lat = grad_lat.reshape(per_seq // 2, 2, rows, latent)
            total = lax.dynamic_index_in_dim(grad_lat, core, 1, False) + core_swap(
                lax.dynamic_index_in_dim(grad_lat, 1 - core, 1, False)
            )
            near = rank // 2
            total = lax.dynamic_index_in_dim(total, near, 0, False) + z_swap(
                lax.dynamic_index_in_dim(total, 1 - near, 0, False), 1
            )
            lat_parts.append(total)
        if layer == 0:
            lat_parts[1] = tie(lat_parts[1], feed_parts, *hooks[2]())
        else:
            lat_parts[1] = tie(lat_parts[1], feed_parts, *hooks[2]())
        lat_own = by_group(jnp.stack(lat_parts[::-1]))
        lat_own = jnp.concatenate([lat_own[0], lat_own[1]], axis=1)
        grad_norm = grad_norms[0] + grad_norms[1] + dot_nt(lat_own, latents_w[layer])
        grad_x, gain_first = norm_back(x.astype(f32), gain[0], grad_norm)
        grad_x = (grad_x + grad_residual).astype(bf16)

        lat_w = dot_tn(normed, lat_own).astype(bf16).reshape(planes, dp, width // planes // dp * 2, latent)
        gain_g = jnp.stack([gain_first, gain_second]).astype(bf16)
        gain_g = gain_g.reshape(2, planes, dp, -1).transpose(1, 2, 0, 3).reshape(planes, dp, 1, -1)
        gain_g = jnp.pad(gain_g, ((0, 0), (0, 0), (0, 31), (0, latent - gain_g.shape[3])))
        small = jnp.swapaxes(by_plane(jnp.concatenate([lat_w, gain_g], axis=2), z), 0, 1)
        half = small.shape[2] // 2
        small_keep = lax.dynamic_slice_in_dim(small, core * half, half, 2)
        small_send = lax.dynamic_slice_in_dim(small, (1 - core) * half, half, 2)
        small_parts = (small_keep, core_swap(small_send))

        feed_sums = jnp.sum(tie(feed_parts, grad_x).astype(f32), axis=0).astype(bf16)
        if layer == 0:
            pack_parts_here = [(a, tie(b, grad_x)) for a, b in pack_parts_here]
        pack_total = jnp.concatenate([a + b for a, b in pack_parts_here[::-1]], axis=1)
        small_total = small_parts[0] + small_parts[1]
        pack_parts = lax.all_to_all(jnp.concatenate([pack_total, small_total], axis=2), "dp", 0, 0)

        def finish_feed():
            pairs = [((1 - layer) * planes + i, layer * planes + (i ^ (planes // 2))) for i in range(planes)]
            far = lax.ppermute(feed_sums, ("section", "tensor"), pairs)
            return feed_sums.astype(f32) + far.astype(f32), far

        def finish_pack(*after):
            parts = tie(pack_parts, *after)
            sums = jnp.sum(parts.astype(f32), axis=0).astype(bf16)
            sums = sums[0::2] + z_swap(sums[1::2], 1)
            return sums[0] + z_swap(sums[1], 2)

        return grad_x, pack_parts, finish_feed, finish_pack

    lat0 = first_latents()
    first_out, messages = first_attention(feed_far, lat0, out_there, *feed_there)
    main0 = gather(out_far + [feed_far], (), messages)
    outs0 = (out_here, out_there) + main0 + (0, out_piece)
    at = (planes - 1) * out_piece
    feed0 = (feed_here, feed_there, [main0 + (at + k * feed_piece, feed_piece) for k in range(3)])
    mixed0, lse0, residual0, normed2_0 = attend_out_call(info, 0, own_in, messages, outs0, gains_all[0][1][None])
    near_heads1 = gather_slow(over_planes(head_pieces[1]), (first_out,))
    part0, saved0, far_normed2 = feed_own(0, normed2_0, feed0)
    far_normed2 = tie(far_normed2, near_heads1)
    main_piece = tie(main_pieces[1], *messages)
    far_main = over_planes(main_piece[:out_piece]) + [z_swap(main_piece[out_piece:], planes // 2)]
    near1 = gather_near(far_main, part0)
    out0, far_saved0 = feed_rest(0, residual0, part0, far_normed2, feed0)
    kept0 = [normed2_0, far_normed2, saved0, far_saved0]
    main1 = near1, core_swap(tie(near1, out0))
    heads1 = (heads_here, heads_there, near_heads1, core_swap(near_heads1), 0, head_piece)
    outs1 = (out_here, out_there) + main1 + (0, out_piece)
    feed1 = (feed_here, feed_there, [main1 + (at + k * feed_piece, feed_piece) for k in range(3)])

    normed1, lat1, mixed1, lse1, residual1, normed2_1 = attention(1, out0, (heads1, outs1))
    part1, saved1, far_normed2 = feed_own(1, normed2_1, feed1)
    out1, far_saved1 = feed_rest(1, residual1, part1, far_normed2, feed1)
    kept1 = [normed2_1, far_normed2, saved1, far_saved1]
    def gather_rows(own):
        return lax.all_gather(own, "tensor", axis=0, tiled=False)

    def to_core(layer, found):
        return found, lax.ppermute(found, "section", [(1 - layer, layer)])

    rows_out = [gather_rows(out0), gather_rows(out1)]
    near_heads0 = gather_slow(over_planes(tie(head_pieces[0], normed2_1)), (part1,))
    heads0 = (heads_here, heads_there, near_heads0, core_swap(tie(near_heads0, out1)), 0, head_piece)
    grad1, pack_parts1, finish_feed1, finish_pack1 = backward(
        1, own_target, out0, normed1, lat1, mixed1, lse1, residual1, kept1, (heads1, outs1), feed1,
        [lambda: (rows_out[0],), lambda token: (), lambda: (rows_out[1],), lambda: ()],
    )
    normed0 = normalise(own_in, gains_all[0][0])
    later = {}

    def before_weights():
        later["feed"], far = finish_feed1()
        return (pack_parts1, far)

    def during_attention(token):
        return ()

    def after_attention():
        later["pack"] = finish_pack1()
        later["grad"] = gather_rows(grad1)
        return (later["pack"], later["grad"])

    grad0, _, finish_feed0, finish_pack0 = backward(
        0, grad1, own_in, normed0, lat0, mixed0, lse0, residual0, kept0, (heads0, outs0), feed0,
        [lambda: (), during_attention, after_attention, before_weights],
    )
    rows_grad0 = gather_rows(grad0)
    layer_outputs = rows_call(info, *to_core(0, rows_out[0]), *to_core(1, rows_out[1]))
    input_grads = rows_call(info, *to_core(0, rows_grad0), *to_core(1, later["grad"]))

    feed_final0, feed_far0 = finish_feed0()
    feed_total = jnp.where(core == 0, feed_final0, later["feed"])
    gate_t, up_t, down_t = feed_total[:, :, :hidden_cols]
    halves = finish_core(finish_pack0(), later["pack"]).astype(f32)
    main = (head_rows + width) // dp // 2
    query_t, key_t = halves[0, : width // dp], halves[0, width // dp : main]
    value_t, out_t = halves[1, : latent // dp], halves[1, latent // dp : main]
    small = halves[:, main:].reshape(-1, latent)
    lat_rows = width // planes // dp * 2
    lat_t = small[:lat_rows].reshape(lat_rows // 2, 2 * latent)
    gain_t = small[lat_rows, : 2 * width // planes // dp].reshape(2, -1)
    return (
        layer_outputs[None],
        input_grads[None],
        query_t[None],
        lat_t[None],
        key_t[None],
        value_t[None],
        out_t.T[None],
        gain_t[None],
        gate_t[None],
        up_t[None],
        down_t.T[None],
    )


def solution(mesh):
    placed = (
        P("dp", None),
        P("dp", None),
        P("dp"),
        P("section", None, "tensor"),
        P("section", None, None),
        P("section", None, "tensor"),
        P("section", None, "tensor"),
        P("section", "tensor", None),
        P("section", None, None),
        P("section", None, "tensor"),
        P("section", None, "tensor"),
        P("section", "tensor", None),
    )
    return jax.shard_map(
        shards,
        mesh=mesh,
        in_specs=placed,
        out_specs=(
            P("section", "dp", None),
            P("section", "dp", None),
            P("section", "dp", "tensor"),
            P("section", ("tensor", "dp"), None),
            P("section", "dp", "tensor"),
            P("section", "dp", "tensor"),
            P("section", "tensor", "dp"),
            P("section", None, ("tensor", "dp")),
            P("section", "dp", "tensor"),
            P("section", "dp", "tensor"),
            P("section", "tensor", "dp"),
        ),
        check_vma=False,
    )
```
